32 devices in a mesh: dp: 8 (over y, x, core), fsdp: 4 (over z).
Axes of the slice: x: 2, y: 2, z: 4, core: 2. Of those that a mesh axis runs over, the one named last changes fastest.
Arguments:
- picture_encoder_outputs: bfloat16 [8192, 1152], P(('dp', 'fsdp')), may hold values from -6 to 6
- caption_encoder_vectors: bfloat16 [8192, 1152], P(('dp', 'fsdp')), may hold values from -6 to 6
- linear_map_matrix: bfloat16 [1152, 1152], P('fsdp'), may hold values from -0.1875 to 0.1875
- sharpness_learned: float32 [1], replicated, may hold values from 20 to 40
- shift_learned_bias: float32 [1], replicated, may hold values from -2 to 2
Outputs:
- head_grad: float32 [8, 1152, 1152], P('dp', 'fsdp')
- text_embedding_gradient: float32 [8192, 1152], P(('dp', 'fsdp'))
The draws below stay inside these ranges and needn't reach their ends.
All inputs are finite; a program needn't handle non-finite values.
Results may differ from the reference program's by a relative error of at most 0.0095.
Values may be sent and summed in bfloat16 or wider, within the bound.
No kernel may reach another device: no remote copies, remote signals or barrier semaphores. Data moves between devices by JAX's collectives and lax.ppermute only.
A program may use at most 64 MiB of HBM per device.

```python
import jax
import jax.numpy as jnp
from jax import lax

D = 1152
ROWS = 256
STEPS = 3
BATCH = 8192
N_DP = 8
N_FSDP = 4


def steps_of(key, extent, cuts, low, high):
    loudness, own = 1.0, jax.random.fold_in(key, 6)
    for position, shards_of in cuts:
        steps = jnp.exp(jax.random.uniform(jax.random.fold_in(own, position), (shards_of,), jnp.float32, low / len(cuts), high / len(cuts)))
        loudness = loudness * jnp.repeat(steps, extent[position] // shards_of).reshape([-1 if axis == position else 1 for axis in range(len(extent))])
    return loudness


def noise(key, extent, spread, most, split=(), kind=jnp.bfloat16):
    array = jax.random.normal(key, extent, jnp.float32) * spread
    if len(split) > 0:
        array = steps_of(key, extent, split, -0.22, 0.18) * array
    return jnp.clip(array, min=-most, max=most).astype(kind)


def setup_inputs(seed: int = 0) -> dict:
    arg_keys = jax.random.split(jax.random.key(seed), 6)
    picture_encoder_outputs = noise(arg_keys[0], (BATCH, D), 1.0, 6.0, ((0, 32),))
    caption_encoder_vectors = noise(arg_keys[1], (BATCH, D), 1.0, 6.0, ((0, 32),))
    linear_map_matrix = noise(arg_keys[2], (D, D), D ** -0.5, 0.1875, ((0, 4),))
    sharpness_learned = jnp.clip(jax.random.uniform(arg_keys[3], (1,), jnp.float32, 20.0, 40.0), 20.0, 40.0)
    shift_learned_bias = jnp.clip(jax.random.uniform(arg_keys[4], (1,), jnp.float32, -2.0, 2.0), -2.0, 2.0)
    return {"picture_encoder_outputs": picture_encoder_outputs, "caption_encoder_vectors": caption_encoder_vectors, "linear_map_matrix": linear_map_matrix, "sharpness_learned": sharpness_learned, "shift_learned_bias": shift_learned_bias}


def reference(picture_encoder_outputs, caption_encoder_vectors, linear_map_matrix, sharpness_learned, shift_learned_bias):
    proj = jnp.dot(picture_encoder_outputs, linear_map_matrix, preferred_element_type=jnp.float32)
    img_norm = jnp.sqrt(lax.optimization_barrier(jnp.sum(proj * proj, axis=-1, keepdims=True)) + 1e-06)
    img_dir = proj / img_norm
    photo_normalized = img_dir.astype(jnp.bfloat16)
    text_block_window = caption_encoder_vectors.astype(jnp.float32)
    txt_norm = jnp.sqrt(lax.optimization_barrier(jnp.sum(text_block_window * text_block_window, axis=-1, keepdims=True)) + 1e-06)
    txt_dir = text_block_window / txt_norm
    txt_unit = txt_dir.astype(jnp.bfloat16)
    dimensions4 = (N_DP, N_FSDP, ROWS, D)
    photo_rows_4d = photo_normalized.reshape(dimensions4).astype(jnp.float32)
    txt4 = txt_unit.reshape(dimensions4).astype(jnp.float32)
    sharpness_exponentiated = sharpness_learned[0]
    eye = jnp.eye(ROWS, dtype=jnp.float32)
    photo_slope_accumulated = jnp.zeros(dimensions4, jnp.float32)
    txt_grad = jnp.zeros(dimensions4, jnp.float32)
    for step in range(STEPS):
        counterpart_index = jnp.roll(txt4, step, axis=0)
        similarity_scores = sharpness_exponentiated * jnp.einsum('mvdr,mvyr->mvdy', photo_rows_4d, counterpart_index) + shift_learned_bias[0]
        loss_weight_coefficient = jax.nn.sigmoid(similarity_scores)
        if step == 0:
            loss_weight_coefficient = loss_weight_coefficient - eye
        loss_weight_coefficient = loss_weight_coefficient.astype(jnp.bfloat16).astype(jnp.float32)
        photo_slope_accumulated = photo_slope_accumulated + sharpness_exponentiated * jnp.einsum('puvg,pugy->puvy', loss_weight_coefficient, counterpart_index)
        part = sharpness_exponentiated * jnp.einsum('xonr,xonh->xorh', loss_weight_coefficient, photo_rows_4d)
        txt_grad = txt_grad + jnp.roll(part, -step, axis=0)
    photo_slope_accumulated = photo_slope_accumulated.reshape(BATCH, D)
    txt_grad = txt_grad.reshape(BATCH, D)
    grad_proj = ((photo_slope_accumulated - img_dir * lax.optimization_barrier(jnp.sum(img_dir * photo_slope_accumulated, axis=-1, keepdims=True))) / img_norm).astype(jnp.bfloat16)
    text_embedding_gradient = (txt_grad - txt_dir * lax.optimization_barrier(jnp.sum(txt_dir * txt_grad, axis=-1, keepdims=True))) / txt_norm
    feats4 = picture_encoder_outputs.reshape(N_DP, N_FSDP, ROWS, D)
    grads4 = grad_proj.reshape(N_DP, N_FSDP, ROWS, D)

    def one_group(pair):
        feats, grads = pair
        partial_value = jnp.einsum('bir,bic->brc', feats.astype(jnp.float32), grads.astype(jnp.float32))
        return lax.optimization_barrier(jnp.sum(partial_value.astype(jnp.bfloat16).astype(jnp.float32), axis=0))
    head_grad = lax.map(one_group, (feats4, grads4))
    return (head_grad, text_embedding_gradient)
```

```python
import functools

import jax
import jax.numpy as jnp
from jax import lax
from jax.experimental import pallas as pl
from jax.experimental.pallas import tpu as pltpu
from jax.sharding import PartitionSpec as P

STEPS = 3
EPS = 1e-06
CUTS = (256, 384, 512)
VMEM_BYTES = 48 * 1024 * 1024
BF16, F32 = jnp.bfloat16, jnp.float32


def spaces(count):
    return [pl.BlockSpec(memory_space=pltpu.VMEM)] * count


def params():
    return pltpu.CompilerParams(vmem_limit_bytes=VMEM_BYTES)


def cost(flops, *arrays):
    size = sum(a.size * a.dtype.itemsize for a in arrays)
    return pl.CostEstimate(flops=flops, bytes_accessed=size, transcendentals=0)


def prepare_kernel(t0, t1, t2, x, far_x, units, x_t):
    rows = t0.shape[0]
    for k, block in enumerate((t0, t1, t2)):
        values = block[...].astype(F32)
        norm = jnp.sqrt(jnp.sum(values * values, axis=-1, keepdims=True) + EPS)
        units[k * rows : (k + 1) * rows, :] = (values / norm).astype(BF16)
    x_t[:, :rows] = x[...].T
    x_t[:, rows:] = far_x[...].T


def prepare(t0, t1, t2, x, far_x):
    rows, width = t0.shape
    outs = (
        jax.ShapeDtypeStruct((STEPS * rows, width), BF16),
        jax.ShapeDtypeStruct((width, 2 * rows), BF16),
    )
    return pl.pallas_call(
        prepare_kernel,
        out_shape=outs,
        in_specs=spaces(5),
        out_specs=spaces(2),
        compiler_params=params(),
        cost_estimate=cost(0, t0, t1, t2, x, far_x, *outs),
        name="prepare",
    )(t0, t1, t2, x, far_x)


def picture_kernel(n_fsdp, x, units, sharp, bias, own, *rest):
    hops = n_fsdp - 1
    pieces, (grad, unit, w, proj, sem) = rest[: 4 * hops], rest[4 * hops :]
    part, core = lax.axis_index("fsdp"), lax.rem(lax.axis_index("dp"), 2)
    depth = own.shape[0]
    half = depth // 2
    rows = x.shape[0]

    def moves():
        for k in range(1, n_fsdp):
            for from_left in (True, False):
                there = part - k if from_left else part + k
                valid = there >= 0 if from_left else there < n_fsdp
                base = (0 if from_left else hops) + k - 1
                for sibling in (0, 1):
                    side = core if sibling == 0 else 1 - core
                    start = pl.multiple_of(there * depth + side * half, 16)
                    index = base + sibling * 2 * hops
                    yield valid, pieces[index], start, index

    first = pltpu.make_async_copy(
        own, w.at[pl.ds(pl.multiple_of(part * depth, 16), depth), :], sem.at[4 * hops]
    )
    first.start()
    for valid, source, start, index in moves():

        @pl.when(valid)
        def _():
            pltpu.make_async_copy(source, w.at[pl.ds(start, half), :], sem.at[index]).start()

    first.wait()
    for valid, source, start, index in moves():

        @pl.when(valid)
        def _():
            pltpu.make_async_copy(source, w.at[pl.ds(start, half), :], sem.at[index]).wait()

    proj[...] = jnp.dot(x[...], w[...], preferred_element_type=F32)
    values = proj[...]
    norm = jnp.sqrt(jnp.sum(values * values, axis=-1, keepdims=True) + EPS)
    unit[...] = (values / norm).astype(BF16)
    scale = sharp[0]
    logits = scale * lax.dot_general(
        unit[...], units[...], (((1,), (1,)), ((), ())), preferred_element_type=F32
    ) + bias[0]
    coefficient = jax.nn.sigmoid(logits)
    row = lax.broadcasted_iota(jnp.int32, coefficient.shape, 0)
    column = lax.broadcasted_iota(jnp.int32, coefficient.shape, 1)
    coefficient = jnp.where(row == column, coefficient - 1.0, coefficient).astype(BF16)
    slope = scale * jnp.dot(coefficient, units[...], preferred_element_type=F32)
    direction = proj[...] / norm
    along = jnp.sum(direction * slope, axis=-1, keepdims=True)
    grad[...] = ((slope - direction * along) / norm).astype(BF16)


def picture_side(n_fsdp, x, units, sharp, bias, own, pieces):
    rows, width = x.shape
    out = jax.ShapeDtypeStruct((rows, width), BF16)
    hops = n_fsdp - 1
    smem = pl.BlockSpec(memory_space=pltpu.SMEM)
    return pl.pallas_call(
        functools.partial(picture_kernel, n_fsdp),
        out_shape=(out, out),
        in_specs=spaces(2) + [smem, smem] + [pl.BlockSpec(memory_space=pl.ANY)] * (1 + 4 * hops),
        out_specs=spaces(2),
        scratch_shapes=[
            pltpu.VMEM((width, width), BF16),
            pltpu.VMEM((rows, width), F32),
            pltpu.SemaphoreType.DMA((4 * hops + 1,)),
        ],
        compiler_params=params(),
        cost_estimate=cost(2 * rows * width * (width + 2 * STEPS * rows), x, units, own, out, out),
        name="picture_side",
    )(x, units, sharp, bias, own, *pieces)


def text_kernel(text, u0, u1, u2, sharp, bias, out, units):
    rows = text.shape[0]
    for k, block in enumerate((u0, u1, u2)):
        units[k * rows : (k + 1) * rows, :] = block[...]
    values = text[...].astype(F32)
    norm = jnp.sqrt(jnp.sum(values * values, axis=-1, keepdims=True) + EPS)
    direction = values / norm
    scale = sharp[0]
    logits = scale * lax.dot_general(
        direction.astype(BF16), units[...], (((1,), (1,)), ((), ())), preferred_element_type=F32
    ) + bias[0]
    coefficient = jax.nn.sigmoid(logits)
    row = lax.broadcasted_iota(jnp.int32, coefficient.shape, 0)
    column = lax.broadcasted_iota(jnp.int32, coefficient.shape, 1)
    coefficient = jnp.where(row == column, coefficient - 1.0, coefficient).astype(BF16)
    slope = scale * jnp.dot(coefficient, units[...], preferred_element_type=F32)
    along = jnp.sum(direction * slope, axis=-1, keepdims=True)
    out[...] = (slope - direction * along) / norm


def text_side(text, u0, u1, u2, sharp, bias):
    rows, width = text.shape
    out = jax.ShapeDtypeStruct((rows, width), F32)
    smem = pl.BlockSpec(memory_space=pltpu.SMEM)
    return pl.pallas_call(
        text_kernel,
        out_shape=out,
        in_specs=spaces(4) + [smem, smem],
        out_specs=pl.BlockSpec(memory_space=pltpu.VMEM),
        scratch_shapes=[pltpu.VMEM((STEPS * rows, width), BF16)],
        compiler_params=params(),
        cost_estimate=cost(4 * STEPS * rows * rows * width, text, u0, u1, u2, out),
        name="text_side",
    )(text, u0, u1, u2, sharp, bias)


def rows_of(ref, block, depth):
    return ref[pl.ds(pl.multiple_of(block * depth, 16), depth), :]


def outward_kernel(depth, x_t, grad, out):
    rows = grad.shape[0]
    part = lax.axis_index("fsdp")
    block = jnp.where(lax.rem(part, 2) == 0, part + 1, part - 1)
    out[...] = jnp.dot(
        rows_of(x_t, block, depth)[:, :rows], grad[...], preferred_element_type=F32
    ).astype(BF16)


def outward(depth, x_t, grad):
    out = jax.ShapeDtypeStruct((depth, grad.shape[1]), BF16)
    return pl.pallas_call(
        functools.partial(outward_kernel, depth),
        out_shape=out,
        in_specs=spaces(2),
        out_specs=pl.BlockSpec(memory_space=pltpu.VMEM),
        compiler_params=params(),
        cost_estimate=cost(2 * depth * grad.size, x_t, grad, out),
        name="outward",
    )(x_t, grad)


def pair_kernel(depth, begin, x_t, grad, far_grad, kept, near, far):
    rows = grad.shape[0]
    part = lax.axis_index("fsdp")
    size = far_grad.shape[1]
    mine = grad[:, begin : begin + size]
    for block, out in ((3 - part, near), (lax.rem(part + 2, 4), far), (part, kept)):
        left = rows_of(x_t, block, depth)
        out[...] = (
            jnp.dot(left[:, :rows], mine, preferred_element_type=F32)
            + jnp.dot(left[:, rows:], far_grad[...], preferred_element_type=F32)
        ).astype(out.dtype)


def pair_product(depth, begin, x_t, grad, far_grad):
    size = far_grad.shape[1]
    outs = tuple(jax.ShapeDtypeStruct((depth, size), t) for t in (F32, BF16, BF16))
    return pl.pallas_call(
        functools.partial(pair_kernel, depth, begin),
        out_shape=outs,
        in_specs=spaces(3),
        out_specs=spaces(3),
        compiler_params=params(),
        cost_estimate=cost(12 * depth * far_grad.size, x_t, grad, far_grad, *outs),
        name="pair_product",
    )(x_t, grad, far_grad)


def total_kernel(count, *refs):
    kept, near, far, (direct, out) = refs[:count], refs[count : 2 * count], refs[2 * count : 3 * count], refs[3 * count :]
    begin = 0
    for a, b, c in zip(kept, near, far):
        stop = begin + a.shape[1]
        out[0, :, begin:stop] = (
            a[...]
            + b[...].astype(F32)
            + c[...].astype(F32)
            + direct[:, begin:stop].astype(F32)
        )
        begin = stop


def total(kept, near, far, direct):
    out = jax.ShapeDtypeStruct((1,) + direct.shape, F32)
    return pl.pallas_call(
        functools.partial(total_kernel, len(kept)),
        out_shape=out,
        in_specs=spaces(3 * len(kept) + 1),
        out_specs=pl.BlockSpec(memory_space=pltpu.VMEM),
        compiler_params=params(),
        cost_estimate=cost(0, *kept, *near, *far, direct, out),
        name="total",
    )(*kept, *near, *far, direct)


def line_body(n_dp, n_fsdp, x, text, w, sharp, bias):
    depth = w.shape[0]
    half = depth // 2
    core = lax.rem(lax.axis_index("dp"), 2)
    both = ("dp", "fsdp")

    def along(value, pairs):
        return lax.ppermute(value, "fsdp", pairs)

    def across(value, parts):
        pairs = [(d * n_fsdp + f, (d ^ 1) * n_fsdp + f) for d in range(n_dp) for f in parts]
        return lax.ppermute(value, both, pairs)

    def shifted(value, by):
        return lax.ppermute(value, "dp", [(d, (d + by) % n_dp) for d in range(n_dp)])

    own = lax.dynamic_slice_in_dim(w, core * half, half, 0)
    rights, lefts = [], []
    right = left = own
    for k in range(1, n_fsdp):
        right = along(right, [(f, f + 1) for f in range(k - 1, n_fsdp - 1)])
        left = along(left, [(f, f - 1) for f in range(1, n_fsdp - k + 1)])
        rights.append(right)
        lefts.append(left)
    far_x = along(x, [(0, 1), (3, 2)])
    text2 = shifted(text, 2)
    text1 = across(jnp.where(core == 0, text, text2), range(n_fsdp))
    right_twins = [across(r, range(k + 1, n_fsdp)) for k, r in enumerate(rights)]
    left_twins = [across(r, range(n_fsdp - 1 - k)) for k, r in enumerate(lefts)]

    units, x_t = prepare(text, text1, text2, x, far_x)
    grad, unit = picture_side(
        n_fsdp, x, units, sharp, bias, w, rights + lefts + right_twins + left_twins
    )

    begin, far_grads = 0, []
    for size in CUTS:
        far_grads.append((begin, along(grad[:, begin : begin + size], [(0, 1), (3, 2)])))
        begin += size
    direct = along(outward(depth, x_t, grad), [(1, 0), (2, 3)])
    unit2 = shifted(unit, -2)
    unit1 = across(jnp.where(core == 0, unit2, unit), range(n_fsdp))
    kept, nears, fars = [], [], []
    for begin, far_grad in far_grads:
        mine, near, far = pair_product(depth, begin, x_t, grad, far_grad)
        kept.append(mine)
        nears.append(along(near, [(1, 2), (2, 1)]))
        fars.append(along(far, [(1, 3), (2, 0)]))
    text_grad = text_side(text, unit, unit1, unit2, sharp, bias)
    return total(kept, nears, fars, direct), text_grad


def plain_body(n_dp, n_fsdp, x, text, w, sharp, bias):
    def shifted(value, by):
        return lax.ppermute(value, "dp", [(d, (d + by) % n_dp) for d in range(n_dp)])

    rows, width = x.shape
    proj = jnp.dot(
        x, lax.all_gather(w, "fsdp", axis=0, tiled=True), preferred_element_type=F32
    )
    norm = jnp.sqrt(jnp.sum(proj * proj, axis=-1, keepdims=True) + EPS)
    direction = proj / norm
    unit = direction.astype(BF16)
    values = text.astype(F32)
    txt_norm = jnp.sqrt(jnp.sum(values * values, axis=-1, keepdims=True) + EPS)
    txt_dir = values / txt_norm
    slot = txt_dir.astype(BF16)
    scale = sharp[0]
    slope = jnp.zeros((rows, width), F32)
    txt_slope = jnp.zeros((rows, width), F32)
    for step in range(STEPS):
        if step > 0:
            slot = shifted(slot, 1)
        logits = scale * jnp.dot(unit, slot.T, preferred_element_type=F32) + bias[0]
        coefficient = jax.nn.sigmoid(logits)
        if step == 0:
            coefficient = coefficient - jnp.eye(rows, dtype=F32)
        coefficient = coefficient.astype(BF16)
        slope = slope + scale * jnp.dot(coefficient, slot, preferred_element_type=F32)
        share = scale * lax.dot_general(
            coefficient, unit, (((0,), (0,)), ((), ())), preferred_element_type=F32
        )
        if step > 0:
            share = shifted(share.astype(BF16), -step).astype(F32)
        txt_slope = txt_slope + share
    grad = (
        (slope - direction * jnp.sum(direction * slope, axis=-1, keepdims=True)) / norm
    ).astype(BF16)
    text_grad = (
        txt_slope - txt_dir * jnp.sum(txt_dir * txt_slope, axis=-1, keepdims=True)
    ) / txt_norm
    partial = lax.dot_general(
        x, grad, (((0,), (0,)), ((), ())), preferred_element_type=F32
    ).astype(BF16)
    head = lax.psum_scatter(partial, "fsdp", scatter_dimension=0, tiled=True).astype(F32)
    return head[None], text_grad


def solution(mesh):
    n_dp, n_fsdp = mesh.shape["dp"], mesh.shape["fsdp"]
    line = n_fsdp == 4 and n_dp % 2 == 0 and n_dp >= STEPS
    placed = (P(("dp", "fsdp"), None), P(("dp", "fsdp"), None), P("fsdp", None), P(), P())
    return jax.shard_map(
        functools.partial(line_body if line else plain_body, n_dp, n_fsdp),
        mesh=mesh,
        in_specs=placed,
        out_specs=(P("dp", "fsdp", None), P(("dp", "fsdp"), None)),
        check_vma=False,
    )
```

```python
import functools

import jax
import jax.numpy as jnp
from jax import lax
from jax.experimental import pallas as pl
from jax.experimental.pallas import tpu as pltpu
from jax.sharding import PartitionSpec as P

STEPS = 3
EPS = 1e-06
SHARES = (1, 2)
VMEM_BYTES = 24 * 1024 * 1024
BF16, F32 = jnp.bfloat16, jnp.float32


def spaces(count):
    return [pl.BlockSpec(memory_space=pltpu.VMEM)] * count


def params():
    return pltpu.CompilerParams(vmem_limit_bytes=VMEM_BYTES)


def cost(flops, *arrays):
    size = sum(a.size * a.dtype.itemsize for a in arrays)
    return pl.CostEstimate(flops=flops, bytes_accessed=size, transcendentals=0)


def place(n_dp):
    where = lax.axis_index("dp")
    return lax.axis_index("fsdp"), lax.rem(where, 2), lax.div(where, n_dp // 2)


def cut_kernel(n_dp, short, own, whole, part, sem):
    _, core, side = place(n_dp)
    half = whole.shape[0]
    first = pltpu.make_async_copy(
        own.at[pl.ds(pl.multiple_of(core * half, 16), half), :], whole, sem.at[0]
    )
    start = pl.multiple_of(core * half + side * (half - short), 16)
    second = pltpu.make_async_copy(own.at[pl.ds(start, short), :], part, sem.at[1])
    first.start()
    second.start()
    first.wait()
    second.wait()


def cut(n_dp, short, own):
    half, width = own.shape[0] // 2, own.shape[1]
    outs = (
        jax.ShapeDtypeStruct((half, width), BF16),
        jax.ShapeDtypeStruct((short, width), BF16),
    )
    return pl.pallas_call(
        functools.partial(cut_kernel, n_dp, short),
        out_shape=outs,
        in_specs=[pl.BlockSpec(memory_space=pl.ANY)],
        out_specs=spaces(2),
        scratch_shapes=[pltpu.SemaphoreType.DMA((2,))],
        compiler_params=params(),
        cost_estimate=cost(0, *outs, *outs),
        name="cut",
    )(own)


def prepare_kernel(t0, t1, t2, units):
    rows = t0.shape[0]
    for k, block in enumerate((t0, t1, t2)):
        values = block[...].astype(F32)
        inverse = 1.0 / jnp.sqrt(jnp.sum(values * values, axis=-1, keepdims=True) + EPS)
        units[k * rows : (k + 1) * rows, :] = (values * inverse).astype(BF16)


def prepare(t0, t1, t2):
    rows, width = t0.shape
    out = jax.ShapeDtypeStruct((STEPS * rows, width), BF16)
    return pl.pallas_call(
        prepare_kernel,
        out_shape=out,
        in_specs=spaces(3),
        out_specs=pl.BlockSpec(memory_space=pltpu.VMEM),
        compiler_params=params(),
        cost_estimate=cost(0, t0, t1, t2, out),
        name="prepare",
    )(t0, t1, t2)


def turn_kernel(x, x_t):
    x_t[...] = x[...].T


def turned(x):
    out = jax.ShapeDtypeStruct(x.shape[::-1], BF16)
    return pl.pallas_call(
        turn_kernel,
        out_shape=out,
        in_specs=spaces(1),
        out_specs=pl.BlockSpec(memory_space=pltpu.VMEM),
        compiler_params=params(),
        cost_estimate=cost(0, x, out),
        name="turned",
    )(x)


def rows_of(ref, block, depth):
    return ref[pl.ds(pl.multiple_of(block * depth, 16), depth), :]


def picture_kernel(n_dp, x, x_t, units, sharp, bias, own, *rest):
    pieces, outs = rest[:8], rest[8 : 8 + len(SHARES)]
    grad, unit, w, proj, sem = rest[8 + len(SHARES) :]
    part, core, side = place(n_dp)
    depth = own.shape[0]
    half = depth // 2
    short = pieces[2].shape[0]
    rest_rows = half - short
    rows = x.shape[0]
    step = 1 - 2 * side
    copies = [
        pltpu.make_async_copy(
            own, w.at[pl.ds(pl.multiple_of(part * depth, 16), depth), :], sem.at[8]
        )
    ]
    for twin in (0, 1):
        lane = core if twin == 0 else 1 - core
        straight, crossed, two, two_crossed = pieces[4 * twin : 4 * twin + 4]
        for index, piece, from_part in ((0, straight, part + 4 - step), (1, crossed, part + 4 + step)):
            start = pl.multiple_of(lax.rem(from_part, 4) * depth + lane * half, 16)
            copies.append(
                pltpu.make_async_copy(piece, w.at[pl.ds(start, half), :], sem.at[4 * twin + index])
            )
        base = lax.rem(part + 2, 4) * depth + lane * half
        start = pl.multiple_of(base + side * rest_rows, 16)
        copies.append(
            pltpu.make_async_copy(two, w.at[pl.ds(start, short), :], sem.at[4 * twin + 2])
        )
        source = pl.multiple_of((1 - side) * (short - rest_rows), 16)
        start = pl.multiple_of(base + (1 - side) * short, 16)
        copies.append(
            pltpu.make_async_copy(
                two_crossed.at[pl.ds(source, rest_rows), :],
                w.at[pl.ds(start, rest_rows), :],
                sem.at[4 * twin + 3],
            )
        )
    for copy in copies:
        copy.start()
    for copy in copies:
        copy.wait()

    proj[...] = jnp.dot(x[...], w[...], preferred_element_type=F32)
    values = proj[...]
    inverse = 1.0 / jnp.sqrt(jnp.sum(values * values, axis=-1, keepdims=True) + EPS)
    unit[...] = (values * inverse).astype(BF16)
    scale = sharp[0]
    logits = scale * lax.dot_general(
        unit[...], units[...], (((1,), (1,)), ((), ())), preferred_element_type=F32
    ) + bias[0]
    coefficient = jax.nn.sigmoid(logits)
    row = lax.broadcasted_iota(jnp.int32, coefficient.shape, 0)
    column = lax.broadcasted_iota(jnp.int32, coefficient.shape, 1)
    coefficient = jnp.where(row == column, coefficient - 1.0, coefficient).astype(BF16)
    slope = scale * jnp.dot(coefficient, units[...], preferred_element_type=F32)
    direction = proj[...] * inverse
    along = jnp.sum(direction * slope, axis=-1, keepdims=True)
    grad[...] = ((slope - direction * along) * inverse).astype(BF16)
    inner = jnp.logical_or(part == 1, part == 2)

    @pl.when(inner)
    def _():
        block = rows_of(x_t, 3 * (part - 1), depth)
        begin = 0
        for out in outs:
            stop = begin + out.shape[1]
            out[...] = jnp.dot(block, grad[:, begin:stop], preferred_element_type=F32).astype(BF16)
            begin = stop

    @pl.when(jnp.logical_not(inner))
    def _():
        begin = 0
        for out in outs:
            stop = begin + out.shape[1]
            out[:rows, :] = grad[:, begin:stop]
            out[rows:, :] = jnp.zeros((depth - rows, stop - begin), BF16)
            begin = stop


def picture_side(n_dp, x, x_t, units, sharp, bias, own, pieces):
    rows, width = x.shape
    depth = own.shape[0]
    out = jax.ShapeDtypeStruct((rows, width), BF16)
    smem = pl.BlockSpec(memory_space=pltpu.SMEM)
    sizes = [width * share // sum(SHARES) for share in SHARES]
    outs = tuple(jax.ShapeDtypeStruct((depth, size), BF16) for size in sizes) + (out, out)
    return pl.pallas_call(
        functools.partial(picture_kernel, n_dp),
        out_shape=outs,
        in_specs=spaces(3) + [smem, smem] + [pl.BlockSpec(memory_space=pl.ANY)] * 9,
        out_specs=spaces(len(outs)),
        scratch_shapes=[
            pltpu.VMEM((width, width), BF16),
            pltpu.VMEM((rows, width), F32),
            pltpu.SemaphoreType.DMA((9,)),
        ],
        compiler_params=params(),
        cost_estimate=cost(2 * rows * width * (width + 2 * STEPS * rows), x, units, own, out, out),
        name="picture_side",
    )(x, x_t, units, sharp, bias, own, *pieces)


def text_kernel(text, u0, u1, u2, sharp, bias, out, units):
    rows = text.shape[0]
    for k, block in enumerate((u0, u1, u2)):
        units[k * rows : (k + 1) * rows, :] = block[...]
    values = text[...].astype(F32)
    inverse = 1.0 / jnp.sqrt(jnp.sum(values * values, axis=-1, keepdims=True) + EPS)
    direction = values * inverse
    scale = sharp[0]
    logits = scale * lax.dot_general(
        direction.astype(BF16), units[...], (((1,), (1,)), ((), ())), preferred_element_type=F32
    ) + bias[0]
    coefficient = jax.nn.sigmoid(logits)
    row = lax.broadcasted_iota(jnp.int32, coefficient.shape, 0)
    column = lax.broadcasted_iota(jnp.int32, coefficient.shape, 1)
    coefficient = jnp.where(row == column, coefficient - 1.0, coefficient).astype(BF16)
    slope = scale * jnp.dot(coefficient, units[...], preferred_element_type=F32)
    along = jnp.sum(direction * slope, axis=-1, keepdims=True)
    out[...] = (slope - direction * along) * inverse


def text_side(text, u0, u1, u2, sharp, bias):
    rows, width = text.shape
    out = jax.ShapeDtypeStruct((rows, width), F32)
    smem = pl.BlockSpec(memory_space=pltpu.SMEM)
    return pl.pallas_call(
        text_kernel,
        out_shape=out,
        in_specs=spaces(4) + [smem, smem],
        out_specs=pl.BlockSpec(memory_space=pltpu.VMEM),
        scratch_shapes=[pltpu.VMEM((STEPS * rows, width), BF16)],
        compiler_params=params(),
        cost_estimate=cost(4 * STEPS * rows * rows * width, text, u0, u1, u2, out),
        name="text_side",
    )(text, u0, u1, u2, sharp, bias)


def pair_kernel(begin, x_t, far_t, grad, arrived, kept, near, far):
    rows = grad.shape[0]
    depth, size = arrived.shape
    part = lax.axis_index("fsdp")
    inner = jnp.logical_or(part == 1, part == 2)
    mine = grad[:, begin : begin + size]

    def product(block):
        return jnp.dot(rows_of(x_t, block, depth), mine, preferred_element_type=F32)

    @pl.when(inner)
    def _():
        other = arrived[:rows, :]
        for block, out in ((3 - part, near), (lax.rem(part + 2, 4), far), (part, kept)):
            both = product(block) + jnp.dot(
                rows_of(far_t, block, depth), other, preferred_element_type=F32
            )
            out[...] = both.astype(out.dtype)

    @pl.when(jnp.logical_not(inner))
    def _():
        kept[...] = product(part) + arrived[...].astype(F32)
        near[...] = jnp.zeros_like(near)
        far[...] = jnp.zeros_like(far)


def pair_product(begin, x_t, far_t, grad, arrived):
    outs = tuple(jax.ShapeDtypeStruct(arrived.shape, t) for t in (F32, BF16, BF16))
    return pl.pallas_call(
        functools.partial(pair_kernel, begin),
        out_shape=outs,
        in_specs=spaces(4),
        out_specs=spaces(3),
        compiler_params=params(),
        cost_estimate=cost(12 * grad.shape[0] * arrived.size, x_t, far_t, grad, arrived, *outs),
        name="pair_product",
    )(x_t, far_t, grad, arrived)


def total_kernel(*refs):
    kept, near, far = (refs[k : len(refs) - 1 : 3] for k in range(3))
    out = refs[-1]
    begin = 0
    for a, b, c in zip(kept, near, far):
        stop = begin + a.shape[1]
        out[0, :, begin:stop] = a[...] + b[...].astype(F32) + c[...].astype(F32)
        begin = stop


def total(terms, depth, width):
    out = jax.ShapeDtypeStruct((1, depth, width), F32)
    return pl.pallas_call(
        total_kernel,
        out_shape=out,
        in_specs=spaces(len(terms)),
        out_specs=pl.BlockSpec(memory_space=pltpu.VMEM),
        compiler_params=params(),
        cost_estimate=cost(0, *terms, out),
        name="total",
    )(*terms)


def line_body(n_dp, n_fsdp, x, text, w, sharp, bias):
    depth, width = w.shape
    half = depth // 2
    short = (half // 2 + 15) // 16 * 16
    core = lax.rem(lax.axis_index("dp"), 2)
    side = n_dp // 2

    def along(value, pairs):
        return lax.ppermute(value, "fsdp", pairs)

    def across(value):
        return lax.ppermute(value, "dp", [(d, d ^ 1) for d in range(n_dp)])

    def over(value):
        return lax.ppermute(value, "dp", [(d, (d + side) % n_dp) for d in range(n_dp)])

    def shifted(value, by):
        return lax.ppermute(value, "dp", [(d, (d + by) % n_dp) for d in range(n_dp)])

    whole, piece = cut(n_dp, short, w)
    turns = [
        (d * n_fsdp + f, d * n_fsdp + (f + (1 if d < side else n_fsdp - 1)) % n_fsdp)
        for d in range(n_dp)
        for f in range(n_fsdp)
    ]
    straight = lax.ppermute(whole, ("dp", "fsdp"), turns)
    text2 = shifted(text, 2)
    two = along(piece, [(f, (f + 2) % n_fsdp) for f in range(n_fsdp)])
    far_x = along(x, [(0, 1), (3, 2)])
    crossed = over(straight)
    two_crossed = over(two)
    pieces = [straight, crossed, two, two_crossed]
    pieces = pieces + [across(piece) for piece in pieces]
    text1 = across(jnp.where(core == 0, text, text2))

    x_t, far_t = turned(x), turned(far_x)
    units = prepare(text, text1, text2)
    *outward, grad, unit = picture_side(n_dp, x, x_t, units, sharp, bias, w, pieces)

    arrived = [along(o, [(0, 1), (1, 0), (2, 3), (3, 2)]) for o in outward]
    begin, terms = 0, []
    for k, block in enumerate(arrived):
        kept, near, far = pair_product(begin, x_t, far_t, grad, block)
        begin += block.shape[1]
        if k == 0:
            unit, near, far = lax.optimization_barrier((unit, near, far))
        terms += [kept, along(near, [(1, 2), (2, 1)]), along(far, [(1, 3), (2, 0)])]
    unit2 = shifted(unit, -2)
    unit1 = across(jnp.where(core == 0, unit2, unit))
    text_grad = text_side(text, unit, unit1, unit2, sharp, bias)
    return total(terms, depth, width), text_grad


def plain_body(n_dp, n_fsdp, x, text, w, sharp, bias):
    def shifted(value, by):
        return lax.ppermute(value, "dp", [(d, (d + by) % n_dp) for d in range(n_dp)])

    rows, width = x.shape
    proj = jnp.dot(
        x, lax.all_gather(w, "fsdp", axis=0, tiled=True), preferred_element_type=F32
    )
    norm = jnp.sqrt(jnp.sum(proj * proj, axis=-1, keepdims=True) + EPS)
    direction = proj / norm
    unit = direction.astype(BF16)
    values = text.astype(F32)
    txt_norm = jnp.sqrt(jnp.sum(values * values, axis=-1, keepdims=True) + EPS)
    txt_dir = values / txt_norm
    slot = txt_dir.astype(BF16)
    scale = sharp[0]
    slope = jnp.zeros((rows, width), F32)
    txt_slope = jnp.zeros((rows, width), F32)
    for step in range(STEPS):
        if step > 0:
            slot = shifted(slot, 1)
        logits = scale * jnp.dot(unit, slot.T, preferred_element_type=F32) + bias[0]
        coefficient = jax.nn.sigmoid(logits)
        if step == 0:
            coefficient = coefficient - jnp.eye(rows, dtype=F32)
        coefficient = coefficient.astype(BF16)
        slope = slope + scale * jnp.dot(coefficient, slot, preferred_element_type=F32)
        share = scale * lax.dot_general(
            coefficient, unit, (((0,), (0,)), ((), ())), preferred_element_type=F32
        )
        if step > 0:
            share = shifted(share.astype(BF16), -step).astype(F32)
        txt_slope = txt_slope + share
    grad = (
        (slope - direction * jnp.sum(direction * slope, axis=-1, keepdims=True)) / norm
    ).astype(BF16)
    text_grad = (
        txt_slope - txt_dir * jnp.sum(txt_dir * txt_slope, axis=-1, keepdims=True)
    ) / txt_norm
    partial = lax.dot_general(
        x, grad, (((0,), (0,)), ((), ())), preferred_element_type=F32
    ).astype(BF16)
    head = lax.psum_scatter(partial, "fsdp", scatter_dimension=0, tiled=True).astype(F32)
    return head[None], text_grad


def solution(mesh):
    n_dp, n_fsdp = mesh.shape["dp"], mesh.shape["fsdp"]
    line = n_fsdp == 4 and n_dp % 4 == 0
    placed = (P(("dp", "fsdp"), None), P(("dp", "fsdp"), None), P("fsdp", None), P(), P())
    return jax.shard_map(
        functools.partial(line_body if line else plain_body, n_dp, n_fsdp),
        mesh=mesh,
        in_specs=placed,
        out_specs=(P("dp", "fsdp", None), P(("dp", "fsdp"), None)),
        check_vma=False,
    )
```

```python
import functools

import jax
import jax.numpy as jnp
from jax import lax
from jax.experimental import pallas as pl
from jax.experimental.pallas import tpu as pltpu
from jax.sharding import PartitionSpec as P

STEPS = 3
EPS = 1e-06
SHARES = (1, 2)
VMEM_BYTES = 24 * 1024 * 1024
BF16, F32 = jnp.bfloat16, jnp.float32


def spaces(count):
    return [pl.BlockSpec(memory_space=pltpu.VMEM)] * count


def params(size=VMEM_BYTES):
    return pltpu.CompilerParams(vmem_limit_bytes=size)


def cost():
    return pl.CostEstimate(flops=0, bytes_accessed=0, transcendentals=0)


IN_HBM = pl.BlockSpec(memory_space=pltpu.HBM)


def place(n_dp):
    where = lax.axis_index("dp")
    return lax.axis_index("fsdp"), lax.rem(where, 2), lax.div(where, n_dp // 2)


def cut_kernel(n_dp, short, own, whole, part, sem):
    _, core, side = place(n_dp)
    half = whole.shape[0]
    first = pltpu.make_async_copy(
        own.at[pl.ds(pl.multiple_of(core * half, 16), half), :], whole, sem.at[0]
    )
    start = pl.multiple_of(core * half + side * (half - short), 16)
    second = pltpu.make_async_copy(own.at[pl.ds(start, short), :], part, sem.at[1])
    first.start()
    second.start()
    first.wait()
    second.wait()


def cut(n_dp, short, own):
    half, width = own.shape[0] // 2, own.shape[1]
    outs = (
        jax.ShapeDtypeStruct((half, width), BF16),
        jax.ShapeDtypeStruct((short, width), BF16),
    )
    return pl.pallas_call(
        functools.partial(cut_kernel, n_dp, short),
        out_shape=outs,
        in_specs=[IN_HBM],
        out_specs=spaces(2),
        scratch_shapes=[pltpu.SemaphoreType.DMA((2,))],
        compiler_params=params(60 * 1024 * 1024),
        cost_estimate=cost(),
        name="cut",
    )(own)


def prepare_kernel(n_dp, t0, twin0, twin2, t2, _, units):
    rows = t0.shape[0]
    _, core, _ = place(n_dp)

    def fill(k, block):
        values = block[...].astype(F32)
        inverse = 1.0 / jnp.sqrt(jnp.sum(values * values, axis=-1, keepdims=True) + EPS)
        units[k * rows : (k + 1) * rows, :] = (values * inverse).astype(BF16)

    fill(0, t0)
    fill(2, t2)
    pl.when(core == 0)(lambda: fill(1, twin2))
    pl.when(core == 1)(lambda: fill(1, twin0))


def prepare(n_dp, t0, twin0, twin2, t2, after):
    rows, width = t0.shape
    out = jax.ShapeDtypeStruct((STEPS * rows, width), BF16)
    return pl.pallas_call(
        functools.partial(prepare_kernel, n_dp),
        out_shape=out,
        in_specs=spaces(5),
        out_specs=pl.BlockSpec(memory_space=pltpu.VMEM),
        compiler_params=params(),
        cost_estimate=cost(),
        name="prepare",
    )(t0, twin0, twin2, t2, after)


def turn_kernel(x, x_t):
    x_t[...] = x[...].T


def turned(x):
    out = jax.ShapeDtypeStruct(x.shape[::-1], BF16)
    return pl.pallas_call(
        turn_kernel,
        out_shape=out,
        in_specs=spaces(1),
        out_specs=pl.BlockSpec(memory_space=pltpu.VMEM),
        compiler_params=params(),
        cost_estimate=cost(),
        name="turned",
    )(x)


def rows_of(ref, block, depth):
    return ref[pl.ds(pl.multiple_of(block * depth, 16), depth), :]


def picture_kernel(n_dp, x, x_t, units, sharp, bias, own, *rest):
    pieces, outs = rest[:8], rest[8 : 8 + len(SHARES)]
    unit, grad, w, proj, sem = rest[8 + len(SHARES) :]
    part, core, side = place(n_dp)
    depth = own.shape[0]
    half = depth // 2
    short = pieces[2].shape[0]
    rest_rows = half - short
    rows = x.shape[0]
    step = 1 - 2 * side
    copies = [
        pltpu.make_async_copy(
            own, w.at[pl.ds(pl.multiple_of(part * depth, 16), depth), :], sem.at[8]
        )
    ]
    for twin in (0, 1):
        lane = core if twin == 0 else 1 - core
        straight, crossed, two, two_crossed = pieces[4 * twin : 4 * twin + 4]
        for index, piece, from_part in ((0, straight, part + 4 - step), (1, crossed, part + 4 + step)):
            start = pl.multiple_of(lax.rem(from_part, 4) * depth + lane * half, 16)
            copies.append(
                pltpu.make_async_copy(piece, w.at[pl.ds(start, half), :], sem.at[4 * twin + index])
            )
        base = lax.rem(part + 2, 4) * depth + lane * half
        start = pl.multiple_of(base + side * rest_rows, 16)
        copies.append(
            pltpu.make_async_copy(two, w.at[pl.ds(start, short), :], sem.at[4 * twin + 2])
        )
        source = pl.multiple_of((1 - side) * (short - rest_rows), 16)
        start = pl.multiple_of(base + (1 - side) * short, 16)
        copies.append(
            pltpu.make_async_copy(
                two_crossed.at[pl.ds(source, rest_rows), :],
                w.at[pl.ds(start, rest_rows), :],
                sem.at[4 * twin + 3],
            )
        )
    for copy in copies:
        copy.start()
    for copy in copies:
        copy.wait()

    proj[...] = jnp.dot(x[...], w[...], preferred_element_type=F32)
    values = proj[...]
    inverse = 1.0 / jnp.sqrt(jnp.sum(values * values, axis=-1, keepdims=True) + EPS)
    unit[...] = (values * inverse).astype(BF16)
    scale = sharp[0]
    logits = scale * lax.dot_general(
        unit[...], units[...], (((1,), (1,)), ((), ())), preferred_element_type=F32
    ) + bias[0]
    coefficient = jax.nn.sigmoid(logits)
    row = lax.broadcasted_iota(jnp.int32, coefficient.shape, 0)
    column = lax.broadcasted_iota(jnp.int32, coefficient.shape, 1)
    coefficient = jnp.where(row == column, coefficient - 1.0, coefficient).astype(BF16)
    slope = scale * jnp.dot(coefficient, units[...], preferred_element_type=F32)
    direction = proj[...] * inverse
    along = jnp.sum(direction * slope, axis=-1, keepdims=True)
    grad[...] = ((slope - direction * along) * inverse).astype(BF16)
    inner = jnp.logical_or(part == 1, part == 2)

    @pl.when(inner)
    def _():
        block = rows_of(x_t, 3 * (part - 1), depth)
        begin = 0
        for out in outs:
            stop = begin + out.shape[1]
            out[...] = jnp.dot(block, grad[:, begin:stop], preferred_element_type=F32).astype(BF16)
            begin = stop

    @pl.when(jnp.logical_not(inner))
    def _():
        begin = 0
        for out in outs:
            stop = begin + out.shape[1]
            out[:rows, :] = grad[:, begin:stop]
            out[rows:, :] = jnp.zeros((depth - rows, stop - begin), BF16)
            begin = stop


def picture_side(n_dp, x, x_t, units, sharp, bias, own, pieces):
    rows, width = x.shape
    depth = own.shape[0]
    out = jax.ShapeDtypeStruct((rows, width), BF16)
    smem = pl.BlockSpec(memory_space=pltpu.SMEM)
    sizes = [width * share // sum(SHARES) for share in SHARES]
    outs = tuple(jax.ShapeDtypeStruct((depth, size), BF16) for size in sizes)
    outs = outs + (out, out)
    return pl.pallas_call(
        functools.partial(picture_kernel, n_dp),
        out_shape=outs,
        in_specs=spaces(3) + [smem, smem] + [pl.BlockSpec(memory_space=pl.ANY)] * 9,
        out_specs=spaces(len(outs)),
        scratch_shapes=[
            pltpu.VMEM((width, width), BF16),
            pltpu.VMEM((rows, width), F32),
            pltpu.SemaphoreType.DMA((9,)),
        ],
        compiler_params=params(),
        cost_estimate=cost(),
        name="picture_side",
    )(x, x_t, units, sharp, bias, own, *pieces)


def text_kernel(n_dp, text, sharp, bias, u0, twin0, twin2, u2, out, done, units):
    rows = text.shape[0]
    _, core, _ = place(n_dp)
    done[...] = jnp.zeros_like(done)
    units[:rows, :] = u0[...]
    units[2 * rows :, :] = u2[...]
    for lane, block in ((0, twin0), (1, twin2)):

        @pl.when(core == lane)
        def _():
            units[rows : 2 * rows, :] = block[...]

    values = text[...].astype(F32)
    inverse = 1.0 / jnp.sqrt(jnp.sum(values * values, axis=-1, keepdims=True) + EPS)
    direction = values * inverse
    scale = sharp[0]
    logits = scale * lax.dot_general(
        direction.astype(BF16), units[...], (((1,), (1,)), ((), ())), preferred_element_type=F32
    ) + bias[0]
    coefficient = jax.nn.sigmoid(logits)
    row = lax.broadcasted_iota(jnp.int32, coefficient.shape, 0)
    column = lax.broadcasted_iota(jnp.int32, coefficient.shape, 1)
    coefficient = jnp.where(row == column, coefficient - 1.0, coefficient).astype(BF16)
    slope = scale * jnp.dot(coefficient, units[...], preferred_element_type=F32)
    along = jnp.sum(direction * slope, axis=-1, keepdims=True)
    out[...] = (slope - direction * along) * inverse


def text_side(n_dp, text, sharp, bias, *units):
    rows, width = text.shape
    smem = pl.BlockSpec(memory_space=pltpu.SMEM)
    return pl.pallas_call(
        functools.partial(text_kernel, n_dp),
        out_shape=(jax.ShapeDtypeStruct((rows, width), F32), jax.ShapeDtypeStruct((8, 128), F32)),
        in_specs=spaces(1) + [smem, smem] + spaces(4),
        out_specs=tuple(spaces(2)),
        scratch_shapes=[pltpu.VMEM((STEPS * rows, width), BF16)],
        compiler_params=params(),
        cost_estimate=cost(),
        name="text_side",
    )(text, sharp, bias, *units)


def pair_kernel(begin, x_t, far_t, grad, arrived, *rest):
    kept, near, far = rest[-3:]
    rows = grad.shape[0]
    depth, size = arrived.shape
    part = lax.axis_index("fsdp")
    inner = jnp.logical_or(part == 1, part == 2)
    mine = grad[:, begin : begin + size]

    def product(block):
        return jnp.dot(rows_of(x_t, block, depth), mine, preferred_element_type=F32)

    @pl.when(inner)
    def _():
        other = arrived[:rows, :]
        for block, out in ((3 - part, near), (lax.rem(part + 2, 4), far), (part, kept)):
            both = product(block) + jnp.dot(
                rows_of(far_t, block, depth), other, preferred_element_type=F32
            )
            out[...] = both.astype(out.dtype)

    @pl.when(jnp.logical_not(inner))
    def _():
        kept[...] = product(part) + arrived[...].astype(F32)
        near[...] = jnp.zeros_like(near)
        far[...] = jnp.zeros_like(far)


def pair_product(begin, x_t, far_t, grad, arrived, after):
    outs = tuple(jax.ShapeDtypeStruct(arrived.shape, t) for t in (F32, BF16, BF16))
    return pl.pallas_call(
        functools.partial(pair_kernel, begin),
        out_shape=outs,
        in_specs=spaces(4 + len(after)),
        out_specs=spaces(3),
        compiler_params=params(),
        cost_estimate=cost(),
        name="pair_product",
    )(x_t, far_t, grad, arrived, *after)


def total_kernel(begin, kept, near, far, *rest):
    out, summed, sem = rest[-3:]
    summed[...] = kept[...] + near[...].astype(F32) + far[...].astype(F32)
    copy = pltpu.make_async_copy(summed, out.at[0, :, begin : begin + kept.shape[1]], sem)
    copy.start()
    copy.wait()


def total(begin, width, kept, near, far, held):
    depth = kept.shape[0]
    return pl.pallas_call(
        functools.partial(total_kernel, begin),
        out_shape=jax.ShapeDtypeStruct((1, depth, width), F32),
        in_specs=spaces(3) + [IN_HBM] * len(held[:1]) + spaces(len(held[1:])),
        out_specs=IN_HBM,
        scratch_shapes=[pltpu.VMEM(kept.shape, F32), pltpu.SemaphoreType.DMA],
        input_output_aliases={3: 0} if held else {},
        compiler_params=params(),
        cost_estimate=cost(),
        name="total",
    )(kept, near, far, *held)


def line_body(n_dp, n_fsdp, x, text, w, sharp, bias):
    depth, width = w.shape
    half = depth // 2
    short = (half // 2 + 15) // 16 * 16
    core = lax.rem(lax.axis_index("dp"), 2)
    side = n_dp // 2

    def along(value, pairs):
        return lax.ppermute(value, "fsdp", pairs)

    def across(value):
        return lax.ppermute(value, "dp", [(d, d ^ 1) for d in range(n_dp)])

    def over(value):
        return lax.ppermute(value, "dp", [(d, (d + side) % n_dp) for d in range(n_dp)])

    def shifted(value, by):
        return lax.ppermute(value, "dp", [(d, (d + by) % n_dp) for d in range(n_dp)])

    whole, piece = cut(n_dp, short, w)
    turns = [
        (d * n_fsdp + f, d * n_fsdp + (f + (1 if d < side else n_fsdp - 1)) % n_fsdp)
        for d in range(n_dp)
        for f in range(n_fsdp)
    ]
    straight = lax.ppermute(whole, ("dp", "fsdp"), turns)
    text2 = shifted(text, 2)
    two = along(piece, [(f, (f + 2) % n_fsdp) for f in range(n_fsdp)])
    far_x = along(x, [(0, 1), (3, 2)])
    crossed = over(straight)
    two_crossed = over(two)
    pieces = [straight, crossed, two, two_crossed]
    pieces = pieces + [across(piece) for piece in pieces]
    x_t, far_t = turned(x), turned(far_x)
    units = prepare(n_dp, text, across(text), across(text2), text2, far_t)
    *outward, unit, grad = picture_side(n_dp, x, x_t, units, sharp, bias, w, pieces)

    arrived = [along(o, [(0, 1), (1, 0), (2, 3), (3, 2)]) for o in outward]
    unit2 = shifted(unit, -2)
    begin, terms, after = 0, [], []
    for block in arrived:
        kept, near, far = pair_product(begin, x_t, far_t, grad, block, after)
        near, far = along(near, [(1, 2), (2, 1)]), along(far, [(1, 3), (2, 0)])
        after = [near, far, unit2]
        terms.append((begin, width, kept, near, far))
        begin += block.shape[1]
    text_grad, done = text_side(n_dp, text, sharp, bias, unit, across(unit), across(unit2), unit2)
    head = total(*terms[0], [])
    for term in terms[1:]:
        head = total(*term, [head, done])
    return head, text_grad


def plain_body(n_dp, n_fsdp, x, text, w, sharp, bias):
    def shifted(value, by):
        return lax.ppermute(value, "dp", [(d, (d + by) % n_dp) for d in range(n_dp)])

    rows, width = x.shape
    proj = jnp.dot(
        x, lax.all_gather(w, "fsdp", axis=0, tiled=True), preferred_element_type=F32
    )
    norm = jnp.sqrt(jnp.sum(proj * proj, axis=-1, keepdims=True) + EPS)
    direction = proj / norm
    unit = direction.astype(BF16)
    values = text.astype(F32)
    txt_norm = jnp.sqrt(jnp.sum(values * values, axis=-1, keepdims=True) + EPS)
    txt_dir = values / txt_norm
    slot = txt_dir.astype(BF16)
    scale = sharp[0]
    slope = jnp.zeros((rows, width), F32)
    txt_slope = jnp.zeros((rows, width), F32)
    for step in range(STEPS):
        if step > 0:
            slot = shifted(slot, 1)
        logits = scale * jnp.dot(unit, slot.T, preferred_element_type=F32) + bias[0]
        coefficient = jax.nn.sigmoid(logits)
        if step == 0:
            coefficient = coefficient - jnp.eye(rows, dtype=F32)
        coefficient = coefficient.astype(BF16)
        slope = slope + scale * jnp.dot(coefficient, slot, preferred_element_type=F32)
        share = scale * lax.dot_general(
            coefficient, unit, (((0,), (0,)), ((), ())), preferred_element_type=F32
        )
        if step > 0:
            share = shifted(share.astype(BF16), -step).astype(F32)
        txt_slope = txt_slope + share
    grad = (
        (slope - direction * jnp.sum(direction * slope, axis=-1, keepdims=True)) / norm
    ).astype(BF16)
    text_grad = (
        txt_slope - txt_dir * jnp.sum(txt_dir * txt_slope, axis=-1, keepdims=True)
    ) / txt_norm
    partial = lax.dot_general(
        x, grad, (((0,), (0,)), ((), ())), preferred_element_type=F32
    ).astype(BF16)
    head = lax.psum_scatter(partial, "fsdp", scatter_dimension=0, tiled=True).astype(F32)
    return head[None], text_grad


def solution(mesh):
    n_dp, n_fsdp = mesh.shape["dp"], mesh.shape["fsdp"]
    line = n_fsdp == 4 and n_dp % 4 == 0
    placed = (P(("dp", "fsdp"), None), P(("dp", "fsdp"), None), P("fsdp", None), P(), P())
    return jax.shard_map(
        functools.partial(line_body if line else plain_body, n_dp, n_fsdp),
        mesh=mesh,
        in_specs=placed,
        out_specs=(P("dp", "fsdp", None), P(("dp", "fsdp"), None)),
        check_vma=False,
    )
```

```python
import functools

import jax
import jax.numpy as jnp
from jax import lax
from jax.experimental import pallas as pl
from jax.experimental.pallas import tpu as pltpu
from jax.sharding import PartitionSpec as P

STEPS = 3
EPS = 1e-06
SHARES = (1, 2)
UNIT_PARTS = 3
VMEM_BYTES = 24 * 1024 * 1024
BF16, F32 = jnp.bfloat16, jnp.float32


def spaces(count):
    return [pl.BlockSpec(memory_space=pltpu.VMEM)] * count


def params(size=VMEM_BYTES):
    return pltpu.CompilerParams(vmem_limit_bytes=size)


def cost():
    return pl.CostEstimate(flops=0, bytes_accessed=0, transcendentals=0)


IN_HBM = pl.BlockSpec(memory_space=pltpu.HBM)


def place(n_dp):
    where = lax.axis_index("dp")
    return lax.axis_index("fsdp"), lax.rem(where, 2), lax.div(where, n_dp // 2)


def cut_kernel(n_dp, short, own, whole, part, sem):
    _, core, side = place(n_dp)
    half = whole.shape[0]
    first = pltpu.make_async_copy(
        own.at[pl.ds(pl.multiple_of(core * half, 16), half), :], whole, sem.at[0]
    )
    start = pl.multiple_of(core * half + side * (half - short), 16)
    second = pltpu.make_async_copy(own.at[pl.ds(start, short), :], part, sem.at[1])
    first.start()
    second.start()
    first.wait()
    second.wait()


def cut(n_dp, short, own):
    half, width = own.shape[0] // 2, own.shape[1]
    outs = (
        jax.ShapeDtypeStruct((half, width), BF16),
        jax.ShapeDtypeStruct((short, width), BF16),
    )
    return pl.pallas_call(
        functools.partial(cut_kernel, n_dp, short),
        out_shape=outs,
        in_specs=[IN_HBM],
        out_specs=spaces(2),
        scratch_shapes=[pltpu.SemaphoreType.DMA((2,))],
        compiler_params=params(),
        cost_estimate=cost(),
        name="cut",
    )(own)


def prepare_kernel(n_dp, t0, twin0, twin2, t2, units):
    rows = t0.shape[0]
    _, core, _ = place(n_dp)

    def fill(k, block):
        values = block[...].astype(F32)
        inverse = 1.0 / jnp.sqrt(jnp.sum(values * values, axis=-1, keepdims=True) + EPS)
        units[k * rows : (k + 1) * rows, :] = (values * inverse).astype(BF16)

    fill(0, t0)
    fill(2, t2)
    pl.when(core == 0)(lambda: fill(1, twin2))
    pl.when(core == 1)(lambda: fill(1, twin0))


def prepare(n_dp, t0, twin0, twin2, t2):
    rows, width = t0.shape
    out = jax.ShapeDtypeStruct((STEPS * rows, width), BF16)
    return pl.pallas_call(
        functools.partial(prepare_kernel, n_dp),
        out_shape=out,
        in_specs=spaces(4),
        out_specs=pl.BlockSpec(memory_space=pltpu.VMEM),
        compiler_params=params(),
        cost_estimate=cost(),
        name="prepare",
    )(t0, twin0, twin2, t2)


def turn_kernel(x, _, x_t):
    x_t[...] = x[...].T


def turned(x, after):
    out = jax.ShapeDtypeStruct(x.shape[::-1], BF16)
    return pl.pallas_call(
        turn_kernel,
        out_shape=out,
        in_specs=spaces(2),
        out_specs=pl.BlockSpec(memory_space=pltpu.VMEM),
        compiler_params=params(),
        cost_estimate=cost(),
        name="turned",
    )(x, after)


def rows_of(ref, block, depth):
    return ref[pl.ds(pl.multiple_of(block * depth, 16), depth), :]


def picture_kernel(n_dp, x, x_t, units, sharp, bias, own, *rest):
    pieces, outs = rest[:8], rest[8 : 8 + len(SHARES)]
    unit_parts = rest[8 + len(SHARES) : -5]
    grad, unit, w, proj, sem = rest[-5:]
    part, core, side = place(n_dp)
    depth = own.shape[0]
    half = depth // 2
    short = pieces[2].shape[0]
    rest_rows = half - short
    rows = x.shape[0]
    step = 1 - 2 * side
    copies = [
        pltpu.make_async_copy(
            own, w.at[pl.ds(pl.multiple_of(part * depth, 16), depth), :], sem.at[8]
        )
    ]
    for twin in (0, 1):
        lane = core if twin == 0 else 1 - core
        straight, crossed, two, two_crossed = pieces[4 * twin : 4 * twin + 4]
        for index, piece, from_part in ((0, straight, part + 4 - step), (1, crossed, part + 4 + step)):
            start = pl.multiple_of(lax.rem(from_part, 4) * depth + lane * half, 16)
            copies.append(
                pltpu.make_async_copy(piece, w.at[pl.ds(start, half), :], sem.at[4 * twin + index])
            )
        base = lax.rem(part + 2, 4) * depth + lane * half
        start = pl.multiple_of(base + side * rest_rows, 16)
        copies.append(
            pltpu.make_async_copy(two, w.at[pl.ds(start, short), :], sem.at[4 * twin + 2])
        )
        source = pl.multiple_of((1 - side) * (short - rest_rows), 16)
        start = pl.multiple_of(base + (1 - side) * short, 16)
        copies.append(
            pltpu.make_async_copy(
                two_crossed.at[pl.ds(source, rest_rows), :],
                w.at[pl.ds(start, rest_rows), :],
                sem.at[4 * twin + 3],
            )
        )
    for copy in copies:
        copy.start()
    for copy in copies:
        copy.wait()

    proj[...] = jnp.dot(x[...], w[...], preferred_element_type=F32)
    values = proj[...]
    inverse = 1.0 / jnp.sqrt(jnp.sum(values * values, axis=-1, keepdims=True) + EPS)
    unit[...] = (values * inverse).astype(BF16)
    size = unit.shape[1] // UNIT_PARTS
    for k, out in enumerate(unit_parts):
        out[...] = unit[:, k * size : (k + 1) * size]
    scale = sharp[...]
    logits = scale * lax.dot_general(
        unit[...], units[...], (((1,), (1,)), ((), ())), preferred_element_type=F32
    ) + bias[...]
    coefficient = jax.nn.sigmoid(logits)
    row = lax.broadcasted_iota(jnp.int32, coefficient.shape, 0)
    column = lax.broadcasted_iota(jnp.int32, coefficient.shape, 1)
    coefficient = jnp.where(row == column, coefficient - 1.0, coefficient).astype(BF16)
    slope = scale * jnp.dot(coefficient, units[...], preferred_element_type=F32)
    direction = proj[...] * inverse
    along = jnp.sum(direction * slope, axis=-1, keepdims=True)
    grad[...] = ((slope - direction * along) * inverse).astype(BF16)
    inner = jnp.logical_or(part == 1, part == 2)

    @pl.when(inner)
    def _():
        block = rows_of(x_t, 3 * (part - 1), depth)
        begin = 0
        for out in outs:
            stop = begin + out.shape[1]
            out[...] = jnp.dot(block, grad[:, begin:stop], preferred_element_type=F32).astype(BF16)
            begin = stop

    @pl.when(jnp.logical_not(inner))
    def _():
        begin = 0
        for out in outs:
            stop = begin + out.shape[1]
            out[:rows, :] = grad[:, begin:stop]
            out[rows:, :] = jnp.zeros((depth - rows, stop - begin), BF16)
            begin = stop


def picture_side(n_dp, x, x_t, units, sharp, bias, own, pieces):
    rows, width = x.shape
    depth = own.shape[0]
    out = jax.ShapeDtypeStruct((rows, width), BF16)
    sizes = [width * share // sum(SHARES) for share in SHARES]
    outs = tuple(jax.ShapeDtypeStruct((depth, size), BF16) for size in sizes)
    part = jax.ShapeDtypeStruct((rows, width // UNIT_PARTS), BF16)
    outs = outs + (part,) * UNIT_PARTS + (out,)
    return pl.pallas_call(
        functools.partial(picture_kernel, n_dp),
        out_shape=outs,
        in_specs=spaces(3) + spaces(2) + [pl.BlockSpec(memory_space=pl.ANY)] * 9,
        out_specs=spaces(len(outs)),
        scratch_shapes=[
            pltpu.VMEM((rows, width), BF16),
            pltpu.VMEM((width, width), BF16),
            pltpu.VMEM((rows, width), F32),
            pltpu.SemaphoreType.DMA((9,)),
        ],
        compiler_params=params(),
        cost_estimate=cost(),
        name="picture_side",
    )(x, x_t, units, sharp, bias, own, *pieces)


def text_kernel(n_dp, text, sharp, bias, *refs):
    blocks, (out, done, units) = refs[:-3], refs[-3:]
    rows = text.shape[0]
    _, core, _ = place(n_dp)
    done[...] = jnp.zeros_like(done)
    size = blocks[0].shape[1]
    for k in range(UNIT_PARTS):
        u0, twin0, twin2, u2 = blocks[k::UNIT_PARTS]
        columns = slice(k * size, (k + 1) * size)
        units[:rows, columns] = u0[...]
        units[2 * rows :, columns] = u2[...]
        for lane, block in ((0, twin0), (1, twin2)):

            @pl.when(core == lane)
            def _():
                units[rows : 2 * rows, columns] = block[...]

    values = text[...].astype(F32)
    inverse = 1.0 / jnp.sqrt(jnp.sum(values * values, axis=-1, keepdims=True) + EPS)
    direction = values * inverse
    scale = sharp[...]
    logits = scale * lax.dot_general(
        direction.astype(BF16), units[...], (((1,), (1,)), ((), ())), preferred_element_type=F32
    ) + bias[...]
    coefficient = jax.nn.sigmoid(logits)
    row = lax.broadcasted_iota(jnp.int32, coefficient.shape, 0)
    column = lax.broadcasted_iota(jnp.int32, coefficient.shape, 1)
    coefficient = jnp.where(row == column, coefficient - 1.0, coefficient).astype(BF16)
    slope = scale * jnp.dot(coefficient, units[...], preferred_element_type=F32)
    along = jnp.sum(direction * slope, axis=-1, keepdims=True)
    out[...] = (slope - direction * along) * inverse


def text_side(n_dp, text, sharp, bias, *units):
    rows, width = text.shape
    return pl.pallas_call(
        functools.partial(text_kernel, n_dp),
        out_shape=(jax.ShapeDtypeStruct((rows, width), F32), jax.ShapeDtypeStruct((8, 128), F32)),
        in_specs=spaces(3 + 4 * UNIT_PARTS),
        out_specs=tuple(spaces(2)),
        scratch_shapes=[pltpu.VMEM((STEPS * rows, width), BF16)],
        compiler_params=params(),
        cost_estimate=cost(),
        name="text_side",
    )(text, sharp, bias, *units)


def pair_kernel(begin, x_t, far_t, grad, arrived, *rest):
    kept, near, far = rest[-3:]
    rows = grad.shape[0]
    depth, size = arrived.shape
    part = lax.axis_index("fsdp")
    inner = jnp.logical_or(part == 1, part == 2)
    mine = grad[:, begin : begin + size]

    def product(block):
        return jnp.dot(rows_of(x_t, block, depth), mine, preferred_element_type=F32)

    @pl.when(inner)
    def _():
        other = arrived[:rows, :]
        for block, out in ((3 - part, near), (lax.rem(part + 2, 4), far), (part, kept)):
            both = product(block) + jnp.dot(
                rows_of(far_t, block, depth), other, preferred_element_type=F32
            )
            out[...] = both.astype(out.dtype)

    @pl.when(jnp.logical_not(inner))
    def _():
        kept[...] = product(part) + arrived[...].astype(F32)
        near[...] = jnp.zeros_like(near)
        far[...] = jnp.zeros_like(far)


def pair_product(begin, x_t, far_t, grad, arrived, after):
    outs = tuple(jax.ShapeDtypeStruct(arrived.shape, t) for t in (F32, BF16, BF16))
    return pl.pallas_call(
        functools.partial(pair_kernel, begin),
        out_shape=outs,
        in_specs=spaces(4 + len(after)),
        out_specs=spaces(3),
        compiler_params=params(),
        cost_estimate=cost(),
        name="pair_product",
    )(x_t, far_t, grad, arrived, *after)


def total_kernel(begin, kept, near, far, *rest):
    out, summed, sem = rest[-3:]
    summed[...] = kept[...] + near[...].astype(F32) + far[...].astype(F32)
    copy = pltpu.make_async_copy(summed, out.at[0, :, begin : begin + kept.shape[1]], sem)
    copy.start()
    copy.wait()


def total(begin, width, kept, near, far, held):
    depth = kept.shape[0]
    return pl.pallas_call(
        functools.partial(total_kernel, begin),
        out_shape=jax.ShapeDtypeStruct((1, depth, width), F32),
        in_specs=spaces(3) + [IN_HBM] * len(held[:1]) + spaces(len(held[1:])),
        out_specs=IN_HBM,
        scratch_shapes=[pltpu.VMEM(kept.shape, F32), pltpu.SemaphoreType.DMA],
        input_output_aliases={3: 0} if held else {},
        compiler_params=params(),
        cost_estimate=cost(),
        name="total",
    )(kept, near, far, *held)


def line_body(n_dp, n_fsdp, x, text, w, sharp, bias):
    depth, width = w.shape
    half = depth // 2
    short = (half // 2 + 15) // 16 * 16
    core = lax.rem(lax.axis_index("dp"), 2)
    side = n_dp // 2

    def along(value, pairs):
        return lax.ppermute(value, "fsdp", pairs)

    def across(value):
        return lax.ppermute(value, "dp", [(d, d ^ 1) for d in range(n_dp)])

    def over(value):
        return lax.ppermute(value, "dp", [(d, (d + side) % n_dp) for d in range(n_dp)])

    def shifted(value, by):
        return lax.ppermute(value, "dp", [(d, (d + by) % n_dp) for d in range(n_dp)])

    sharp, bias = sharp.reshape(1, 1), bias.reshape(1, 1)
    whole, piece = cut(n_dp, short, w)
    whole, piece, text = lax.optimization_barrier((whole, piece, text))
    turns = [
        (d * n_fsdp + f, d * n_fsdp + (f + (1 if d < side else n_fsdp - 1)) % n_fsdp)
        for d in range(n_dp)
        for f in range(n_fsdp)
    ]
    straight = lax.ppermute(whole, ("dp", "fsdp"), turns)
    text2 = shifted(text, 2)
    two = along(piece, [(f, (f + 2) % n_fsdp) for f in range(n_fsdp)])
    text2, two = lax.optimization_barrier((text2, two))
    crossed = over(straight)
    two_crossed = over(two)
    pieces = [straight, crossed, two, two_crossed]
    pieces = pieces + [across(piece) for piece in pieces]
    x_t = turned(x, text2)
    far_t = along(x_t, [(0, 1), (3, 2)])
    units = prepare(n_dp, text, across(text), across(text2), text2)
    results = picture_side(n_dp, x, x_t, units, sharp, bias, w, pieces)
    outward, unit, grad = results[: len(SHARES)], results[len(SHARES) : -1], results[-1]

    arrived = []
    for block in outward:
        if arrived:
            block, arrived[-1] = lax.optimization_barrier((block, arrived[-1]))
        arrived.append(along(block, [(0, 1), (1, 0), (2, 3), (3, 2)]))
    unit2 = [shifted(u, -2) for u in unit]
    begin, terms, after = 0, [], []
    for block in arrived:
        kept, near, far = pair_product(begin, x_t, far_t, grad, block, after)
        near, far = along(near, [(1, 2), (2, 1)]), along(far, [(1, 3), (2, 0)])
        after = [near, far]
        terms.append((begin, width, kept, near, far))
        begin += block.shape[1]
    twin0, twin2 = [across(u) for u in unit], [across(u) for u in unit2]
    text_grad, done = text_side(n_dp, text, sharp, bias, *unit, *twin0, *twin2, *unit2)
    head = total(*terms[0], [])
    for term in terms[1:]:
        head = total(*term, [head, done])
    return head, text_grad


def plain_body(n_dp, n_fsdp, x, text, w, sharp, bias):
    def shifted(value, by):
        return lax.ppermute(value, "dp", [(d, (d + by) % n_dp) for d in range(n_dp)])

    rows, width = x.shape
    proj = jnp.dot(
        x, lax.all_gather(w, "fsdp", axis=0, tiled=True), preferred_element_type=F32
    )
    norm = jnp.sqrt(jnp.sum(proj * proj, axis=-1, keepdims=True) + EPS)
    direction = proj / norm
    unit = direction.astype(BF16)
    values = text.astype(F32)
    txt_norm = jnp.sqrt(jnp.sum(values * values, axis=-1, keepdims=True) + EPS)
    txt_dir = values / txt_norm
    slot = txt_dir.astype(BF16)
    scale = sharp[0]
    slope = jnp.zeros((rows, width), F32)
    txt_slope = jnp.zeros((rows, width), F32)
    for step in range(STEPS):
        if step > 0:
            slot = shifted(slot, 1)
        logits = scale * jnp.dot(unit, slot.T, preferred_element_type=F32) + bias[0]
        coefficient = jax.nn.sigmoid(logits)
        if step == 0:
            coefficient = coefficient - jnp.eye(rows, dtype=F32)
        coefficient = coefficient.astype(BF16)
        slope = slope + scale * jnp.dot(coefficient, slot, preferred_element_type=F32)
        share = scale * lax.dot_general(
            coefficient, unit, (((0,), (0,)), ((), ())), preferred_element_type=F32
        )
        if step > 0:
            share = shifted(share.astype(BF16), -step).astype(F32)
        txt_slope = txt_slope + share
    grad = (
        (slope - direction * jnp.sum(direction * slope, axis=-1, keepdims=True)) / norm
    ).astype(BF16)
    text_grad = (
        txt_slope - txt_dir * jnp.sum(txt_dir * txt_slope, axis=-1, keepdims=True)
    ) / txt_norm
    partial = lax.dot_general(
        x, grad, (((0,), (0,)), ((), ())), preferred_element_type=F32
    ).astype(BF16)
    head = lax.psum_scatter(partial, "fsdp", scatter_dimension=0, tiled=True).astype(F32)
    return head[None], text_grad


def solution(mesh):
    n_dp, n_fsdp = mesh.shape["dp"], mesh.shape["fsdp"]
    line = n_fsdp == 4 and n_dp % 4 == 0
    placed = (P(("dp", "fsdp"), None), P(("dp", "fsdp"), None), P("fsdp", None), P(), P())
    return jax.shard_map(
        functools.partial(line_body if line else plain_body, n_dp, n_fsdp),
        mesh=mesh,
        in_specs=placed,
        out_specs=(P("dp", "fsdp", None), P(("dp", "fsdp"), None)),
        check_vma=False,
    )
```

```python
import functools

import jax
import jax.numpy as jnp
from jax import lax
from jax.experimental import pallas as pl
from jax.experimental.pallas import tpu as pltpu
from jax.sharding import PartitionSpec as P

STEPS = 3
EPS = 1e-06
SHARES = (1, 2)
UNIT_PARTS = 3
VMEM_BYTES = 24 * 1024 * 1024
BF16, F32 = jnp.bfloat16, jnp.float32


def spaces(count):
    return [pl.BlockSpec(memory_space=pltpu.VMEM)] * count


def params(size=VMEM_BYTES):
    return pltpu.CompilerParams(vmem_limit_bytes=size)


def cost():
    return pl.CostEstimate(flops=0, bytes_accessed=0, transcendentals=0)


IN_HBM = pl.BlockSpec(memory_space=pltpu.HBM)


def place(n_dp):
    where = lax.axis_index("dp")
    return lax.axis_index("fsdp"), lax.rem(where, 2), lax.div(where, n_dp // 2)


def cut_kernel(n_dp, short, own, whole, part, sem):
    _, core, side = place(n_dp)
    half = whole.shape[0]
    first = pltpu.make_async_copy(
        own.at[pl.ds(pl.multiple_of(core * half, 16), half), :], whole, sem.at[0]
    )
    start = pl.multiple_of(core * half + side * (half - short), 16)
    second = pltpu.make_async_copy(own.at[pl.ds(start, short), :], part, sem.at[1])
    first.start()
    second.start()
    first.wait()
    second.wait()


def cut(n_dp, short, own):
    half, width = own.shape[0] // 2, own.shape[1]
    outs = (
        jax.ShapeDtypeStruct((half, width), BF16),
        jax.ShapeDtypeStruct((short, width), BF16),
    )
    return pl.pallas_call(
        functools.partial(cut_kernel, n_dp, short),
        out_shape=outs,
        in_specs=[IN_HBM],
        out_specs=spaces(2),
        scratch_shapes=[pltpu.SemaphoreType.DMA((2,))],
        compiler_params=params(),
        cost_estimate=cost(),
        name="cut",
    )(own)


def prepare_kernel(n_dp, t0, twin0, twin2, t2, sharp, bias, units, scalars):
    rows = t0.shape[0]
    scalars[0:1, :] = jnp.broadcast_to(sharp[...], (1, scalars.shape[1]))
    scalars[1:2, :] = jnp.broadcast_to(bias[...], (1, scalars.shape[1]))
    _, core, _ = place(n_dp)

    def fill(k, block):
        values = block[...].astype(F32)
        inverse = 1.0 / jnp.sqrt(jnp.sum(values * values, axis=-1, keepdims=True) + EPS)
        units[k * rows : (k + 1) * rows, :] = (values * inverse).astype(BF16)

    fill(0, t0)
    fill(2, t2)
    pl.when(core == 0)(lambda: fill(1, twin2))
    pl.when(core == 1)(lambda: fill(1, twin0))


def prepare(n_dp, t0, twin0, twin2, t2, sharp, bias):
    rows, width = t0.shape
    return pl.pallas_call(
        functools.partial(prepare_kernel, n_dp),
        out_shape=(
            jax.ShapeDtypeStruct((STEPS * rows, width), BF16),
            jax.ShapeDtypeStruct((8, 128), F32),
        ),
        in_specs=spaces(6),
        out_specs=tuple(spaces(2)),
        compiler_params=params(),
        cost_estimate=cost(),
        name="prepare",
    )(t0, twin0, twin2, t2, sharp, bias)


def turn_kernel(x, x_t):
    x_t[...] = x[...].T


def turned(x):
    out = jax.ShapeDtypeStruct(x.shape[::-1], BF16)
    return pl.pallas_call(
        turn_kernel,
        out_shape=out,
        in_specs=spaces(1),
        out_specs=pl.BlockSpec(memory_space=pltpu.VMEM),
        compiler_params=params(),
        cost_estimate=cost(),
        name="turned",
    )(x)


def rows_of(ref, block, depth):
    return ref[pl.ds(pl.multiple_of(block * depth, 16), depth), :]


def picture_kernel(n_dp, x, x_t, units, scalars, own, *rest):
    pieces, outs = rest[:8], rest[8 : 8 + len(SHARES)]
    unit_parts = rest[8 + len(SHARES) : -5]
    grad, unit, w, proj, sem = rest[-5:]
    part, core, side = place(n_dp)
    depth = own.shape[0]
    half = depth // 2
    short = pieces[2].shape[0]
    rest_rows = half - short
    rows = x.shape[0]
    step = 1 - 2 * side
    copies = [
        pltpu.make_async_copy(
            own, w.at[pl.ds(pl.multiple_of(part * depth, 16), depth), :], sem.at[8]
        )
    ]
    for twin in (0, 1):
        lane = core if twin == 0 else 1 - core
        straight, crossed, two, two_crossed = pieces[4 * twin : 4 * twin + 4]
        for index, piece, from_part in ((0, straight, part + 4 - step), (1, crossed, part + 4 + step)):
            start = pl.multiple_of(lax.rem(from_part, 4) * depth + lane * half, 16)
            copies.append(
                pltpu.make_async_copy(piece, w.at[pl.ds(start, half), :], sem.at[4 * twin + index])
            )
        base = lax.rem(part + 2, 4) * depth + lane * half
        start = pl.multiple_of(base + side * rest_rows, 16)
        copies.append(
            pltpu.make_async_copy(two, w.at[pl.ds(start, short), :], sem.at[4 * twin + 2])
        )
        source = pl.multiple_of((1 - side) * (short - rest_rows), 16)
        start = pl.multiple_of(base + (1 - side) * short, 16)
        copies.append(
            pltpu.make_async_copy(
                two_crossed.at[pl.ds(source, rest_rows), :],
                w.at[pl.ds(start, rest_rows), :],
                sem.at[4 * twin + 3],
            )
        )
    for copy in copies:
        copy.start()
    for copy in copies:
        copy.wait()

    proj[...] = jnp.dot(x[...], w[...], preferred_element_type=F32)
    values = proj[...]
    inverse = 1.0 / jnp.sqrt(jnp.sum(values * values, axis=-1, keepdims=True) + EPS)
    unit[...] = (values * inverse).astype(BF16)
    size = unit.shape[1] // UNIT_PARTS
    for k, out in enumerate(unit_parts):
        out[...] = unit[:, k * size : (k + 1) * size]
    scale = scalars[0:1, 0:1]
    logits = scale * lax.dot_general(
        unit[...], units[...], (((1,), (1,)), ((), ())), preferred_element_type=F32
    ) + scalars[1:2, 0:1]
    coefficient = jax.nn.sigmoid(logits)
    row = lax.broadcasted_iota(jnp.int32, coefficient.shape, 0)
    column = lax.broadcasted_iota(jnp.int32, coefficient.shape, 1)
    coefficient = jnp.where(row == column, coefficient - 1.0, coefficient).astype(BF16)
    slope = scale * jnp.dot(coefficient, units[...], preferred_element_type=F32)
    direction = proj[...] * inverse
    along = jnp.sum(direction * slope, axis=-1, keepdims=True)
    grad[...] = ((slope - direction * along) * inverse).astype(BF16)
    inner = jnp.logical_or(part == 1, part == 2)

    @pl.when(inner)
    def _():
        block = rows_of(x_t, 3 * (part - 1), depth)
        begin = 0
        for out in outs:
            stop = begin + out.shape[1]
            out[...] = jnp.dot(block, grad[:, begin:stop], preferred_element_type=F32).astype(BF16)
            begin = stop

    @pl.when(jnp.logical_not(inner))
    def _():
        begin = 0
        for out in outs:
            stop = begin + out.shape[1]
            out[:rows, :] = grad[:, begin:stop]
            out[rows:, :] = jnp.zeros((depth - rows, stop - begin), BF16)
            begin = stop


def picture_side(n_dp, x, x_t, units, scalars, own, pieces):
    rows, width = x.shape
    depth = own.shape[0]
    out = jax.ShapeDtypeStruct((rows, width), BF16)
    sizes = [width * share // sum(SHARES) for share in SHARES]
    outs = tuple(jax.ShapeDtypeStruct((depth, size), BF16) for size in sizes)
    part = jax.ShapeDtypeStruct((rows, width // UNIT_PARTS), BF16)
    outs = outs + (part,) * UNIT_PARTS + (out,)
    return pl.pallas_call(
        functools.partial(picture_kernel, n_dp),
        out_shape=outs,
        in_specs=spaces(4) + [pl.BlockSpec(memory_space=pl.ANY)] * 9,
        out_specs=spaces(len(outs)),
        scratch_shapes=[
            pltpu.VMEM((rows, width), BF16),
            pltpu.VMEM((width, width), BF16),
            pltpu.VMEM((rows, width), F32),
            pltpu.SemaphoreType.DMA((9,)),
        ],
        compiler_params=params(),
        cost_estimate=cost(),
        name="picture_side",
    )(x, x_t, units, scalars, own, *pieces)


def text_kernel(n_dp, text, scalars, *refs):
    blocks, (out, done, units) = refs[:-3], refs[-3:]
    rows = text.shape[0]
    _, core, _ = place(n_dp)
    done[...] = jnp.zeros_like(done)
    size = blocks[0].shape[1]
    for k in range(UNIT_PARTS):
        u0, twin0, twin2, u2 = blocks[k::UNIT_PARTS]
        columns = slice(k * size, (k + 1) * size)
        units[:rows, columns] = u0[...]
        units[2 * rows :, columns] = u2[...]
        for lane, block in ((0, twin0), (1, twin2)):

            @pl.when(core == lane)
            def _():
                units[rows : 2 * rows, columns] = block[...]

    values = text[...].astype(F32)
    inverse = 1.0 / jnp.sqrt(jnp.sum(values * values, axis=-1, keepdims=True) + EPS)
    direction = values * inverse
    scale = scalars[0:1, 0:1]
    logits = scale * lax.dot_general(
        direction.astype(BF16), units[...], (((1,), (1,)), ((), ())), preferred_element_type=F32
    ) + scalars[1:2, 0:1]
    coefficient = jax.nn.sigmoid(logits)
    row = lax.broadcasted_iota(jnp.int32, coefficient.shape, 0)
    column = lax.broadcasted_iota(jnp.int32, coefficient.shape, 1)
    coefficient = jnp.where(row == column, coefficient - 1.0, coefficient).astype(BF16)
    slope = scale * jnp.dot(coefficient, units[...], preferred_element_type=F32)
    along = jnp.sum(direction * slope, axis=-1, keepdims=True)
    out[...] = (slope - direction * along) * inverse


def text_side(n_dp, text, scalars, *units):
    rows, width = text.shape
    return pl.pallas_call(
        functools.partial(text_kernel, n_dp),
        out_shape=(jax.ShapeDtypeStruct((rows, width), F32), jax.ShapeDtypeStruct((8, 128), F32)),
        in_specs=spaces(2 + 4 * UNIT_PARTS),
        out_specs=tuple(spaces(2)),
        scratch_shapes=[pltpu.VMEM((STEPS * rows, width), BF16)],
        compiler_params=params(),
        cost_estimate=cost(),
        name="text_side",
    )(text, scalars, *units)


def pair_kernel(begin, x_t, far_t, grad, arrived, *rest):
    kept, near, far = rest[-3:]
    rows = grad.shape[0]
    depth, size = arrived.shape
    part = lax.axis_index("fsdp")
    inner = jnp.logical_or(part == 1, part == 2)
    mine = grad[:, begin : begin + size]

    def product(block):
        return jnp.dot(rows_of(x_t, block, depth), mine, preferred_element_type=F32)

    @pl.when(inner)
    def _():
        other = arrived[:rows, :]
        for block, out in ((3 - part, near), (lax.rem(part + 2, 4), far), (part, kept)):
            both = product(block) + jnp.dot(
                rows_of(far_t, block, depth), other, preferred_element_type=F32
            )
            out[...] = both.astype(out.dtype)

    @pl.when(jnp.logical_not(inner))
    def _():
        kept[...] = product(part) + arrived[...].astype(F32)
        near[...] = jnp.zeros_like(near)
        far[...] = jnp.zeros_like(far)


def pair_product(begin, x_t, far_t, grad, arrived, after):
    outs = tuple(jax.ShapeDtypeStruct(arrived.shape, t) for t in (F32, BF16, BF16))
    return pl.pallas_call(
        functools.partial(pair_kernel, begin),
        out_shape=outs,
        in_specs=spaces(4 + len(after)),
        out_specs=spaces(3),
        compiler_params=params(),
        cost_estimate=cost(),
        name="pair_product",
    )(x_t, far_t, grad, arrived, *after)


def total_kernel(begin, kept, near, far, *rest):
    out, summed, sem = rest[-3:]
    summed[...] = kept[...] + near[...].astype(F32) + far[...].astype(F32)
    copy = pltpu.make_async_copy(summed, out.at[0, :, begin : begin + kept.shape[1]], sem)
    copy.start()
    copy.wait()


def total(begin, width, kept, near, far, held):
    depth = kept.shape[0]
    return pl.pallas_call(
        functools.partial(total_kernel, begin),
        out_shape=jax.ShapeDtypeStruct((1, depth, width), F32),
        in_specs=spaces(3) + [IN_HBM] * len(held[:1]) + spaces(len(held[1:])),
        out_specs=IN_HBM,
        scratch_shapes=[pltpu.VMEM(kept.shape, F32), pltpu.SemaphoreType.DMA],
        input_output_aliases={3: 0} if held else {},
        compiler_params=params(),
        cost_estimate=cost(),
        name="total",
    )(kept, near, far, *held)


def line_body(n_dp, n_fsdp, x, text, w, sharp, bias):
    depth, width = w.shape
    half = depth // 2
    short = (half // 2 + 15) // 16 * 16
    core = lax.rem(lax.axis_index("dp"), 2)
    side = n_dp // 2

    def along(value, pairs):
        return lax.ppermute(value, "fsdp", pairs)

    def across(value):
        return lax.ppermute(value, "dp", [(d, d ^ 1) for d in range(n_dp)])

    def over(value):
        return lax.ppermute(value, "dp", [(d, (d + side) % n_dp) for d in range(n_dp)])

    def shifted(value, by):
        return lax.ppermute(value, "dp", [(d, (d + by) % n_dp) for d in range(n_dp)])

    sharp, bias = sharp.reshape(1, 1), bias.reshape(1, 1)
    swap = [(0, 1), (1, 0), (2, 3), (3, 2)]
    whole, piece = cut(n_dp, short, w)
    whole, piece, text = lax.optimization_barrier((whole, piece, text))
    turns = [
        (d * n_fsdp + f, d * n_fsdp + (f + (1 if d < side else n_fsdp - 1)) % n_fsdp)
        for d in range(n_dp)
        for f in range(n_fsdp)
    ]
    straight = lax.ppermute(whole, ("dp", "fsdp"), turns)
    text2 = shifted(text, 2)
    piece, straight = lax.optimization_barrier((piece, straight))
    crossed = over(straight)
    two = along(piece, [(f, (f + 2) % n_fsdp) for f in range(n_fsdp)])
    two, x = lax.optimization_barrier((two, x))
    two_crossed = over(two)
    far_x = along(x, swap)
    x_t = turned(x)
    crossed, x_t, text2 = lax.optimization_barrier((crossed, x_t, text2))
    units, scalars = prepare(n_dp, text, across(text), across(text2), text2, sharp, bias)
    two_crossed, units, scalars = lax.optimization_barrier((two_crossed, units, scalars))
    pieces = [straight, crossed, two, two_crossed]
    pieces = pieces + [across(piece) for piece in pieces]
    results = picture_side(n_dp, x, x_t, units, scalars, w, pieces)
    outward, unit, grad = list(results[: len(SHARES)]), results[len(SHARES) : -1], results[-1]
    grad, far_x = lax.optimization_barrier((grad, far_x))
    far_t = turned(far_x)
    outward[0], far_t = lax.optimization_barrier((outward[0], far_t))

    arrived = []
    for block in outward:
        if arrived:
            block, arrived[-1] = lax.optimization_barrier((block, arrived[-1]))
        arrived.append(along(block, swap))
    unit2 = [shifted(u, -2) for u in unit]
    begin, terms, after = 0, [], []
    for block in arrived:
        kept, near, far = pair_product(begin, x_t, far_t, grad, block, after)
        near = along(near, [(1, 2), (2, 1), (0, 0), (3, 3)])
        far = along(far, [(1, 3), (2, 0), (0, 1), (3, 2)])
        after = [near, far]
        terms.append((begin, width, kept, near, far))
        begin += block.shape[1]
    twin0, twin2 = [across(u) for u in unit], [across(u) for u in unit2]
    text_grad, done = text_side(n_dp, text, scalars, *unit, *twin0, *twin2, *unit2)
    head = total(*terms[0], [])
    for term in terms[1:]:
        head = total(*term, [head, done])
    return head, text_grad


def plain_body(n_dp, n_fsdp, x, text, w, sharp, bias):
    def shifted(value, by):
        return lax.ppermute(value, "dp", [(d, (d + by) % n_dp) for d in range(n_dp)])

    rows, width = x.shape
    proj = jnp.dot(
        x, lax.all_gather(w, "fsdp", axis=0, tiled=True), preferred_element_type=F32
    )
    norm = jnp.sqrt(jnp.sum(proj * proj, axis=-1, keepdims=True) + EPS)
    direction = proj / norm
    unit = direction.astype(BF16)
    values = text.astype(F32)
    txt_norm = jnp.sqrt(jnp.sum(values * values, axis=-1, keepdims=True) + EPS)
    txt_dir = values / txt_norm
    slot = txt_dir.astype(BF16)
    scale = sharp[0]
    slope = jnp.zeros((rows, width), F32)
    txt_slope = jnp.zeros((rows, width), F32)
    for step in range(STEPS):
        if step > 0:
            slot = shifted(slot, 1)
        logits = scale * jnp.dot(unit, slot.T, preferred_element_type=F32) + bias[0]
        coefficient = jax.nn.sigmoid(logits)
        if step == 0:
            coefficient = coefficient - jnp.eye(rows, dtype=F32)
        coefficient = coefficient.astype(BF16)
        slope = slope + scale * jnp.dot(coefficient, slot, preferred_element_type=F32)
        share = scale * lax.dot_general(
            coefficient, unit, (((0,), (0,)), ((), ())), preferred_element_type=F32
        )
        if step > 0:
            share = shifted(share.astype(BF16), -step).astype(F32)
        txt_slope = txt_slope + share
    grad = (
        (slope - direction * jnp.sum(direction * slope, axis=-1, keepdims=True)) / norm
    ).astype(BF16)
    text_grad = (
        txt_slope - txt_dir * jnp.sum(txt_dir * txt_slope, axis=-1, keepdims=True)
    ) / txt_norm
    partial = lax.dot_general(
        x, grad, (((0,), (0,)), ((), ())), preferred_element_type=F32
    ).astype(BF16)
    head = lax.psum_scatter(partial, "fsdp", scatter_dimension=0, tiled=True).astype(F32)
    return head[None], text_grad


def solution(mesh):
    n_dp, n_fsdp = mesh.shape["dp"], mesh.shape["fsdp"]
    line = n_fsdp == 4 and n_dp % 4 == 0
    placed = (P(("dp", "fsdp"), None), P(("dp", "fsdp"), None), P("fsdp", None), P(), P())
    return jax.shard_map(
        functools.partial(line_body if line else plain_body, n_dp, n_fsdp),
        mesh=mesh,
        in_specs=placed,
        out_specs=(P("dp", "fsdp", None), P(("dp", "fsdp"), None)),
        check_vma=False,
    )
```

```python
import functools

import jax
import jax.numpy as jnp
from jax import lax
from jax.experimental import pallas as pl
from jax.experimental.pallas import tpu as pltpu
from jax.sharding import PartitionSpec as P

STEPS = 3
EPS = 1e-06
SHARES = (1, 2)
UNIT_PARTS = 4
TEXT_PARTS = 4
VMEM_BYTES = 24 * 1024 * 1024
BF16, F32 = jnp.bfloat16, jnp.float32


def spaces(count):
    return [pl.BlockSpec(memory_space=pltpu.VMEM)] * count


def params(size=VMEM_BYTES):
    return pltpu.CompilerParams(vmem_limit_bytes=size)


def cost():
    return pl.CostEstimate(flops=0, bytes_accessed=0, transcendentals=0)


IN_HBM = pl.BlockSpec(memory_space=pltpu.HBM)


def place(n_dp):
    where = lax.axis_index("dp")
    column = lax.rem(lax.div(where, 2), 2)
    return lax.axis_index("fsdp"), lax.rem(where, 2), lax.div(where, n_dp // 2), column


def cut_kernel(n_dp, short, own, whole, part, sem):
    _, core, _, column = place(n_dp)
    half = whole.shape[0]
    first = pltpu.make_async_copy(
        own.at[pl.ds(pl.multiple_of(core * half, 16), half), :], whole, sem.at[0]
    )
    start = pl.multiple_of(core * half + column * (half - short), 16)
    second = pltpu.make_async_copy(own.at[pl.ds(start, short), :], part, sem.at[1])
    first.start()
    second.start()
    first.wait()
    second.wait()


def cut(n_dp, short, own):
    half, width = own.shape[0] // 2, own.shape[1]
    outs = (
        jax.ShapeDtypeStruct((half, width), BF16),
        jax.ShapeDtypeStruct((short, width), BF16),
    )
    return pl.pallas_call(
        functools.partial(cut_kernel, n_dp, short),
        out_shape=outs,
        in_specs=[IN_HBM],
        out_specs=spaces(2),
        scratch_shapes=[pltpu.SemaphoreType.DMA((2,))],
        compiler_params=params(),
        cost_estimate=cost(),
        name="cut",
    )(own)


def prepare_kernel(n_dp, t0, twin0, t2, sharp, bias, *rest):
    twin2, (units, scalars) = rest[:TEXT_PARTS], rest[TEXT_PARTS:]
    rows = t0.shape[0]
    _, core, _, _ = place(n_dp)
    scalars[0:1, :] = jnp.broadcast_to(sharp[...], (1, scalars.shape[1]))
    scalars[1:2, :] = jnp.broadcast_to(bias[...], (1, scalars.shape[1]))

    def fill(start, block):
        values = block[...].astype(F32)
        inverse = 1.0 / jnp.sqrt(jnp.sum(values * values, axis=-1, keepdims=True) + EPS)
        units[start : start + block.shape[0], :] = (values * inverse).astype(BF16)

    fill(0, t0)
    fill(2 * rows, t2)

    @pl.when(core == 0)
    def _():
        for k, block in enumerate(twin2):
            fill(rows + k * block.shape[0], block)

    pl.when(core == 1)(lambda: fill(rows, twin0))


def prepare(n_dp, t0, twin0, t2, sharp, bias, twin2):
    rows, width = t0.shape
    return pl.pallas_call(
        functools.partial(prepare_kernel, n_dp),
        out_shape=(
            jax.ShapeDtypeStruct((STEPS * rows, width), BF16),
            jax.ShapeDtypeStruct((8, 128), F32),
        ),
        in_specs=spaces(5 + TEXT_PARTS),
        out_specs=tuple(spaces(2)),
        compiler_params=params(),
        cost_estimate=cost(),
        name="prepare",
    )(t0, twin0, t2, sharp, bias, *twin2)


def turn_kernel(x, x_t):
    x_t[...] = x[...].T


def turned(x):
    out = jax.ShapeDtypeStruct(x.shape[::-1], BF16)
    return pl.pallas_call(
        turn_kernel,
        out_shape=out,
        in_specs=spaces(1),
        out_specs=pl.BlockSpec(memory_space=pltpu.VMEM),
        compiler_params=params(),
        cost_estimate=cost(),
        name="turned",
    )(x)


def rows_of(ref, block, depth):
    return ref[pl.ds(pl.multiple_of(block * depth, 16), depth), :]


def weights(mine, others, scale, bias):
    product = lax.dot_general(
        mine, others, (((1,), (1,)), ((), ())), preferred_element_type=F32
    )
    coefficient = jax.nn.sigmoid(scale * product + bias)
    row = lax.broadcasted_iota(jnp.int32, coefficient.shape, 0)
    column = lax.broadcasted_iota(jnp.int32, coefficient.shape, 1)
    coefficient = jnp.where(row == column, coefficient - 1.0, coefficient).astype(BF16)
    return coefficient, scale * jnp.sum(coefficient.astype(F32) * product, axis=-1, keepdims=True)


def picture_kernel(n_dp, x, x_t, units, scalars, own, *rest):
    pieces, outs = rest[:8], rest[8 : 8 + len(SHARES)]
    unit_parts = rest[8 + len(SHARES) : -4]
    grad, unit, w, proj = rest[-4:]
    part, core, side, column = place(n_dp)
    depth = own.shape[0]
    half = depth // 2
    short = pieces[2].shape[0]
    rest_rows = half - short
    rows = x.shape[0]
    step = 1 - 2 * side
    w[pl.ds(pl.multiple_of(part * depth, 16), depth), :] = own[...]
    for twin in (0, 1):
        lane = core if twin == 0 else 1 - core
        straight, crossed, two, two_crossed = pieces[4 * twin : 4 * twin + 4]
        for piece, from_part in ((straight, part + 4 - step), (crossed, part + 4 + step)):
            start = pl.multiple_of(lax.rem(from_part, 4) * depth + lane * half, 16)
            w[pl.ds(start, half), :] = piece[...]
        base = lax.rem(part + 2, 4) * depth + lane * half
        start = pl.multiple_of(base + column * rest_rows, 16)
        w[pl.ds(start, short), :] = two[...]
        source = pl.multiple_of((1 - column) * (short - rest_rows), 16)
        start = pl.multiple_of(base + (1 - column) * short, 16)
        w[pl.ds(start, rest_rows), :] = two_crossed[pl.ds(source, rest_rows), :]

    proj[...] = jnp.dot(x[...], w[...], preferred_element_type=F32)
    values = proj[...]
    inverse = 1.0 / jnp.sqrt(jnp.sum(values * values, axis=-1, keepdims=True) + EPS)
    unit[...] = (values * inverse).astype(BF16)
    size = rows // UNIT_PARTS
    for k, out in enumerate(unit_parts):
        out[...] = unit[k * size : (k + 1) * size, :]
    scale = scalars[0:1, 0:1]
    coefficient, along = weights(unit[...], units[...], scale, scalars[1:2, 0:1])
    slope = jnp.dot(coefficient, units[...], preferred_element_type=F32)
    grad[...] = (slope * (scale * inverse) - proj[...] * (along * inverse * inverse)).astype(BF16)
    inner = jnp.logical_or(part == 1, part == 2)

    @pl.when(inner)
    def _():
        block = rows_of(x_t, 3 * (part - 1), depth)
        begin = 0
        for out in outs:
            stop = begin + out.shape[1]
            out[...] = jnp.dot(block, grad[:, begin:stop], preferred_element_type=F32).astype(BF16)
            begin = stop

    @pl.when(jnp.logical_not(inner))
    def _():
        begin = 0
        for out in outs:
            stop = begin + out.shape[1]
            out[:rows, :] = grad[:, begin:stop]
            out[rows:, :] = jnp.zeros((depth - rows, stop - begin), BF16)
            begin = stop


def picture_side(n_dp, x, x_t, units, scalars, own, pieces):
    rows, width = x.shape
    depth = own.shape[0]
    out = jax.ShapeDtypeStruct((rows, width), BF16)
    sizes = [width * share // sum(SHARES) for share in SHARES]
    outs = tuple(jax.ShapeDtypeStruct((depth, size), BF16) for size in sizes)
    part = jax.ShapeDtypeStruct((rows // UNIT_PARTS, width), BF16)
    outs = outs + (part,) * UNIT_PARTS + (out,)
    return pl.pallas_call(
        functools.partial(picture_kernel, n_dp),
        out_shape=outs,
        in_specs=spaces(13),
        out_specs=spaces(len(outs)),
        scratch_shapes=[
            pltpu.VMEM((rows, width), BF16),
            pltpu.VMEM((width, width), BF16),
            pltpu.VMEM((rows, width), F32),
        ],
        compiler_params=params(),
        cost_estimate=cost(),
        name="picture_side",
    )(x, x_t, units, scalars, own, *pieces)


def text_kernel(n_dp, text, scalars, *refs):
    blocks, (out, done, units) = refs[:-3], refs[-3:]
    rows = text.shape[0]
    _, core, _, _ = place(n_dp)
    done[...] = jnp.zeros_like(done)
    size = blocks[0].shape[0]
    for k in range(UNIT_PARTS):
        u0, twin0, twin2, u2 = blocks[k::UNIT_PARTS]
        for step, block in ((0, u0), (2, u2)):
            start = step * rows + k * size
            units[start : start + size, :] = block[...]
        for lane, block in ((0, twin0), (1, twin2)):

            @pl.when(core == lane)
            def _():
                units[rows + k * size : rows + (k + 1) * size, :] = block[...]

    values = text[...].astype(F32)
    inverse = 1.0 / jnp.sqrt(jnp.sum(values * values, axis=-1, keepdims=True) + EPS)
    scale = scalars[0:1, 0:1]
    coefficient, along = weights(
        (values * inverse).astype(BF16), units[...], scale, scalars[1:2, 0:1]
    )
    slope = jnp.dot(coefficient, units[...], preferred_element_type=F32)
    out[...] = slope * (scale * inverse) - values * (along * inverse * inverse)


def text_side(n_dp, text, scalars, *units):
    rows, width = text.shape
    return pl.pallas_call(
        functools.partial(text_kernel, n_dp),
        out_shape=(jax.ShapeDtypeStruct((rows, width), F32), jax.ShapeDtypeStruct((8, 128), F32)),
        in_specs=spaces(2 + 4 * UNIT_PARTS),
        out_specs=tuple(spaces(2)),
        scratch_shapes=[pltpu.VMEM((STEPS * rows, width), BF16)],
        compiler_params=params(),
        cost_estimate=cost(),
        name="text_side",
    )(text, scalars, *units)


def pair_kernel(begin, x_t, far_t, grad, arrived, *rest):
    kept, near, far = rest[-3:]
    rows = grad.shape[0]
    depth, size = arrived.shape
    part = lax.axis_index("fsdp")
    inner = jnp.logical_or(part == 1, part == 2)
    mine = grad[:, begin : begin + size]

    def product(block):
        return jnp.dot(rows_of(x_t, block, depth), mine, preferred_element_type=F32)

    @pl.when(inner)
    def _():
        other = arrived[:rows, :]
        for block, out in ((3 - part, near), (lax.rem(part + 2, 4), far), (part, kept)):
            both = product(block) + jnp.dot(
                rows_of(far_t, block, depth), other, preferred_element_type=F32
            )
            out[...] = both.astype(out.dtype)

    @pl.when(jnp.logical_not(inner))
    def _():
        kept[...] = product(part) + arrived[...].astype(F32)
        near[...] = jnp.zeros_like(near)
        far[...] = jnp.zeros_like(far)


def pair_product(begin, x_t, far_t, grad, arrived, after):
    outs = tuple(jax.ShapeDtypeStruct(arrived.shape, t) for t in (F32, BF16, BF16))
    return pl.pallas_call(
        functools.partial(pair_kernel, begin),
        out_shape=outs,
        in_specs=spaces(4 + len(after)),
        out_specs=spaces(3),
        compiler_params=params(),
        cost_estimate=cost(),
        name="pair_product",
    )(x_t, far_t, grad, arrived, *after)


def total_kernel(begin, kept, near, far, *rest):
    out, summed, sem = rest[-3:]
    summed[...] = kept[...] + near[...].astype(F32) + far[...].astype(F32)
    copy = pltpu.make_async_copy(summed, out.at[0, :, begin : begin + kept.shape[1]], sem)
    copy.start()
    copy.wait()


def total(begin, width, kept, near, far, held):
    depth = kept.shape[0]
    return pl.pallas_call(
        functools.partial(total_kernel, begin),
        out_shape=jax.ShapeDtypeStruct((1, depth, width), F32),
        in_specs=spaces(3) + [IN_HBM] * len(held[:1]) + spaces(len(held[1:])),
        out_specs=IN_HBM,
        scratch_shapes=[pltpu.VMEM(kept.shape, F32), pltpu.SemaphoreType.DMA],
        input_output_aliases={3: 0} if held else {},
        compiler_params=params(),
        cost_estimate=cost(),
        name="total",
    )(kept, near, far, *held)


def line_body(n_dp, n_fsdp, x, text, w, sharp, bias):
    depth, width = w.shape
    half = depth // 2
    short = (half // 2 + 15) // 16 * 16
    core = lax.rem(lax.axis_index("dp"), 2)
    side = n_dp // 2

    def along(value, pairs):
        return lax.ppermute(value, "fsdp", pairs)

    def across(value):
        return lax.ppermute(value, "dp", [(d, d ^ 1) for d in range(n_dp)])

    def over(value):
        return lax.ppermute(value, "dp", [(d, (d + side) % n_dp) for d in range(n_dp)])

    def shifted(value, by):
        return lax.ppermute(value, "dp", [(d, (d + by) % n_dp) for d in range(n_dp)])

    sharp, bias = sharp.reshape(1, 1), bias.reshape(1, 1)
    swap = [(0, 1), (1, 0), (2, 3), (3, 2)]
    whole, piece = cut(n_dp, short, w)
    whole, piece, text = lax.optimization_barrier((whole, piece, text))
    turns = [
        (d * n_fsdp + f, d * n_fsdp + (f + (1 if d < side else n_fsdp - 1)) % n_fsdp)
        for d in range(n_dp)
        for f in range(n_fsdp)
    ]
    straight = lax.ppermute(whole, ("dp", "fsdp"), turns)
    text2 = shifted(text, 2)
    piece, straight = lax.optimization_barrier((piece, straight))
    crossed = over(straight)
    two = along(piece, [(f, (f + 2) % n_fsdp) for f in range(n_fsdp)])
    two, x = lax.optimization_barrier((two, x))
    two_crossed = lax.ppermute(two, "dp", [(d, d ^ 2) for d in range(n_dp)])
    far_x = along(x, swap)
    x_t = turned(x)
    crossed, x_t, text2 = lax.optimization_barrier((crossed, x_t, text2))
    size = text.shape[0] // TEXT_PARTS
    twin2 = [across(text2[k * size : (k + 1) * size]) for k in range(TEXT_PARTS)]
    two_crossed, *twin2 = lax.optimization_barrier((two_crossed, *twin2))
    units, scalars = prepare(n_dp, text, across(text), text2, sharp, bias, twin2)
    two_crossed, units, scalars = lax.optimization_barrier((two_crossed, units, scalars))
    pieces = [straight, crossed, two, two_crossed]
    pieces = pieces + [across(piece) for piece in pieces]
    results = picture_side(n_dp, x, x_t, units, scalars, w, pieces)
    outward, unit, grad = list(results[: len(SHARES)]), results[len(SHARES) : -1], results[-1]
    grad, far_x = lax.optimization_barrier((grad, far_x))
    far_t = turned(far_x)
    outward[0], far_t = lax.optimization_barrier((outward[0], far_t))

    arrived = []
    for block in outward:
        if arrived:
            block, arrived[-1] = lax.optimization_barrier((block, arrived[-1]))
        arrived.append(along(block, swap))
    unit2 = [shifted(u, -2) for u in unit]
    begin, terms, after = 0, [], []
    for block in arrived:
        kept, near, far = pair_product(begin, x_t, far_t, grad, block, after)
        near = along(near, [(1, 2), (2, 1), (0, 0), (3, 3)])
        far = along(far, [(1, 3), (2, 0), (0, 1), (3, 2)])
        after = [near, far, *unit2]
        terms.append((begin, width, kept, near, far))
        begin += block.shape[1]
    twin0, twin2 = [across(u) for u in unit], [across(u) for u in unit2]
    text_grad, done = text_side(n_dp, text, scalars, *unit, *twin0, *twin2, *unit2)
    head = total(*terms[0], [])
    for term in terms[1:]:
        head = total(*term, [head, done])
    return head, text_grad


def plain_body(n_dp, n_fsdp, x, text, w, sharp, bias):
    def shifted(value, by):
        return lax.ppermute(value, "dp", [(d, (d + by) % n_dp) for d in range(n_dp)])

    rows, width = x.shape
    proj = jnp.dot(
        x, lax.all_gather(w, "fsdp", axis=0, tiled=True), preferred_element_type=F32
    )
    norm = jnp.sqrt(jnp.sum(proj * proj, axis=-1, keepdims=True) + EPS)
    direction = proj / norm
    unit = direction.astype(BF16)
    values = text.astype(F32)
    txt_norm = jnp.sqrt(jnp.sum(values * values, axis=-1, keepdims=True) + EPS)
    txt_dir = values / txt_norm
    slot = txt_dir.astype(BF16)
    scale = sharp[0]
    slope = jnp.zeros((rows, width), F32)
    txt_slope = jnp.zeros((rows, width), F32)
    for step in range(STEPS):
        if step > 0:
            slot = shifted(slot, 1)
        logits = scale * jnp.dot(unit, slot.T, preferred_element_type=F32) + bias[0]
        coefficient = jax.nn.sigmoid(logits)
        if step == 0:
            coefficient = coefficient - jnp.eye(rows, dtype=F32)
        coefficient = coefficient.astype(BF16)
        slope = slope + scale * jnp.dot(coefficient, slot, preferred_element_type=F32)
        share = scale * lax.dot_general(
            coefficient, unit, (((0,), (0,)), ((), ())), preferred_element_type=F32
        )
        if step > 0:
            share = shifted(share.astype(BF16), -step).astype(F32)
        txt_slope = txt_slope + share
    grad = (
        (slope - direction * jnp.sum(direction * slope, axis=-1, keepdims=True)) / norm
    ).astype(BF16)
    text_grad = (
        txt_slope - txt_dir * jnp.sum(txt_dir * txt_slope, axis=-1, keepdims=True)
    ) / txt_norm
    partial = lax.dot_general(
        x, grad, (((0,), (0,)), ((), ())), preferred_element_type=F32
    ).astype(BF16)
    head = lax.psum_scatter(partial, "fsdp", scatter_dimension=0, tiled=True).astype(F32)
    return head[None], text_grad


def solution(mesh):
    n_dp, n_fsdp = mesh.shape["dp"], mesh.shape["fsdp"]
    line = n_fsdp == 4 and n_dp % 4 == 0
    placed = (P(("dp", "fsdp"), None), P(("dp", "fsdp"), None), P("fsdp", None), P(), P())
    return jax.shard_map(
        functools.partial(line_body if line else plain_body, n_dp, n_fsdp),
        mesh=mesh,
        in_specs=placed,
        out_specs=(P("dp", "fsdp", None), P(("dp", "fsdp"), None)),
        check_vma=False,
    )
```

```python
import functools

import jax
import jax.numpy as jnp
from jax import lax
from jax.experimental import pallas as pl
from jax.experimental.pallas import tpu as pltpu
from jax.sharding import PartitionSpec as P

STEPS = 3
EPS = 1e-06
SHARES = (1, 2)
UNIT_PARTS = 1
TEXT_PARTS = 2
VMEM_BYTES = 24 * 1024 * 1024
BF16, F32 = jnp.bfloat16, jnp.float32


def spaces(count):
    return [pl.BlockSpec(memory_space=pltpu.VMEM)] * count


def params(size=VMEM_BYTES):
    return pltpu.CompilerParams(vmem_limit_bytes=size)


def cost():
    return pl.CostEstimate(flops=0, bytes_accessed=0, transcendentals=0)


IN_HBM = pl.BlockSpec(memory_space=pltpu.HBM)


def place():
    where = lax.axis_index("dp")
    return lax.axis_index("fsdp"), lax.rem(where, 2), lax.rem(lax.div(where, 2), 2)


def cut_kernel(short, own, whole, part, sem):
    _, core, column = place()
    half = whole.shape[0]
    first = pltpu.make_async_copy(
        own.at[pl.ds(pl.multiple_of(core * half, 16), half), :], whole, sem.at[0]
    )
    start = pl.multiple_of(core * half + column * (half - short), 16)
    second = pltpu.make_async_copy(own.at[pl.ds(start, short), :], part, sem.at[1])
    first.start()
    second.start()
    first.wait()
    second.wait()


def cut(short, own):
    half, width = own.shape[0] // 2, own.shape[1]
    outs = (
        jax.ShapeDtypeStruct((half, width), BF16),
        jax.ShapeDtypeStruct((short, width), BF16),
    )
    return pl.pallas_call(
        functools.partial(cut_kernel, short),
        out_shape=outs,
        in_specs=[IN_HBM],
        out_specs=spaces(2),
        scratch_shapes=[pltpu.SemaphoreType.DMA((2,))],
        compiler_params=params(),
        cost_estimate=cost(),
        name="cut",
    )(own)


def prepare_kernel(t0, twin0, t2, sharp, bias, *rest):
    twin2, (units, scalars) = rest[:TEXT_PARTS], rest[TEXT_PARTS:]
    rows = t0.shape[0]
    _, core, _ = place()
    scalars[0:1, :] = jnp.broadcast_to(sharp[...], (1, scalars.shape[1]))
    scalars[1:2, :] = jnp.broadcast_to(bias[...], (1, scalars.shape[1]))

    def fill(start, block):
        values = block[...].astype(F32)
        inverse = 1.0 / jnp.sqrt(jnp.sum(values * values, axis=-1, keepdims=True) + EPS)
        units[start : start + block.shape[0], :] = (values * inverse).astype(BF16)

    fill(0, t0)
    fill(2 * rows, t2)

    @pl.when(core == 0)
    def _():
        for k, block in enumerate(twin2):
            fill(rows + k * block.shape[0], block)

    pl.when(core == 1)(lambda: fill(rows, twin0))


def prepare(t0, twin0, t2, sharp, bias, twin2):
    rows, width = t0.shape
    return pl.pallas_call(
        prepare_kernel,
        out_shape=(
            jax.ShapeDtypeStruct((STEPS * rows, width), BF16),
            jax.ShapeDtypeStruct((8, 128), F32),
        ),
        in_specs=spaces(5 + TEXT_PARTS),
        out_specs=tuple(spaces(2)),
        compiler_params=params(),
        cost_estimate=cost(),
        name="prepare",
    )(t0, twin0, t2, sharp, bias, *twin2)


def turn_kernel(depth, x, x_t, outer_t):
    x_t[...] = x[...].T
    start = jnp.where(lax.axis_index("fsdp") == 0, depth, 0)
    outer_t[...] = x_t[pl.ds(pl.multiple_of(start, 16), outer_t.shape[0]), :]


def turned(depth, x):
    rows, width = x.shape
    return pl.pallas_call(
        functools.partial(turn_kernel, depth),
        out_shape=(
            jax.ShapeDtypeStruct((width, rows), BF16),
            jax.ShapeDtypeStruct((width - depth, rows), BF16),
        ),
        in_specs=spaces(1),
        out_specs=tuple(spaces(2)),
        compiler_params=params(),
        cost_estimate=cost(),
        name="turned",
    )(x)


def rows_of(ref, block, depth):
    return ref[pl.ds(pl.multiple_of(block * depth, 16), depth), :]


def weights(mine, others, scale, bias):
    product = lax.dot_general(
        mine, others, (((1,), (1,)), ((), ())), preferred_element_type=F32
    )
    coefficient = jax.nn.sigmoid(scale * product + bias)
    row = lax.broadcasted_iota(jnp.int32, coefficient.shape, 0)
    column = lax.broadcasted_iota(jnp.int32, coefficient.shape, 1)
    coefficient = jnp.where(row == column, coefficient - 1.0, coefficient).astype(BF16)
    return coefficient, scale * jnp.sum(coefficient.astype(F32) * product, axis=-1, keepdims=True)


def picture_kernel(x, x_t, units, scalars, own, *rest):
    pieces, outs = rest[:8], rest[8 : 8 + len(SHARES)]
    unit_parts = rest[8 + len(SHARES) : -4]
    grad, unit, w, proj = rest[-4:]
    part, core, column = place()
    depth = own.shape[0]
    half = depth // 2
    short = pieces[2].shape[0]
    rest_rows = half - short
    rows = x.shape[0]
    w[pl.ds(pl.multiple_of(part * depth, 16), depth), :] = own[...]
    for twin in (0, 1):
        lane = core if twin == 0 else 1 - core
        plus, minus, two, two_crossed = pieces[4 * twin : 4 * twin + 4]
        for piece, from_part in ((plus, part + 3), (minus, part + 1)):
            start = pl.multiple_of(lax.rem(from_part, 4) * depth + lane * half, 16)
            w[pl.ds(start, half), :] = piece[...]
        base = lax.rem(part + 2, 4) * depth + lane * half
        start = pl.multiple_of(base + column * rest_rows, 16)
        w[pl.ds(start, short), :] = two[...]
        source = pl.multiple_of((1 - column) * (short - rest_rows), 16)
        start = pl.multiple_of(base + (1 - column) * short, 16)
        w[pl.ds(start, rest_rows), :] = two_crossed[pl.ds(source, rest_rows), :]

    proj[...] = jnp.dot(x[...], w[...], preferred_element_type=F32)
    values = proj[...]
    inverse = 1.0 / jnp.sqrt(jnp.sum(values * values, axis=-1, keepdims=True) + EPS)
    unit[...] = (values * inverse).astype(BF16)
    size = rows // UNIT_PARTS
    for k, out in enumerate(unit_parts):
        out[...] = unit[k * size : (k + 1) * size, :]
    scale = scalars[0:1, 0:1]
    coefficient, along = weights(unit[...], units[...], scale, scalars[1:2, 0:1])
    slope = jnp.dot(coefficient, units[...], preferred_element_type=F32)
    grad[...] = (slope * (scale * inverse) - proj[...] * (along * inverse * inverse)).astype(BF16)
    inner = jnp.logical_or(part == 1, part == 2)

    @pl.when(inner)
    def _():
        block = rows_of(x_t, 3 * (part - 1), depth)
        begin = 0
        for out in outs:
            stop = begin + out.shape[1]
            out[...] = jnp.dot(block, grad[:, begin:stop], preferred_element_type=F32).astype(BF16)
            begin = stop

    @pl.when(jnp.logical_not(inner))
    def _():
        begin = 0
        for out in outs:
            stop = begin + out.shape[1]
            out[:rows, :] = grad[:, begin:stop]
            out[rows:, :] = jnp.zeros((depth - rows, stop - begin), BF16)
            begin = stop


def picture_side(x, x_t, units, scalars, own, pieces):
    rows, width = x.shape
    depth = own.shape[0]
    out = jax.ShapeDtypeStruct((rows, width), BF16)
    sizes = [width * share // sum(SHARES) for share in SHARES]
    outs = tuple(jax.ShapeDtypeStruct((depth, size), BF16) for size in sizes)
    part = jax.ShapeDtypeStruct((rows // UNIT_PARTS, width), BF16)
    outs = outs + (part,) * UNIT_PARTS + (out,)
    return pl.pallas_call(
        picture_kernel,
        out_shape=outs,
        in_specs=spaces(13),
        out_specs=spaces(len(outs)),
        scratch_shapes=[
            pltpu.VMEM((rows, width), BF16),
            pltpu.VMEM((width, width), BF16),
            pltpu.VMEM((rows, width), F32),
        ],
        compiler_params=params(),
        cost_estimate=cost(),
        name="picture_side",
    )(x, x_t, units, scalars, own, *pieces)


def text_kernel(text, scalars, *refs):
    blocks, (out, done, units) = refs[:-3], refs[-3:]
    rows = text.shape[0]
    _, core, _ = place()
    done[...] = jnp.zeros_like(done)
    size = blocks[0].shape[0]
    for k in range(UNIT_PARTS):
        u0, twin0, twin2, u2 = blocks[k::UNIT_PARTS]
        for step, block in ((0, u0), (2, u2)):
            start = step * rows + k * size
            units[start : start + size, :] = block[...]
        for lane, block in ((0, twin0), (1, twin2)):

            @pl.when(core == lane)
            def _():
                units[rows + k * size : rows + (k + 1) * size, :] = block[...]

    values = text[...].astype(F32)
    inverse = 1.0 / jnp.sqrt(jnp.sum(values * values, axis=-1, keepdims=True) + EPS)
    scale = scalars[0:1, 0:1]
    coefficient, along = weights(
        (values * inverse).astype(BF16), units[...], scale, scalars[1:2, 0:1]
    )
    slope = jnp.dot(coefficient, units[...], preferred_element_type=F32)
    out[...] = slope * (scale * inverse) - values * (along * inverse * inverse)


def text_side(text, scalars, *units):
    rows, width = text.shape
    return pl.pallas_call(
        text_kernel,
        out_shape=(jax.ShapeDtypeStruct((rows, width), F32), jax.ShapeDtypeStruct((8, 128), F32)),
        in_specs=spaces(2 + 4 * UNIT_PARTS),
        out_specs=tuple(spaces(2)),
        scratch_shapes=[pltpu.VMEM((STEPS * rows, width), BF16)],
        compiler_params=params(),
        cost_estimate=cost(),
        name="text_side",
    )(text, scalars, *units)


def pair_kernel(begin, x_t, far_t, grad, arrived, *rest):
    kept, near, far = rest[-3:]
    rows = grad.shape[0]
    depth, size = arrived.shape
    part = lax.axis_index("fsdp")
    inner = jnp.logical_or(part == 1, part == 2)
    mine = grad[:, begin : begin + size]

    def product(block):
        return jnp.dot(rows_of(x_t, block, depth), mine, preferred_element_type=F32)

    @pl.when(inner)
    def _():
        other = arrived[:rows, :]
        first = jnp.where(part == 1, 1, 0)
        for block, out in ((3 - part, near), (lax.rem(part + 2, 4), far), (part, kept)):
            both = product(block) + jnp.dot(
                rows_of(far_t, block - first, depth), other, preferred_element_type=F32
            )
            out[...] = both.astype(out.dtype)

    @pl.when(jnp.logical_not(inner))
    def _():
        kept[...] = product(part) + arrived[...].astype(F32)
        near[...] = jnp.zeros_like(near)
        far[...] = jnp.zeros_like(far)


def pair_product(begin, x_t, far_t, grad, arrived, after):
    outs = tuple(jax.ShapeDtypeStruct(arrived.shape, t) for t in (F32, BF16, BF16))
    return pl.pallas_call(
        functools.partial(pair_kernel, begin),
        out_shape=outs,
        in_specs=spaces(4 + len(after)),
        out_specs=spaces(3),
        compiler_params=params(),
        cost_estimate=cost(),
        name="pair_product",
    )(x_t, far_t, grad, arrived, *after)


def total_kernel(begin, kept, near, far, *rest):
    out, summed, sem = rest[-3:]
    summed[...] = kept[...] + near[...].astype(F32) + far[...].astype(F32)
    copy = pltpu.make_async_copy(summed, out.at[0, :, begin : begin + kept.shape[1]], sem)
    copy.start()
    copy.wait()


def total(begin, width, kept, near, far, held):
    depth = kept.shape[0]
    return pl.pallas_call(
        functools.partial(total_kernel, begin),
        out_shape=jax.ShapeDtypeStruct((1, depth, width), F32),
        in_specs=spaces(3) + [IN_HBM] * len(held[:1]) + spaces(len(held[1:])),
        out_specs=IN_HBM,
        scratch_shapes=[pltpu.VMEM(kept.shape, F32), pltpu.SemaphoreType.DMA],
        input_output_aliases={3: 0} if held else {},
        compiler_params=params(),
        cost_estimate=cost(),
        name="total",
    )(kept, near, far, *held)


def line_body(n_dp, n_fsdp, x, text, w, sharp, bias):
    depth, width = w.shape
    half = depth // 2
    short = (half // 2 + 15) // 16 * 16

    def along(value, pairs):
        return lax.ppermute(value, "fsdp", pairs)

    def across(value):
        return lax.ppermute(value, "dp", [(d, d ^ 1) for d in range(n_dp)])

    def shifted(value, by):
        return lax.ppermute(value, "dp", [(d, (d + by) % n_dp) for d in range(n_dp)])

    sharp, bias = sharp.reshape(1, 1), bias.reshape(1, 1)
    swap = [(0, 1), (1, 0), (2, 3), (3, 2)]
    whole, piece = cut(short, w)
    whole, piece, text = lax.optimization_barrier((whole, piece, text))
    two = along(piece, [(f, (f + 2) % n_fsdp) for f in range(n_fsdp)])
    plus = along(whole, [(f, (f + 1) % n_fsdp) for f in range(n_fsdp)])
    minus = along(whole, [(f, (f - 1) % n_fsdp) for f in range(n_fsdp)])
    text2 = shifted(text, 2)
    x_t, outer_t = turned(depth, x)
    two, outer_t, text2 = lax.optimization_barrier((two, outer_t, text2))
    two_crossed = lax.ppermute(two, "dp", [(d, d ^ 2) for d in range(n_dp)])
    far_t = along(outer_t, swap)
    size = text.shape[0] // TEXT_PARTS
    twin2 = [across(text2[k * size : (k + 1) * size]) for k in range(TEXT_PARTS)]
    plus, *twin2 = lax.optimization_barrier((plus, *twin2))
    units, scalars = prepare(text, across(text), text2, sharp, bias, twin2)
    pieces = [plus, minus, two, two_crossed]
    *pieces, units, scalars, x_t = lax.optimization_barrier((*pieces, units, scalars, x_t))
    pieces = pieces + [across(piece) for piece in pieces]
    results = picture_side(x, x_t, units, scalars, w, pieces)
    outward, unit, grad = list(results[: len(SHARES)]), results[len(SHARES) : -1], results[-1]
    grad, far_t = lax.optimization_barrier((grad, far_t))
    outward[0], far_t = lax.optimization_barrier((outward[0], far_t))

    arrived = []
    for block in outward:
        if arrived:
            block, arrived[-1] = lax.optimization_barrier((block, arrived[-1]))
        arrived.append(along(block, swap))
    unit2 = [shifted(u, -2) for u in unit]
    begin, terms, after = 0, [], []
    for block in arrived:
        kept, near, far = pair_product(begin, x_t, far_t, grad, block, after)
        near = along(near, [(1, 2), (2, 1), (0, 0), (3, 3)])
        far = along(far, [(1, 3), (2, 0), (0, 1), (3, 2)])
        after = [near, far, *unit2]
        terms.append((begin, width, kept, near, far))
        begin += block.shape[1]
    twin0, twin2 = [across(u) for u in unit], [across(u) for u in unit2]
    text_grad, done = text_side(text, scalars, *unit, *twin0, *twin2, *unit2)
    head = total(*terms[0], [])
    for term in terms[1:]:
        head = total(*term, [head, done])
    return head, text_grad


def plain_body(n_dp, n_fsdp, x, text, w, sharp, bias):
    def shifted(value, by):
        return lax.ppermute(value, "dp", [(d, (d + by) % n_dp) for d in range(n_dp)])

    rows, width = x.shape
    proj = jnp.dot(
        x, lax.all_gather(w, "fsdp", axis=0, tiled=True), preferred_element_type=F32
    )
    norm = jnp.sqrt(jnp.sum(proj * proj, axis=-1, keepdims=True) + EPS)
    direction = proj / norm
    unit = direction.astype(BF16)
    values = text.astype(F32)
    txt_norm = jnp.sqrt(jnp.sum(values * values, axis=-1, keepdims=True) + EPS)
    txt_dir = values / txt_norm
    slot = txt_dir.astype(BF16)
    scale = sharp[0]
    slope = jnp.zeros((rows, width), F32)
    txt_slope = jnp.zeros((rows, width), F32)
    for step in range(STEPS):
        if step > 0:
            slot = shifted(slot, 1)
        logits = scale * jnp.dot(unit, slot.T, preferred_element_type=F32) + bias[0]
        coefficient = jax.nn.sigmoid(logits)
        if step == 0:
            coefficient = coefficient - jnp.eye(rows, dtype=F32)
        coefficient = coefficient.astype(BF16)
        slope = slope + scale * jnp.dot(coefficient, slot, preferred_element_type=F32)
        share = scale * lax.dot_general(
            coefficient, unit, (((0,), (0,)), ((), ())), preferred_element_type=F32
        )
        if step > 0:
            share = shifted(share.astype(BF16), -step).astype(F32)
        txt_slope = txt_slope + share
    grad = (
        (slope - direction * jnp.sum(direction * slope, axis=-1, keepdims=True)) / norm
    ).astype(BF16)
    text_grad = (
        txt_slope - txt_dir * jnp.sum(txt_dir * txt_slope, axis=-1, keepdims=True)
    ) / txt_norm
    partial = lax.dot_general(
        x, grad, (((0,), (0,)), ((), ())), preferred_element_type=F32
    ).astype(BF16)
    head = lax.psum_scatter(partial, "fsdp", scatter_dimension=0, tiled=True).astype(F32)
    return head[None], text_grad


def solution(mesh):
    n_dp, n_fsdp = mesh.shape["dp"], mesh.shape["fsdp"]
    line = n_fsdp == 4 and n_dp % 4 == 0
    placed = (P(("dp", "fsdp"), None), P(("dp", "fsdp"), None), P("fsdp", None), P(), P())
    return jax.shard_map(
        functools.partial(line_body if line else plain_body, n_dp, n_fsdp),
        mesh=mesh,
        in_specs=placed,
        out_specs=(P("dp", "fsdp", None), P(("dp", "fsdp"), None)),
        check_vma=False,
    )
```

```python
import functools

import jax
import jax.numpy as jnp
from jax import lax
from jax.experimental import pallas as pl
from jax.experimental.pallas import tpu as pltpu
from jax.sharding import PartitionSpec as P

STEPS = 3
EPS = 1e-06
SHARES = (1, 2)
UNIT_PARTS = 1
TEXT_PARTS = 2
VMEM_BYTES = 24 * 1024 * 1024
BF16, F32 = jnp.bfloat16, jnp.float32


def spaces(count):
    return [pl.BlockSpec(memory_space=pltpu.VMEM)] * count


def params(size=VMEM_BYTES):
    return pltpu.CompilerParams(vmem_limit_bytes=size)


def cost():
    return pl.CostEstimate(flops=0, bytes_accessed=0, transcendentals=0)


IN_HBM = pl.BlockSpec(memory_space=pltpu.HBM)


def place():
    where = lax.axis_index("dp")
    return lax.axis_index("fsdp"), lax.rem(where, 2), lax.rem(lax.div(where, 2), 2)


def cut_kernel(short, own, whole, part, sem):
    _, core, column = place()
    half = whole.shape[0]
    first = pltpu.make_async_copy(
        own.at[pl.ds(pl.multiple_of(core * half, 16), half), :], whole, sem.at[0]
    )
    start = pl.multiple_of(core * half + column * (half - short), 16)
    second = pltpu.make_async_copy(own.at[pl.ds(start, short), :], part, sem.at[1])
    first.start()
    second.start()
    first.wait()
    second.wait()


def cut(short, own):
    half, width = own.shape[0] // 2, own.shape[1]
    outs = (
        jax.ShapeDtypeStruct((half, width), BF16),
        jax.ShapeDtypeStruct((short, width), BF16),
    )
    return pl.pallas_call(
        functools.partial(cut_kernel, short),
        out_shape=outs,
        in_specs=[IN_HBM],
        out_specs=spaces(2),
        scratch_shapes=[pltpu.SemaphoreType.DMA((2,))],
        compiler_params=params(),
        cost_estimate=cost(),
        name="cut",
    )(own)


def prepare_kernel(t0, twin0, t2, sharp, bias, *rest):
    twin2, (units, scalars) = rest[:TEXT_PARTS], rest[TEXT_PARTS:]
    rows = t0.shape[0]
    _, core, _ = place()
    scalars[0:1, :] = jnp.broadcast_to(sharp[...], (1, scalars.shape[1]))
    scalars[1:2, :] = jnp.broadcast_to(bias[...], (1, scalars.shape[1]))

    def fill(start, block):
        values = block[...].astype(F32)
        inverse = 1.0 / jnp.sqrt(jnp.sum(values * values, axis=-1, keepdims=True) + EPS)
        units[start : start + block.shape[0], :] = (values * inverse).astype(BF16)

    fill(0, t0)
    fill(2 * rows, t2)

    @pl.when(core == 0)
    def _():
        for k, block in enumerate(twin2):
            fill(rows + k * block.shape[0], block)

    pl.when(core == 1)(lambda: fill(rows, twin0))


def prepare(t0, twin0, t2, sharp, bias, twin2):
    rows, width = t0.shape
    return pl.pallas_call(
        prepare_kernel,
        out_shape=(
            jax.ShapeDtypeStruct((STEPS * rows, width), BF16),
            jax.ShapeDtypeStruct((8, 128), F32),
        ),
        in_specs=spaces(5 + TEXT_PARTS),
        out_specs=tuple(spaces(2)),
        compiler_params=params(),
        cost_estimate=cost(),
        name="prepare",
    )(t0, twin0, t2, sharp, bias, *twin2)


def turn_kernel(depth, x, x_t, outer_t):
    x_t[...] = x[...].T
    start = jnp.where(lax.axis_index("fsdp") == 0, depth, 0)
    outer_t[...] = x_t[pl.ds(pl.multiple_of(start, 16), outer_t.shape[0]), :]


def turned(depth, x):
    rows, width = x.shape
    return pl.pallas_call(
        functools.partial(turn_kernel, depth),
        out_shape=(
            jax.ShapeDtypeStruct((width, rows), BF16),
            jax.ShapeDtypeStruct((width - depth, rows), BF16),
        ),
        in_specs=spaces(1),
        out_specs=tuple(spaces(2)),
        compiler_params=params(),
        cost_estimate=cost(),
        name="turned",
    )(x)


def rows_of(ref, block, depth):
    return ref[pl.ds(pl.multiple_of(block * depth, 16), depth), :]


def weights(mine, others, scale, bias):
    product = lax.dot_general(
        mine, others, (((1,), (1,)), ((), ())), preferred_element_type=F32
    )
    coefficient = jax.nn.sigmoid(scale * product + bias)
    row = lax.broadcasted_iota(jnp.int32, coefficient.shape, 0)
    column = lax.broadcasted_iota(jnp.int32, coefficient.shape, 1)
    coefficient = jnp.where(row == column, coefficient - 1.0, coefficient).astype(BF16)
    return coefficient, scale * jnp.sum(coefficient.astype(F32) * product, axis=-1, keepdims=True)


def picture_kernel(x, x_t, units, scalars, own, *rest):
    pieces, outs = rest[:8], rest[8 : 8 + len(SHARES)]
    unit_parts = rest[8 + len(SHARES) : -4]
    grad, unit, w, proj = rest[-4:]
    part, core, column = place()
    depth = own.shape[0]
    half = depth // 2
    short = pieces[2].shape[0]
    rest_rows = half - short
    rows = x.shape[0]
    w[pl.ds(pl.multiple_of(part * depth, 16), depth), :] = own[...]
    for twin in (0, 1):
        lane = core if twin == 0 else 1 - core
        plus, minus, two, two_crossed = pieces[4 * twin : 4 * twin + 4]
        for piece, from_part in ((plus, part + 3), (minus, part + 1)):
            start = pl.multiple_of(lax.rem(from_part, 4) * depth + lane * half, 16)
            w[pl.ds(start, half), :] = piece[...]
        base = lax.rem(part + 2, 4) * depth + lane * half
        start = pl.multiple_of(base + column * rest_rows, 16)
        w[pl.ds(start, short), :] = two[...]
        source = pl.multiple_of((1 - column) * (short - rest_rows), 16)
        start = pl.multiple_of(base + (1 - column) * short, 16)
        w[pl.ds(start, rest_rows), :] = two_crossed[pl.ds(source, rest_rows), :]

    proj[...] = jnp.dot(x[...], w[...], preferred_element_type=F32)
    values = proj[...]
    inverse = 1.0 / jnp.sqrt(jnp.sum(values * values, axis=-1, keepdims=True) + EPS)
    unit[...] = (values * inverse).astype(BF16)
    size = rows // UNIT_PARTS
    for k, out in enumerate(unit_parts):
        out[...] = unit[k * size : (k + 1) * size, :]
    scale = scalars[0:1, 0:1]
    coefficient, along = weights(unit[...], units[...], scale, scalars[1:2, 0:1])
    slope = jnp.dot(coefficient, units[...], preferred_element_type=F32)
    grad[...] = (slope * (scale * inverse) - proj[...] * (along * inverse * inverse)).astype(BF16)
    inner = jnp.logical_or(part == 1, part == 2)

    @pl.when(inner)
    def _():
        block = rows_of(x_t, 3 * (part - 1), depth)
        begin = 0
        for out in outs:
            stop = begin + out.shape[1]
            out[...] = jnp.dot(block, grad[:, begin:stop], preferred_element_type=F32).astype(BF16)
            begin = stop

    @pl.when(jnp.logical_not(inner))
    def _():
        begin = 0
        for out in outs:
            stop = begin + out.shape[1]
            out[:rows, :] = grad[:, begin:stop]
            out[rows:, :] = jnp.zeros((depth - rows, stop - begin), BF16)
            begin = stop


def picture_side(x, x_t, units, scalars, own, pieces):
    rows, width = x.shape
    depth = own.shape[0]
    out = jax.ShapeDtypeStruct((rows, width), BF16)
    sizes = [width * share // sum(SHARES) for share in SHARES]
    outs = tuple(jax.ShapeDtypeStruct((depth, size), BF16) for size in sizes)
    part = jax.ShapeDtypeStruct((rows // UNIT_PARTS, width), BF16)
    outs = outs + (part,) * UNIT_PARTS + (out,)
    return pl.pallas_call(
        picture_kernel,
        out_shape=outs,
        in_specs=spaces(13),
        out_specs=spaces(len(outs)),
        scratch_shapes=[
            pltpu.VMEM((rows, width), BF16),
            pltpu.VMEM((width, width), BF16),
            pltpu.VMEM((rows, width), F32),
        ],
        compiler_params=params(),
        cost_estimate=cost(),
        name="picture_side",
    )(x, x_t, units, scalars, own, *pieces)


def text_kernel(text, scalars, *refs):
    blocks, (out, done, units) = refs[:-3], refs[-3:]
    rows = text.shape[0]
    _, core, _ = place()
    done[...] = jnp.zeros_like(done)
    size = blocks[0].shape[0]
    for k in range(UNIT_PARTS):
        u0, twin0, twin2, u2 = blocks[k::UNIT_PARTS]
        for step, block in ((0, u0), (2, u2)):
            start = step * rows + k * size
            units[start : start + size, :] = block[...]
        for lane, block in ((0, twin0), (1, twin2)):

            @pl.when(core == lane)
            def _():
                units[rows + k * size : rows + (k + 1) * size, :] = block[...]

    values = text[...].astype(F32)
    inverse = 1.0 / jnp.sqrt(jnp.sum(values * values, axis=-1, keepdims=True) + EPS)
    scale = scalars[0:1, 0:1]
    coefficient, along = weights(
        (values * inverse).astype(BF16), units[...], scale, scalars[1:2, 0:1]
    )
    slope = jnp.dot(coefficient, units[...], preferred_element_type=F32)
    out[...] = slope * (scale * inverse) - values * (along * inverse * inverse)


def text_side(text, scalars, *units):
    rows, width = text.shape
    return pl.pallas_call(
        text_kernel,
        out_shape=(jax.ShapeDtypeStruct((rows, width), F32), jax.ShapeDtypeStruct((8, 128), F32)),
        in_specs=spaces(2 + 4 * UNIT_PARTS),
        out_specs=tuple(spaces(2)),
        scratch_shapes=[pltpu.VMEM((STEPS * rows, width), BF16)],
        compiler_params=params(),
        cost_estimate=cost(),
        name="text_side",
    )(text, scalars, *units)


def pair_kernel(begin, x_t, far_t, grad, arrived, *rest):
    kept, near, far = rest[-3:]
    rows = grad.shape[0]
    depth, size = arrived.shape
    part = lax.axis_index("fsdp")
    inner = jnp.logical_or(part == 1, part == 2)
    mine = grad[:, begin : begin + size]

    def product(block):
        return jnp.dot(rows_of(x_t, block, depth), mine, preferred_element_type=F32)

    @pl.when(inner)
    def _():
        other = arrived[:rows, :]
        first = jnp.where(part == 1, 1, 0)
        for block, out in ((3 - part, near), (lax.rem(part + 2, 4), far), (part, kept)):
            both = product(block) + jnp.dot(
                rows_of(far_t, block - first, depth), other, preferred_element_type=F32
            )
            out[...] = both.astype(out.dtype)

    @pl.when(jnp.logical_not(inner))
    def _():
        kept[...] = product(part) + arrived[...].astype(F32)
        near[...] = jnp.zeros_like(near)
        far[...] = jnp.zeros_like(far)


def pair_product(begin, x_t, far_t, grad, arrived, after):
    outs = tuple(jax.ShapeDtypeStruct(arrived.shape, t) for t in (F32, BF16, BF16))
    return pl.pallas_call(
        functools.partial(pair_kernel, begin),
        out_shape=outs,
        in_specs=spaces(4 + len(after)),
        out_specs=spaces(3),
        compiler_params=params(),
        cost_estimate=cost(),
        name="pair_product",
    )(x_t, far_t, grad, arrived, *after)


def total_kernel(begin, kept, near, far, *rest):
    out, summed, sem = rest[-3:]
    summed[...] = kept[...] + near[...].astype(F32) + far[...].astype(F32)
    copy = pltpu.make_async_copy(summed, out.at[0, :, begin : begin + kept.shape[1]], sem)
    copy.start()
    copy.wait()


def total(begin, width, kept, near, far, held):
    depth = kept.shape[0]
    return pl.pallas_call(
        functools.partial(total_kernel, begin),
        out_shape=jax.ShapeDtypeStruct((1, depth, width), F32),
        in_specs=spaces(3) + [IN_HBM] * len(held[:1]) + spaces(len(held[1:])),
        out_specs=IN_HBM,
        scratch_shapes=[pltpu.VMEM(kept.shape, F32), pltpu.SemaphoreType.DMA],
        input_output_aliases={3: 0} if held else {},
        compiler_params=params(),
        cost_estimate=cost(),
        name="total",
    )(kept, near, far, *held)


def line_body(n_dp, n_fsdp, x, text, w, sharp, bias):
    depth, width = w.shape
    half = depth // 2
    short = (half // 2 + 15) // 16 * 16

    def along(value, pairs):
        return lax.ppermute(value, "fsdp", pairs)

    def across(value):
        return lax.ppermute(value, "dp", [(d, d ^ 1) for d in range(n_dp)])

    def shifted(value, by):
        return lax.ppermute(value, "dp", [(d, (d + by) % n_dp) for d in range(n_dp)])

    sharp, bias = sharp.reshape(1, 1), bias.reshape(1, 1)
    swap = [(0, 1), (1, 0), (2, 3), (3, 2)]
    whole, piece = cut(short, w)
    whole, piece, text = lax.optimization_barrier((whole, piece, text))
    two = along(piece, [(f, (f + 2) % n_fsdp) for f in range(n_fsdp)])
    plus = along(whole, [(f, (f + 1) % n_fsdp) for f in range(n_fsdp)])
    minus = along(whole, [(f, (f - 1) % n_fsdp) for f in range(n_fsdp)])
    text2 = shifted(text, 2)
    x_t, outer_t = turned(depth, x)
    two, outer_t, text2 = lax.optimization_barrier((two, outer_t, text2))
    two_crossed = lax.ppermute(two, "dp", [(d, d ^ 2) for d in range(n_dp)])
    far_t = along(outer_t, swap)
    size = text.shape[0] // TEXT_PARTS
    twin2 = [across(text2[k * size : (k + 1) * size]) for k in range(TEXT_PARTS)]
    units, scalars = prepare(text, across(text), text2, sharp, bias, twin2)
    plus, minus, units, scalars, x_t = lax.optimization_barrier((plus, minus, units, scalars, x_t))
    pieces = [plus, minus, two, two_crossed]
    pieces = pieces + [across(piece) for piece in pieces]
    results = picture_side(x, x_t, units, scalars, w, pieces)
    outward, unit, grad = list(results[: len(SHARES)]), results[len(SHARES) : -1], results[-1]
    grad, far_t = lax.optimization_barrier((grad, far_t))
    outward[0], far_t = lax.optimization_barrier((outward[0], far_t))

    arrived = []
    for block in outward:
        if arrived:
            block, arrived[-1] = lax.optimization_barrier((block, arrived[-1]))
        arrived.append(along(block, swap))
    unit2 = [shifted(u, -2) for u in unit]
    begin, terms, after = 0, [], []
    for block in arrived:
        kept, near, far = pair_product(begin, x_t, far_t, grad, block, after)
        near = along(near, [(1, 2), (2, 1), (0, 0), (3, 3)])
        far = along(far, [(1, 3), (2, 0), (0, 1), (3, 2)])
        after = [near, far, *unit2]
        terms.append((begin, width, kept, near, far))
        begin += block.shape[1]
    twin0, twin2 = [across(u) for u in unit], [across(u) for u in unit2]
    text_grad, done = text_side(text, scalars, *unit, *twin0, *twin2, *unit2)
    head = total(*terms[0], [])
    for term in terms[1:]:
        head = total(*term, [head, done])
    return head, text_grad


def plain_body(n_dp, n_fsdp, x, text, w, sharp, bias):
    def shifted(value, by):
        return lax.ppermute(value, "dp", [(d, (d + by) % n_dp) for d in range(n_dp)])

    rows, width = x.shape
    proj = jnp.dot(
        x, lax.all_gather(w, "fsdp", axis=0, tiled=True), preferred_element_type=F32
    )
    norm = jnp.sqrt(jnp.sum(proj * proj, axis=-1, keepdims=True) + EPS)
    direction = proj / norm
    unit = direction.astype(BF16)
    values = text.astype(F32)
    txt_norm = jnp.sqrt(jnp.sum(values * values, axis=-1, keepdims=True) + EPS)
    txt_dir = values / txt_norm
    slot = txt_dir.astype(BF16)
    scale = sharp[0]
    slope = jnp.zeros((rows, width), F32)
    txt_slope = jnp.zeros((rows, width), F32)
    for step in range(STEPS):
        if step > 0:
            slot = shifted(slot, 1)
        logits = scale * jnp.dot(unit, slot.T, preferred_element_type=F32) + bias[0]
        coefficient = jax.nn.sigmoid(logits)
        if step == 0:
            coefficient = coefficient - jnp.eye(rows, dtype=F32)
        coefficient = coefficient.astype(BF16)
        slope = slope + scale * jnp.dot(coefficient, slot, preferred_element_type=F32)
        share = scale * lax.dot_general(
            coefficient, unit, (((0,), (0,)), ((), ())), preferred_element_type=F32
        )
        if step > 0:
            share = shifted(share.astype(BF16), -step).astype(F32)
        txt_slope = txt_slope + share
    grad = (
        (slope - direction * jnp.sum(direction * slope, axis=-1, keepdims=True)) / norm
    ).astype(BF16)
    text_grad = (
        txt_slope - txt_dir * jnp.sum(txt_dir * txt_slope, axis=-1, keepdims=True)
    ) / txt_norm
    partial = lax.dot_general(
        x, grad, (((0,), (0,)), ((), ())), preferred_element_type=F32
    ).astype(BF16)
    head = lax.psum_scatter(partial, "fsdp", scatter_dimension=0, tiled=True).astype(F32)
    return head[None], text_grad


def solution(mesh):
    n_dp, n_fsdp = mesh.shape["dp"], mesh.shape["fsdp"]
    line = n_fsdp == 4 and n_dp % 4 == 0
    placed = (P(("dp", "fsdp"), None), P(("dp", "fsdp"), None), P("fsdp", None), P(), P())
    return jax.shard_map(
        functools.partial(line_body if line else plain_body, n_dp, n_fsdp),
        mesh=mesh,
        in_specs=placed,
        out_specs=(P("dp", "fsdp", None), P(("dp", "fsdp"), None)),
        check_vma=False,
    )
```

```python
import functools

import jax
import jax.numpy as jnp
from jax import lax
from jax.experimental import pallas as pl
from jax.experimental.pallas import tpu as pltpu
from jax.sharding import PartitionSpec as P

STEPS = 3
EPS = 1e-06
SHARES = (1, 2)
CROSS_PARTS = (1,3)
TEXT_PARTS = 2
VMEM_BYTES = 24 * 1024 * 1024
BF16, F32 = jnp.bfloat16, jnp.float32


def spaces(count):
    return [pl.BlockSpec(memory_space=pltpu.VMEM)] * count


def params(size=VMEM_BYTES):
    return pltpu.CompilerParams(vmem_limit_bytes=size)


def cost():
    return pl.CostEstimate(flops=0, bytes_accessed=0, transcendentals=0)


IN_HBM = pl.BlockSpec(memory_space=pltpu.HBM)


def place():
    where = lax.axis_index("dp")
    return lax.axis_index("fsdp"), lax.rem(where, 2), lax.rem(lax.div(where, 2), 2)


def cut_kernel(short, own, whole, part, sem):
    _, core, column = place()
    half = whole.shape[0]
    first = pltpu.make_async_copy(
        own.at[pl.ds(pl.multiple_of(core * half, 16), half), :], whole, sem.at[0]
    )
    start = pl.multiple_of(core * half + column * (half - short), 16)
    second = pltpu.make_async_copy(own.at[pl.ds(start, short), :], part, sem.at[1])
    first.start()
    second.start()
    first.wait()
    second.wait()


def cut(short, own):
    half, width = own.shape[0] // 2, own.shape[1]
    outs = (
        jax.ShapeDtypeStruct((half, width), BF16),
        jax.ShapeDtypeStruct((short, width), BF16),
    )
    return pl.pallas_call(
        functools.partial(cut_kernel, short),
        out_shape=outs,
        in_specs=[IN_HBM],
        out_specs=spaces(2),
        scratch_shapes=[pltpu.SemaphoreType.DMA((2,))],
        compiler_params=params(),
        cost_estimate=cost(),
        name="cut",
    )(own)


def prepare_kernel(t0, twin0, t2, sharp, bias, *rest):
    twin2, (units, scalars) = rest[:TEXT_PARTS], rest[TEXT_PARTS:]
    rows = t0.shape[0]
    _, core, _ = place()
    scalars[0:1, :] = jnp.broadcast_to(sharp[...], (1, scalars.shape[1]))
    scalars[1:2, :] = jnp.broadcast_to(bias[...], (1, scalars.shape[1]))

    def fill(start, block):
        values = block[...].astype(F32)
        inverse = 1.0 / jnp.sqrt(jnp.sum(values * values, axis=-1, keepdims=True) + EPS)
        units[start : start + block.shape[0], :] = (values * inverse).astype(BF16)

    fill(0, t0)
    fill(2 * rows, t2)

    @pl.when(core == 0)
    def _():
        for k, block in enumerate(twin2):
            fill(rows + k * block.shape[0], block)

    pl.when(core == 1)(lambda: fill(rows, twin0))


def prepare(t0, twin0, t2, sharp, bias, twin2):
    rows, width = t0.shape
    return pl.pallas_call(
        prepare_kernel,
        out_shape=(
            jax.ShapeDtypeStruct((STEPS * rows, width), BF16),
            jax.ShapeDtypeStruct((8, 128), F32),
        ),
        in_specs=spaces(5 + TEXT_PARTS),
        out_specs=tuple(spaces(2)),
        compiler_params=params(),
        cost_estimate=cost(),
        name="prepare",
    )(t0, twin0, t2, sharp, bias, *twin2)


def turn_kernel(depth, x, x_t, outer_t):
    x_t[...] = x[...].T
    start = jnp.where(lax.axis_index("fsdp") == 0, depth, 0)
    outer_t[...] = x_t[pl.ds(pl.multiple_of(start, 16), outer_t.shape[0]), :]


def turned(depth, x):
    rows, width = x.shape
    return pl.pallas_call(
        functools.partial(turn_kernel, depth),
        out_shape=(
            jax.ShapeDtypeStruct((width, rows), BF16),
            jax.ShapeDtypeStruct((width - depth, rows), BF16),
        ),
        in_specs=spaces(1),
        out_specs=tuple(spaces(2)),
        compiler_params=params(),
        cost_estimate=cost(),
        name="turned",
    )(x)


def rows_of(ref, block, depth):
    return ref[pl.ds(pl.multiple_of(block * depth, 16), depth), :]


def weights(mine, others, scale, bias):
    product = lax.dot_general(
        mine, others, (((1,), (1,)), ((), ())), preferred_element_type=F32
    )
    coefficient = jax.nn.sigmoid(scale * product + bias)
    row = lax.broadcasted_iota(jnp.int32, coefficient.shape, 0)
    column = lax.broadcasted_iota(jnp.int32, coefficient.shape, 1)
    coefficient = jnp.where(row == column, coefficient - 1.0, coefficient).astype(BF16)
    return coefficient, scale * jnp.sum(coefficient.astype(F32) * product, axis=-1, keepdims=True)


def picture_kernel(x, x_t, units, scalars, own, *rest):
    pieces, outs = rest[:8], rest[8 : 8 + len(SHARES)]
    unit, grad, w, proj = rest[-4:]
    part, core, column = place()
    depth = own.shape[0]
    half = depth // 2
    short = pieces[2].shape[0]
    rest_rows = half - short
    rows = x.shape[0]
    w[pl.ds(pl.multiple_of(part * depth, 16), depth), :] = own[...]
    for twin in (0, 1):
        lane = core if twin == 0 else 1 - core
        plus, minus, two, two_crossed = pieces[4 * twin : 4 * twin + 4]
        for piece, from_part in ((plus, part + 3), (minus, part + 1)):
            start = pl.multiple_of(lax.rem(from_part, 4) * depth + lane * half, 16)
            w[pl.ds(start, half), :] = piece[...]
        base = lax.rem(part + 2, 4) * depth + lane * half
        start = pl.multiple_of(base + column * rest_rows, 16)
        w[pl.ds(start, short), :] = two[...]
        source = pl.multiple_of((1 - column) * (short - rest_rows), 16)
        start = pl.multiple_of(base + (1 - column) * short, 16)
        w[pl.ds(start, rest_rows), :] = two_crossed[pl.ds(source, rest_rows), :]

    proj[...] = jnp.dot(x[...], w[...], preferred_element_type=F32)
    values = proj[...]
    inverse = 1.0 / jnp.sqrt(jnp.sum(values * values, axis=-1, keepdims=True) + EPS)
    unit[...] = (values * inverse).astype(BF16)
    scale = scalars[0:1, 0:1]
    coefficient, along = weights(unit[...], units[...], scale, scalars[1:2, 0:1])
    slope = jnp.dot(coefficient, units[...], preferred_element_type=F32)
    grad[...] = (slope * (scale * inverse) - proj[...] * (along * inverse * inverse)).astype(BF16)
    inner = jnp.logical_or(part == 1, part == 2)

    @pl.when(inner)
    def _():
        block = rows_of(x_t, 3 * (part - 1), depth)
        begin = 0
        for out in outs:
            stop = begin + out.shape[1]
            out[...] = jnp.dot(block, grad[:, begin:stop], preferred_element_type=F32).astype(BF16)
            begin = stop

    @pl.when(jnp.logical_not(inner))
    def _():
        begin = 0
        for out in outs:
            stop = begin + out.shape[1]
            out[:rows, :] = grad[:, begin:stop]
            out[rows:, :] = jnp.zeros((depth - rows, stop - begin), BF16)
            begin = stop


def picture_side(x, x_t, units, scalars, own, pieces):
    rows, width = x.shape
    depth = own.shape[0]
    out = jax.ShapeDtypeStruct((rows, width), BF16)
    sizes = [width * share // sum(SHARES) for share in SHARES]
    outs = tuple(jax.ShapeDtypeStruct((depth, size), BF16) for size in sizes)
    outs = outs + (out, out)
    return pl.pallas_call(
        picture_kernel,
        out_shape=outs,
        in_specs=spaces(13),
        out_specs=spaces(len(outs)),
        scratch_shapes=[
            pltpu.VMEM((width, width), BF16),
            pltpu.VMEM((rows, width), F32),
        ],
        compiler_params=params(),
        cost_estimate=cost(),
        name="picture_side",
    )(x, x_t, units, scalars, own, *pieces)


def text_kernel(text, scalars, u0, u1, u2, out, done, units):
    rows = text.shape[0]
    done[...] = jnp.zeros_like(done)
    for k, block in enumerate((u0, u1, u2)):
        units[k * rows : (k + 1) * rows, :] = block[...]
    values = text[...].astype(F32)
    inverse = 1.0 / jnp.sqrt(jnp.sum(values * values, axis=-1, keepdims=True) + EPS)
    scale = scalars[0:1, 0:1]
    coefficient, along = weights(
        (values * inverse).astype(BF16), units[...], scale, scalars[1:2, 0:1]
    )
    slope = jnp.dot(coefficient, units[...], preferred_element_type=F32)
    out[...] = slope * (scale * inverse) - values * (along * inverse * inverse)


def text_side(text, scalars, u0, u1, u2):
    rows, width = text.shape
    return pl.pallas_call(
        text_kernel,
        out_shape=(jax.ShapeDtypeStruct((rows, width), F32), jax.ShapeDtypeStruct((8, 128), F32)),
        in_specs=spaces(5),
        out_specs=tuple(spaces(2)),
        scratch_shapes=[pltpu.VMEM((STEPS * rows, width), BF16)],
        compiler_params=params(),
        cost_estimate=cost(),
        name="text_side",
    )(text, scalars, u0, u1, u2)


def pair_kernel(begin, parts, x_t, far_t, grad, arrived, *rest):
    outs = rest[-1 - 2 * parts :]
    kept, nears, fars = outs[0], outs[1 : 1 + parts], outs[1 + parts :]
    rows = grad.shape[0]
    depth, size = arrived.shape
    part = lax.axis_index("fsdp")
    inner = jnp.logical_or(part == 1, part == 2)
    mine = grad[:, begin : begin + size]

    def product(block):
        return jnp.dot(rows_of(x_t, block, depth), mine, preferred_element_type=F32)

    @pl.when(inner)
    def _():
        other = arrived[:rows, :]
        first = jnp.where(part == 1, 1, 0)
        for block, out in ((3 - part, nears), (lax.rem(part + 2, 4), fars), (part, [kept])):
            both = product(block) + jnp.dot(
                rows_of(far_t, block - first, depth), other, preferred_element_type=F32
            )
            size = depth // len(out)
            for k, piece in enumerate(out):
                piece[...] = both[k * size : (k + 1) * size].astype(piece.dtype)

    @pl.when(jnp.logical_not(inner))
    def _():
        kept[...] = product(part) + arrived[...].astype(F32)
        for piece in nears + fars:
            piece[...] = jnp.zeros_like(piece)


def pair_product(begin, parts, x_t, far_t, grad, arrived, after):
    depth, size = arrived.shape
    piece = jax.ShapeDtypeStruct((depth // parts, size), BF16)
    outs = (jax.ShapeDtypeStruct((depth, size), F32),) + (piece,) * (2 * parts)
    return pl.pallas_call(
        functools.partial(pair_kernel, begin, parts),
        out_shape=outs,
        in_specs=spaces(4 + len(after)),
        out_specs=spaces(len(outs)),
        compiler_params=params(),
        cost_estimate=cost(),
        name="pair_product",
    )(x_t, far_t, grad, arrived, *after)


def total_kernel(begin, parts, kept, *rest):
    nears, fars, (out, summed, sem) = rest[:parts], rest[parts : 2 * parts], rest[-3:]
    size = kept.shape[0] // parts
    for k, (near, far) in enumerate(zip(nears, fars)):
        at = slice(k * size, (k + 1) * size)
        summed[at, :] = kept[at, :] + near[...].astype(F32) + far[...].astype(F32)
    copy = pltpu.make_async_copy(summed, out.at[0, :, begin : begin + kept.shape[1]], sem)
    copy.start()
    copy.wait()


def total(begin, width, kept, nears, fars, held):
    depth, parts = kept.shape[0], len(nears)
    return pl.pallas_call(
        functools.partial(total_kernel, begin, parts),
        out_shape=jax.ShapeDtypeStruct((1, depth, width), F32),
        in_specs=spaces(1 + 2 * parts) + [IN_HBM] * len(held[:1]) + spaces(len(held[1:])),
        out_specs=IN_HBM,
        scratch_shapes=[pltpu.VMEM(kept.shape, F32), pltpu.SemaphoreType.DMA],
        input_output_aliases={1 + 2 * parts: 0} if held else {},
        compiler_params=params(),
        cost_estimate=cost(),
        name="total",
    )(kept, *nears, *fars, *held)


def line_body(n_dp, n_fsdp, x, text, w, sharp, bias):
    depth, width = w.shape
    half = depth // 2
    short = (half // 2 + 15) // 16 * 16

    def along(value, pairs):
        return lax.ppermute(value, "fsdp", pairs)

    def across(value):
        return lax.ppermute(value, "dp", [(d, d ^ 1) for d in range(n_dp)])

    def shifted(value, by):
        return lax.ppermute(value, "dp", [(d, (d + by) % n_dp) for d in range(n_dp)])

    sharp, bias = sharp.reshape(1, 1), bias.reshape(1, 1)
    swap = [(0, 1), (1, 0), (2, 3), (3, 2)]
    whole, piece = cut(short, w)
    whole, piece, text = lax.optimization_barrier((whole, piece, text))
    two = along(piece, [(f, (f + 2) % n_fsdp) for f in range(n_fsdp)])
    plus = along(whole, [(f, (f + 1) % n_fsdp) for f in range(n_fsdp)])
    minus = along(whole, [(f, (f - 1) % n_fsdp) for f in range(n_fsdp)])
    text2 = shifted(text, 2)
    x_t, outer_t = turned(depth, x)
    two, outer_t, text2 = lax.optimization_barrier((two, outer_t, text2))
    two_crossed = lax.ppermute(two, "dp", [(d, d ^ 2) for d in range(n_dp)])
    far_t = along(outer_t, swap)
    size = text.shape[0] // TEXT_PARTS
    twin2 = [across(text2[k * size : (k + 1) * size]) for k in range(TEXT_PARTS)]
    units, scalars = prepare(text, across(text), text2, sharp, bias, twin2)
    plus, minus, units, scalars, x_t = lax.optimization_barrier((plus, minus, units, scalars, x_t))
    pieces = [plus, minus, two, two_crossed]
    pieces = pieces + [across(piece) for piece in pieces]
    results = picture_side(x, x_t, units, scalars, w, pieces)
    *outward, unit, grad = results
    grad, far_t = lax.optimization_barrier((grad, far_t))
    outward[0], far_t = lax.optimization_barrier((outward[0], far_t))

    arrived = []
    for block in outward:
        if arrived:
            block, arrived[-1] = lax.optimization_barrier((block, arrived[-1]))
        arrived.append(along(block, swap))
    unit1, unit2 = shifted(unit, -1), shifted(unit, -2)
    begin, terms, after = 0, [], []
    for parts, block in zip(CROSS_PARTS, arrived):
        kept, *sent = pair_product(begin, parts, x_t, far_t, grad, block, after)
        nears = [along(n, [(1, 2), (2, 1), (0, 0), (3, 3)]) for n in sent[:parts]]
        fars = [along(n, [(1, 3), (2, 0), (0, 1), (3, 2)]) for n in sent[parts:]]
        after = []
        terms.append((begin, width, kept, nears, fars))
        begin += block.shape[1]
    text_grad, done = text_side(text, scalars, unit, unit1, unit2)
    head = total(*terms[0], [])
    for term in terms[1:]:
        head = total(*term, [head, done])
    return head, text_grad


def plain_body(n_dp, n_fsdp, x, text, w, sharp, bias):
    def shifted(value, by):
        return lax.ppermute(value, "dp", [(d, (d + by) % n_dp) for d in range(n_dp)])

    rows, width = x.shape
    proj = jnp.dot(
        x, lax.all_gather(w, "fsdp", axis=0, tiled=True), preferred_element_type=F32
    )
    norm = jnp.sqrt(jnp.sum(proj * proj, axis=-1, keepdims=True) + EPS)
    direction = proj / norm
    unit = direction.astype(BF16)
    values = text.astype(F32)
    txt_norm = jnp.sqrt(jnp.sum(values * values, axis=-1, keepdims=True) + EPS)
    txt_dir = values / txt_norm
    slot = txt_dir.astype(BF16)
    scale = sharp[0]
    slope = jnp.zeros((rows, width), F32)
    txt_slope = jnp.zeros((rows, width), F32)
    for step in range(STEPS):
        if step > 0:
            slot = shifted(slot, 1)
        logits = scale * jnp.dot(unit, slot.T, preferred_element_type=F32) + bias[0]
        coefficient = jax.nn.sigmoid(logits)
        if step == 0:
            coefficient = coefficient - jnp.eye(rows, dtype=F32)
        coefficient = coefficient.astype(BF16)
        slope = slope + scale * jnp.dot(coefficient, slot, preferred_element_type=F32)
        share = scale * lax.dot_general(
            coefficient, unit, (((0,), (0,)), ((), ())), preferred_element_type=F32
        )
        if step > 0:
            share = shifted(share.astype(BF16), -step).astype(F32)
        txt_slope = txt_slope + share
    grad = (
        (slope - direction * jnp.sum(direction * slope, axis=-1, keepdims=True)) / norm
    ).astype(BF16)
    text_grad = (
        txt_slope - txt_dir * jnp.sum(txt_dir * txt_slope, axis=-1, keepdims=True)
    ) / txt_norm
    partial = lax.dot_general(
        x, grad, (((0,), (0,)), ((), ())), preferred_element_type=F32
    ).astype(BF16)
    head = lax.psum_scatter(partial, "fsdp", scatter_dimension=0, tiled=True).astype(F32)
    return head[None], text_grad


def solution(mesh):
    n_dp, n_fsdp = mesh.shape["dp"], mesh.shape["fsdp"]
    line = n_fsdp == 4 and n_dp % 4 == 0
    placed = (P(("dp", "fsdp"), None), P(("dp", "fsdp"), None), P("fsdp", None), P(), P())
    return jax.shard_map(
        functools.partial(line_body if line else plain_body, n_dp, n_fsdp),
        mesh=mesh,
        in_specs=placed,
        out_specs=(P("dp", "fsdp", None), P(("dp", "fsdp"), None)),
        check_vma=False,
    )
```

```python
import functools

import jax
import jax.numpy as jnp
from jax import lax
from jax.experimental import pallas as pl
from jax.experimental.pallas import tpu as pltpu
from jax.sharding import PartitionSpec as P

STEPS = 3
EPS = 1e-06
SHARES = (1, 2)
CROSS_PARTS = (1,3)
TEXT_PARTS = 2
VMEM_BYTES = 24 * 1024 * 1024
BF16, F32 = jnp.bfloat16, jnp.float32


def spaces(count):
    return [pl.BlockSpec(memory_space=pltpu.VMEM)] * count


def params(size=VMEM_BYTES):
    return pltpu.CompilerParams(vmem_limit_bytes=size)


def cost():
    return pl.CostEstimate(flops=0, bytes_accessed=0, transcendentals=0)


IN_HBM = pl.BlockSpec(memory_space=pltpu.HBM)


def place():
    where = lax.axis_index("dp")
    return lax.axis_index("fsdp"), lax.rem(where, 2), lax.rem(lax.div(where, 2), 2)


def cut_kernel(short, own, whole, part, sem):
    _, core, column = place()
    half = whole.shape[0]
    first = pltpu.make_async_copy(
        own.at[pl.ds(pl.multiple_of(core * half, 16), half), :], whole, sem.at[0]
    )
    start = pl.multiple_of(core * half + column * (half - short), 16)
    second = pltpu.make_async_copy(own.at[pl.ds(start, short), :], part, sem.at[1])
    first.start()
    second.start()
    first.wait()
    second.wait()


def cut(short, own):
    half, width = own.shape[0] // 2, own.shape[1]
    outs = (
        jax.ShapeDtypeStruct((half, width), BF16),
        jax.ShapeDtypeStruct((short, width), BF16),
    )
    return pl.pallas_call(
        functools.partial(cut_kernel, short),
        out_shape=outs,
        in_specs=[IN_HBM],
        out_specs=spaces(2),
        scratch_shapes=[pltpu.SemaphoreType.DMA((2,))],
        compiler_params=params(),
        cost_estimate=cost(),
        name="cut",
    )(own)


def prepare_kernel(t0, twin0, t2, sharp, bias, *rest):
    twin2, (units, scalars) = rest[:TEXT_PARTS], rest[TEXT_PARTS:]
    rows = t0.shape[0]
    _, core, _ = place()
    scalars[0:1, :] = jnp.broadcast_to(sharp[...], (1, scalars.shape[1]))
    scalars[1:2, :] = jnp.broadcast_to(bias[...], (1, scalars.shape[1]))

    def fill(start, block):
        values = block[...].astype(F32)
        inverse = 1.0 / jnp.sqrt(jnp.sum(values * values, axis=-1, keepdims=True) + EPS)
        units[start : start + block.shape[0], :] = (values * inverse).astype(BF16)

    fill(0, t0)
    fill(2 * rows, t2)

    @pl.when(core == 0)
    def _():
        for k, block in enumerate(twin2):
            fill(rows + k * block.shape[0], block)

    pl.when(core == 1)(lambda: fill(rows, twin0))


def prepare(t0, twin0, t2, sharp, bias, twin2):
    rows, width = t0.shape
    return pl.pallas_call(
        prepare_kernel,
        out_shape=(
            jax.ShapeDtypeStruct((STEPS * rows, width), BF16),
            jax.ShapeDtypeStruct((8, 128), F32),
        ),
        in_specs=spaces(5 + TEXT_PARTS),
        out_specs=tuple(spaces(2)),
        compiler_params=params(),
        cost_estimate=cost(),
        name="prepare",
    )(t0, twin0, t2, sharp, bias, *twin2)


def turn_kernel(depth, x, x_t, outer_t):
    x_t[...] = x[...].T
    start = jnp.where(lax.axis_index("fsdp") == 0, depth, 0)
    outer_t[...] = x_t[pl.ds(pl.multiple_of(start, 16), outer_t.shape[0]), :]


def turned(depth, x):
    rows, width = x.shape
    return pl.pallas_call(
        functools.partial(turn_kernel, depth),
        out_shape=(
            jax.ShapeDtypeStruct((width, rows), BF16),
            jax.ShapeDtypeStruct((width - depth, rows), BF16),
        ),
        in_specs=spaces(1),
        out_specs=tuple(spaces(2)),
        compiler_params=params(),
        cost_estimate=cost(),
        name="turned",
    )(x)


def rows_of(ref, block, depth):
    return ref[pl.ds(pl.multiple_of(block * depth, 16), depth), :]


def weights(mine, others, scale, bias):
    product = lax.dot_general(
        mine, others, (((1,), (1,)), ((), ())), preferred_element_type=F32
    )
    coefficient = jax.nn.sigmoid(scale * product + bias)
    row = lax.broadcasted_iota(jnp.int32, coefficient.shape, 0)
    column = lax.broadcasted_iota(jnp.int32, coefficient.shape, 1)
    coefficient = jnp.where(row == column, coefficient - 1.0, coefficient).astype(BF16)
    return coefficient, scale * jnp.sum(coefficient.astype(F32) * product, axis=-1, keepdims=True)


def picture_kernel(x, x_t, units, scalars, own, *rest):
    pieces, outs = rest[:8], rest[8 : 8 + len(SHARES)]
    unit, grad, w, proj = rest[-4:]
    part, core, column = place()
    depth = own.shape[0]
    half = depth // 2
    short = pieces[2].shape[0]
    rest_rows = half - short
    rows = x.shape[0]
    w[pl.ds(pl.multiple_of(part * depth, 16), depth), :] = own[...]
    for twin in (0, 1):
        lane = core if twin == 0 else 1 - core
        plus, minus, two, two_crossed = pieces[4 * twin : 4 * twin + 4]
        for piece, from_part in ((plus, part + 3), (minus, part + 1)):
            start = pl.multiple_of(lax.rem(from_part, 4) * depth + lane * half, 16)
            w[pl.ds(start, half), :] = piece[...]
        base = lax.rem(part + 2, 4) * depth + lane * half
        start = pl.multiple_of(base + column * rest_rows, 16)
        w[pl.ds(start, short), :] = two[...]
        source = pl.multiple_of((1 - column) * (short - rest_rows), 16)
        start = pl.multiple_of(base + (1 - column) * short, 16)
        w[pl.ds(start, rest_rows), :] = two_crossed[pl.ds(source, rest_rows), :]

    proj[...] = jnp.dot(x[...], w[...], preferred_element_type=F32)
    values = proj[...]
    inverse = 1.0 / jnp.sqrt(jnp.sum(values * values, axis=-1, keepdims=True) + EPS)
    unit[...] = (values * inverse).astype(BF16)
    scale = scalars[0:1, 0:1]
    coefficient, along = weights(unit[...], units[...], scale, scalars[1:2, 0:1])
    slope = jnp.dot(coefficient, units[...], preferred_element_type=F32)
    grad[...] = (slope * (scale * inverse) - proj[...] * (along * inverse * inverse)).astype(BF16)
    inner = jnp.logical_or(part == 1, part == 2)

    @pl.when(inner)
    def _():
        block = rows_of(x_t, 3 * (part - 1), depth)
        begin = 0
        for out in outs:
            stop = begin + out.shape[1]
            out[...] = jnp.dot(block, grad[:, begin:stop], preferred_element_type=F32).astype(BF16)
            begin = stop

    @pl.when(jnp.logical_not(inner))
    def _():
        begin = 0
        for out in outs:
            stop = begin + out.shape[1]
            out[:rows, :] = grad[:, begin:stop]
            out[rows:, :] = jnp.zeros((depth - rows, stop - begin), BF16)
            begin = stop


def picture_side(x, x_t, units, scalars, own, pieces):
    rows, width = x.shape
    depth = own.shape[0]
    out = jax.ShapeDtypeStruct((rows, width), BF16)
    sizes = [width * share // sum(SHARES) for share in SHARES]
    outs = tuple(jax.ShapeDtypeStruct((depth, size), BF16) for size in sizes)
    outs = outs + (out, out)
    return pl.pallas_call(
        picture_kernel,
        out_shape=outs,
        in_specs=spaces(13),
        out_specs=spaces(len(outs)),
        scratch_shapes=[
            pltpu.VMEM((width, width), BF16),
            pltpu.VMEM((rows, width), F32),
        ],
        compiler_params=params(),
        cost_estimate=cost(),
        name="picture_side",
    )(x, x_t, units, scalars, own, *pieces)


def text_kernel(text, scalars, u0, u1, u2, out, done, units):
    rows = text.shape[0]
    done[...] = jnp.zeros_like(done)
    for k, block in enumerate((u0, u1, u2)):
        units[k * rows : (k + 1) * rows, :] = block[...]
    values = text[...].astype(F32)
    inverse = 1.0 / jnp.sqrt(jnp.sum(values * values, axis=-1, keepdims=True) + EPS)
    scale = scalars[0:1, 0:1]
    coefficient, along = weights(
        (values * inverse).astype(BF16), units[...], scale, scalars[1:2, 0:1]
    )
    slope = jnp.dot(coefficient, units[...], preferred_element_type=F32)
    out[...] = slope * (scale * inverse) - values * (along * inverse * inverse)


def text_side(text, scalars, u0, u1, u2):
    rows, width = text.shape
    return pl.pallas_call(
        text_kernel,
        out_shape=(jax.ShapeDtypeStruct((rows, width), F32), jax.ShapeDtypeStruct((8, 128), F32)),
        in_specs=spaces(5),
        out_specs=tuple(spaces(2)),
        scratch_shapes=[pltpu.VMEM((STEPS * rows, width), BF16)],
        compiler_params=params(),
        cost_estimate=cost(),
        name="text_side",
    )(text, scalars, u0, u1, u2)


def pair_kernel(begin, parts, x_t, far_t, grad, arrived, *rest):
    outs = rest[-1 - 2 * parts :]
    kept, nears, fars = outs[0], outs[1 : 1 + parts], outs[1 + parts :]
    rows = grad.shape[0]
    depth, size = arrived.shape
    part = lax.axis_index("fsdp")
    inner = jnp.logical_or(part == 1, part == 2)
    mine = grad[:, begin : begin + size]

    def product(block):
        return jnp.dot(rows_of(x_t, block, depth), mine, preferred_element_type=F32)

    @pl.when(inner)
    def _():
        other = arrived[:rows, :]
        first = jnp.where(part == 1, 1, 0)
        for block, out in ((3 - part, nears), (lax.rem(part + 2, 4), fars), (part, [kept])):
            both = product(block) + jnp.dot(
                rows_of(far_t, block - first, depth), other, preferred_element_type=F32
            )
            size = depth // len(out)
            for k, piece in enumerate(out):
                piece[...] = both[k * size : (k + 1) * size].astype(piece.dtype)

    @pl.when(jnp.logical_not(inner))
    def _():
        kept[...] = product(part) + arrived[...].astype(F32)
        for piece in nears + fars:
            piece[...] = jnp.zeros_like(piece)


def pair_product(begin, parts, x_t, far_t, grad, arrived, after):
    depth, size = arrived.shape
    piece = jax.ShapeDtypeStruct((depth // parts, size), BF16)
    outs = (jax.ShapeDtypeStruct((depth, size), F32),) + (piece,) * (2 * parts)
    return pl.pallas_call(
        functools.partial(pair_kernel, begin, parts),
        out_shape=outs,
        in_specs=spaces(4 + len(after)),
        out_specs=spaces(len(outs)),
        compiler_params=params(),
        cost_estimate=cost(),
        name="pair_product",
    )(x_t, far_t, grad, arrived, *after)


def total_kernel(begin, parts, kept, *rest):
    nears, fars, (out, summed, sem) = rest[:parts], rest[parts : 2 * parts], rest[-3:]
    size = kept.shape[0] // parts
    for k, (near, far) in enumerate(zip(nears, fars)):
        at = slice(k * size, (k + 1) * size)
        summed[at, :] = kept[at, :] + near[...].astype(F32) + far[...].astype(F32)
    copy = pltpu.make_async_copy(summed, out.at[0, :, begin : begin + kept.shape[1]], sem)
    copy.start()
    copy.wait()


def total(begin, width, kept, nears, fars, held):
    depth, parts = kept.shape[0], len(nears)
    return pl.pallas_call(
        functools.partial(total_kernel, begin, parts),
        out_shape=jax.ShapeDtypeStruct((1, depth, width), F32),
        in_specs=spaces(1 + 2 * parts) + [IN_HBM] * len(held[:1]) + spaces(len(held[1:])),
        out_specs=IN_HBM,
        scratch_shapes=[pltpu.VMEM(kept.shape, F32), pltpu.SemaphoreType.DMA],
        input_output_aliases={1 + 2 * parts: 0} if held else {},
        compiler_params=params(),
        cost_estimate=cost(),
        name="total",
    )(kept, *nears, *fars, *held)


def line_body(n_dp, n_fsdp, x, text, w, sharp, bias):
    depth, width = w.shape
    half = depth // 2
    short = (half // 2 + 15) // 16 * 16

    def along(value, pairs):
        return lax.ppermute(value, "fsdp", pairs)

    def across(value):
        return lax.ppermute(value, "dp", [(d, d ^ 1) for d in range(n_dp)])

    def shifted(value, by):
        return lax.ppermute(value, "dp", [(d, (d + by) % n_dp) for d in range(n_dp)])

    sharp, bias = sharp.reshape(1, 1), bias.reshape(1, 1)
    swap = [(0, 1), (1, 0), (2, 3), (3, 2)]
    whole, piece = cut(short, w)
    whole, piece, text = lax.optimization_barrier((whole, piece, text))
    two = along(piece, [(f, (f + 2) % n_fsdp) for f in range(n_fsdp)])
    plus = along(whole, [(f, (f + 1) % n_fsdp) for f in range(n_fsdp)])
    minus = along(whole, [(f, (f - 1) % n_fsdp) for f in range(n_fsdp)])
    text2 = shifted(text, 2)
    x_t, outer_t = turned(depth, x)
    two, outer_t, text2 = lax.optimization_barrier((two, outer_t, text2))
    two_crossed = lax.ppermute(two, "dp", [(d, d ^ 2) for d in range(n_dp)])
    far_t = along(outer_t, swap)
    size = text.shape[0] // TEXT_PARTS
    twin2 = [across(text2[k * size : (k + 1) * size]) for k in range(TEXT_PARTS)]
    units, scalars = prepare(text, across(text), text2, sharp, bias, twin2)
    plus, minus, units, scalars, x_t = lax.optimization_barrier((plus, minus, units, scalars, x_t))
    pieces = [plus, minus, two, two_crossed]
    pieces = pieces + [across(piece) for piece in pieces]
    results = picture_side(x, x_t, units, scalars, w, pieces)
    *outward, unit, grad = results
    grad, far_t = lax.optimization_barrier((grad, far_t))
    outward[0], far_t = lax.optimization_barrier((outward[0], far_t))

    arrived = []
    for block in outward:
        if arrived:
            block, arrived[-1] = lax.optimization_barrier((block, arrived[-1]))
        arrived.append(along(block, swap))
    unit1, unit2 = shifted(unit, -1), shifted(unit, -2)
    begin, terms, after = 0, [], []
    for parts, block in zip(CROSS_PARTS, arrived):
        kept, *sent = pair_product(begin, parts, x_t, far_t, grad, block, after)
        nears = [along(n, [(1, 2), (2, 1), (0, 0), (3, 3)]) for n in sent[:parts]]
        ends = [(0, 1), (3, 2)] if begin > 0 else []
        fars = [along(n, [(1, 3), (2, 0)] + ends) for n in sent[parts:]]
        after = []
        terms.append((begin, width, kept, nears, fars))
        begin += block.shape[1]
    text_grad, done = text_side(text, scalars, unit, unit1, unit2)
    head = total(*terms[0], [])
    for term in terms[1:]:
        head = total(*term, [head, done])
    return head, text_grad


def plain_body(n_dp, n_fsdp, x, text, w, sharp, bias):
    def shifted(value, by):
        return lax.ppermute(value, "dp", [(d, (d + by) % n_dp) for d in range(n_dp)])

    rows, width = x.shape
    proj = jnp.dot(
        x, lax.all_gather(w, "fsdp", axis=0, tiled=True), preferred_element_type=F32
    )
    norm = jnp.sqrt(jnp.sum(proj * proj, axis=-1, keepdims=True) + EPS)
    direction = proj / norm
    unit = direction.astype(BF16)
    values = text.astype(F32)
    txt_norm = jnp.sqrt(jnp.sum(values * values, axis=-1, keepdims=True) + EPS)
    txt_dir = values / txt_norm
    slot = txt_dir.astype(BF16)
    scale = sharp[0]
    slope = jnp.zeros((rows, width), F32)
    txt_slope = jnp.zeros((rows, width), F32)
    for step in range(STEPS):
        if step > 0:
            slot = shifted(slot, 1)
        logits = scale * jnp.dot(unit, slot.T, preferred_element_type=F32) + bias[0]
        coefficient = jax.nn.sigmoid(logits)
        if step == 0:
            coefficient = coefficient - jnp.eye(rows, dtype=F32)
        coefficient = coefficient.astype(BF16)
        slope = slope + scale * jnp.dot(coefficient, slot, preferred_element_type=F32)
        share = scale * lax.dot_general(
            coefficient, unit, (((0,), (0,)), ((), ())), preferred_element_type=F32
        )
        if step > 0:
            share = shifted(share.astype(BF16), -step).astype(F32)
        txt_slope = txt_slope + share
    grad = (
        (slope - direction * jnp.sum(direction * slope, axis=-1, keepdims=True)) / norm
    ).astype(BF16)
    text_grad = (
        txt_slope - txt_dir * jnp.sum(txt_dir * txt_slope, axis=-1, keepdims=True)
    ) / txt_norm
    partial = lax.dot_general(
        x, grad, (((0,), (0,)), ((), ())), preferred_element_type=F32
    ).astype(BF16)
    head = lax.psum_scatter(partial, "fsdp", scatter_dimension=0, tiled=True).astype(F32)
    return head[None], text_grad


def solution(mesh):
    n_dp, n_fsdp = mesh.shape["dp"], mesh.shape["fsdp"]
    line = n_fsdp == 4 and n_dp % 4 == 0
    placed = (P(("dp", "fsdp"), None), P(("dp", "fsdp"), None), P("fsdp", None), P(), P())
    return jax.shard_map(
        functools.partial(line_body if line else plain_body, n_dp, n_fsdp),
        mesh=mesh,
        in_specs=placed,
        out_specs=(P("dp", "fsdp", None), P(("dp", "fsdp"), None)),
        check_vma=False,
    )
```

```python
import functools

import jax
import jax.numpy as jnp
from jax import lax
from jax.experimental import pallas as pl
from jax.experimental.pallas import tpu as pltpu
from jax.sharding import PartitionSpec as P

STEPS = 3
EPS = 1e-06
SHARES = (3, 3, 3)
CROSS_PARTS = (1, 2, 3)
TEXT_PARTS = 2
VMEM_BYTES = 24 * 1024 * 1024
BF16, F32 = jnp.bfloat16, jnp.float32


def spaces(count):
    return [pl.BlockSpec(memory_space=pltpu.VMEM)] * count


def params(size=VMEM_BYTES):
    return pltpu.CompilerParams(vmem_limit_bytes=size)


def cost():
    return pl.CostEstimate(flops=0, bytes_accessed=0, transcendentals=0)


IN_HBM = pl.BlockSpec(memory_space=pltpu.HBM)


def place():
    where = lax.axis_index("dp")
    return lax.axis_index("fsdp"), lax.rem(where, 2), lax.rem(lax.div(where, 2), 2)


def cut_kernel(short, own, whole, part, sem):
    _, core, column = place()
    half = whole.shape[0]
    first = pltpu.make_async_copy(
        own.at[pl.ds(pl.multiple_of(core * half, 16), half), :], whole, sem.at[0]
    )
    start = pl.multiple_of(core * half + column * (half - short), 16)
    second = pltpu.make_async_copy(own.at[pl.ds(start, short), :], part, sem.at[1])
    first.start()
    second.start()
    first.wait()
    second.wait()


def cut(short, own):
    half, width = own.shape[0] // 2, own.shape[1]
    outs = (
        jax.ShapeDtypeStruct((half, width), BF16),
        jax.ShapeDtypeStruct((short, width), BF16),
    )
    return pl.pallas_call(
        functools.partial(cut_kernel, short),
        out_shape=outs,
        in_specs=[IN_HBM],
        out_specs=spaces(2),
        scratch_shapes=[pltpu.SemaphoreType.DMA((2,))],
        compiler_params=params(),
        cost_estimate=cost(),
        name="cut",
    )(own)


def prepare_kernel(t0, twin0, t2, sharp, bias, *rest):
    twin2, (units, scalars) = rest[:TEXT_PARTS], rest[TEXT_PARTS:]
    rows = t0.shape[0]
    _, core, _ = place()
    scalars[0:1, :] = jnp.broadcast_to(sharp[...], (1, scalars.shape[1]))
    scalars[1:2, :] = jnp.broadcast_to(bias[...], (1, scalars.shape[1]))

    def fill(start, block):
        values = block[...].astype(F32)
        inverse = 1.0 / jnp.sqrt(jnp.sum(values * values, axis=-1, keepdims=True) + EPS)
        units[start : start + block.shape[0], :] = (values * inverse).astype(BF16)

    fill(0, t0)
    fill(2 * rows, t2)

    @pl.when(core == 0)
    def _():
        for k, block in enumerate(twin2):
            fill(rows + k * block.shape[0], block)

    pl.when(core == 1)(lambda: fill(rows, twin0))


def prepare(t0, twin0, t2, sharp, bias, twin2):
    rows, width = t0.shape
    return pl.pallas_call(
        prepare_kernel,
        out_shape=(
            jax.ShapeDtypeStruct((STEPS * rows, width), BF16),
            jax.ShapeDtypeStruct((8, 128), F32),
        ),
        in_specs=spaces(5 + TEXT_PARTS),
        out_specs=tuple(spaces(2)),
        compiler_params=params(),
        cost_estimate=cost(),
        name="prepare",
    )(t0, twin0, t2, sharp, bias, *twin2)


def turn_kernel(depth, x, x_t, outer_t):
    x_t[...] = x[...].T
    start = jnp.where(lax.axis_index("fsdp") == 0, depth, 0)
    outer_t[...] = x_t[pl.ds(pl.multiple_of(start, 16), outer_t.shape[0]), :]


def turned(depth, x):
    rows, width = x.shape
    return pl.pallas_call(
        functools.partial(turn_kernel, depth),
        out_shape=(
            jax.ShapeDtypeStruct((width, rows), BF16),
            jax.ShapeDtypeStruct((width - depth, rows), BF16),
        ),
        in_specs=spaces(1),
        out_specs=tuple(spaces(2)),
        compiler_params=params(),
        cost_estimate=cost(),
        name="turned",
    )(x)


def rows_of(ref, block, depth):
    return ref[pl.ds(pl.multiple_of(block * depth, 16), depth), :]


def weights(mine, others, scale, bias):
    product = lax.dot_general(
        mine, others, (((1,), (1,)), ((), ())), preferred_element_type=F32
    )
    coefficient = jax.nn.sigmoid(scale * product + bias)
    row = lax.broadcasted_iota(jnp.int32, coefficient.shape, 0)
    column = lax.broadcasted_iota(jnp.int32, coefficient.shape, 1)
    coefficient = jnp.where(row == column, coefficient - 1.0, coefficient).astype(BF16)
    return coefficient, scale * jnp.sum(coefficient.astype(F32) * product, axis=-1, keepdims=True)


def picture_kernel(x, x_t, units, scalars, own, *rest):
    pieces, outs = rest[:8], rest[8 : 8 + len(SHARES)]
    unit, grad, w, proj = rest[-4:]
    part, core, column = place()
    depth = own.shape[0]
    half = depth // 2
    short = pieces[2].shape[0]
    rest_rows = half - short
    rows = x.shape[0]
    w[pl.ds(pl.multiple_of(part * depth, 16), depth), :] = own[...]
    for twin in (0, 1):
        lane = core if twin == 0 else 1 - core
        plus, minus, two, two_crossed = pieces[4 * twin : 4 * twin + 4]
        for piece, from_part in ((plus, part + 3), (minus, part + 1)):
            start = pl.multiple_of(lax.rem(from_part, 4) * depth + lane * half, 16)
            w[pl.ds(start, half), :] = piece[...]
        base = lax.rem(part + 2, 4) * depth + lane * half
        start = pl.multiple_of(base + column * rest_rows, 16)
        w[pl.ds(start, short), :] = two[...]
        source = pl.multiple_of((1 - column) * (short - rest_rows), 16)
        start = pl.multiple_of(base + (1 - column) * short, 16)
        w[pl.ds(start, rest_rows), :] = two_crossed[pl.ds(source, rest_rows), :]

    proj[...] = jnp.dot(x[...], w[...], preferred_element_type=F32)
    values = proj[...]
    inverse = 1.0 / jnp.sqrt(jnp.sum(values * values, axis=-1, keepdims=True) + EPS)
    unit[...] = (values * inverse).astype(BF16)
    scale = scalars[0:1, 0:1]
    coefficient, along = weights(unit[...], units[...], scale, scalars[1:2, 0:1])
    slope = jnp.dot(coefficient, units[...], preferred_element_type=F32)
    grad[...] = (slope * (scale * inverse) - proj[...] * (along * inverse * inverse)).astype(BF16)
    inner = jnp.logical_or(part == 1, part == 2)

    @pl.when(inner)
    def _():
        block = rows_of(x_t, 3 * (part - 1), depth)
        begin = 0
        for out in outs:
            stop = begin + out.shape[1]
            out[...] = jnp.dot(block, grad[:, begin:stop], preferred_element_type=F32).astype(BF16)
            begin = stop

    @pl.when(jnp.logical_not(inner))
    def _():
        begin = 0
        for out in outs:
            stop = begin + out.shape[1]
            out[:rows, :] = grad[:, begin:stop]
            out[rows:, :] = jnp.zeros((depth - rows, stop - begin), BF16)
            begin = stop


def picture_side(x, x_t, units, scalars, own, pieces):
    rows, width = x.shape
    depth = own.shape[0]
    out = jax.ShapeDtypeStruct((rows, width), BF16)
    sizes = [width * share // sum(SHARES) for share in SHARES]
    outs = tuple(jax.ShapeDtypeStruct((depth, size), BF16) for size in sizes)
    outs = outs + (out, out)
    return pl.pallas_call(
        picture_kernel,
        out_shape=outs,
        in_specs=spaces(13),
        out_specs=spaces(len(outs)),
        scratch_shapes=[
            pltpu.VMEM((width, width), BF16),
            pltpu.VMEM((rows, width), F32),
        ],
        compiler_params=params(),
        cost_estimate=cost(),
        name="picture_side",
    )(x, x_t, units, scalars, own, *pieces)


def text_kernel(text, scalars, u0, u1, u2, out, done, units):
    rows = text.shape[0]
    done[...] = jnp.zeros_like(done)
    for k, block in enumerate((u0, u1, u2)):
        units[k * rows : (k + 1) * rows, :] = block[...]
    values = text[...].astype(F32)
    inverse = 1.0 / jnp.sqrt(jnp.sum(values * values, axis=-1, keepdims=True) + EPS)
    scale = scalars[0:1, 0:1]
    coefficient, along = weights(
        (values * inverse).astype(BF16), units[...], scale, scalars[1:2, 0:1]
    )
    slope = jnp.dot(coefficient, units[...], preferred_element_type=F32)
    out[...] = slope * (scale * inverse) - values * (along * inverse * inverse)


def text_side(text, scalars, u0, u1, u2):
    rows, width = text.shape
    return pl.pallas_call(
        text_kernel,
        out_shape=(jax.ShapeDtypeStruct((rows, width), F32), jax.ShapeDtypeStruct((8, 128), F32)),
        in_specs=spaces(5),
        out_specs=tuple(spaces(2)),
        scratch_shapes=[pltpu.VMEM((STEPS * rows, width), BF16)],
        compiler_params=params(),
        cost_estimate=cost(),
        name="text_side",
    )(text, scalars, u0, u1, u2)


def pair_kernel(begin, parts, x_t, far_t, grad, arrived, *rest):
    outs = rest[-1 - 2 * parts :]
    kept, nears, fars = outs[0], outs[1 : 1 + parts], outs[1 + parts :]
    rows = grad.shape[0]
    depth, size = arrived.shape
    part = lax.axis_index("fsdp")
    inner = jnp.logical_or(part == 1, part == 2)
    mine = grad[:, begin : begin + size]

    def product(block):
        return jnp.dot(rows_of(x_t, block, depth), mine, preferred_element_type=F32)

    @pl.when(inner)
    def _():
        other = arrived[:rows, :]
        first = jnp.where(part == 1, 1, 0)
        for block, out in ((3 - part, nears), (lax.rem(part + 2, 4), fars), (part, [kept])):
            both = product(block) + jnp.dot(
                rows_of(far_t, block - first, depth), other, preferred_element_type=F32
            )
            size = depth // len(out)
            for k, piece in enumerate(out):
                piece[...] = both[k * size : (k + 1) * size].astype(piece.dtype)

    @pl.when(jnp.logical_not(inner))
    def _():
        kept[...] = product(part) + arrived[...].astype(F32)
        for piece in nears + fars:
            piece[...] = jnp.zeros_like(piece)


def pair_product(begin, parts, x_t, far_t, grad, arrived, after):
    depth, size = arrived.shape
    piece = jax.ShapeDtypeStruct((depth // parts, size), BF16)
    outs = (jax.ShapeDtypeStruct((depth, size), F32),) + (piece,) * (2 * parts)
    return pl.pallas_call(
        functools.partial(pair_kernel, begin, parts),
        out_shape=outs,
        in_specs=spaces(4 + len(after)),
        out_specs=spaces(len(outs)),
        compiler_params=params(),
        cost_estimate=cost(),
        name="pair_product",
    )(x_t, far_t, grad, arrived, *after)


def total_kernel(begin, parts, kept, *rest):
    nears, fars, (out, summed, sem) = rest[:parts], rest[parts : 2 * parts], rest[-3:]
    size = kept.shape[0] // parts
    for k, (near, far) in enumerate(zip(nears, fars)):
        at = slice(k * size, (k + 1) * size)
        summed[at, :] = kept[at, :] + near[...].astype(F32) + far[...].astype(F32)
    copy = pltpu.make_async_copy(summed, out.at[0, :, begin : begin + kept.shape[1]], sem)
    copy.start()
    copy.wait()


def total(begin, width, kept, nears, fars, held):
    depth, parts = kept.shape[0], len(nears)
    return pl.pallas_call(
        functools.partial(total_kernel, begin, parts),
        out_shape=jax.ShapeDtypeStruct((1, depth, width), F32),
        in_specs=spaces(1 + 2 * parts) + [IN_HBM] * len(held[:1]) + spaces(len(held[1:])),
        out_specs=IN_HBM,
        scratch_shapes=[pltpu.VMEM(kept.shape, F32), pltpu.SemaphoreType.DMA],
        input_output_aliases={1 + 2 * parts: 0} if held else {},
        compiler_params=params(),
        cost_estimate=cost(),
        name="total",
    )(kept, *nears, *fars, *held)


def line_body(n_dp, n_fsdp, x, text, w, sharp, bias):
    depth, width = w.shape
    half = depth // 2
    short = (half // 2 + 15) // 16 * 16

    def along(value, pairs):
        return lax.ppermute(value, "fsdp", pairs)

    def across(value):
        return lax.ppermute(value, "dp", [(d, d ^ 1) for d in range(n_dp)])

    def shifted(value, by):
        return lax.ppermute(value, "dp", [(d, (d + by) % n_dp) for d in range(n_dp)])

    sharp, bias = sharp.reshape(1, 1), bias.reshape(1, 1)
    swap = [(0, 1), (1, 0), (2, 3), (3, 2)]
    whole, piece = cut(short, w)
    whole, piece, text = lax.optimization_barrier((whole, piece, text))
    two = along(piece, [(f, (f + 2) % n_fsdp) for f in range(n_fsdp)])
    plus = along(whole, [(f, (f + 1) % n_fsdp) for f in range(n_fsdp)])
    minus = along(whole, [(f, (f - 1) % n_fsdp) for f in range(n_fsdp)])
    text2 = shifted(text, 2)
    x_t, outer_t = turned(depth, x)
    two, outer_t, text2 = lax.optimization_barrier((two, outer_t, text2))
    two_crossed = lax.ppermute(two, "dp", [(d, d ^ 2) for d in range(n_dp)])
    far_t = along(outer_t, swap)
    size = text.shape[0] // TEXT_PARTS
    twin2 = [across(text2[k * size : (k + 1) * size]) for k in range(TEXT_PARTS)]
    units, scalars = prepare(text, across(text), text2, sharp, bias, twin2)
    plus, minus, units, scalars, x_t = lax.optimization_barrier((plus, minus, units, scalars, x_t))
    pieces = [plus, minus, two, two_crossed]
    pieces = pieces + [across(piece) for piece in pieces]
    results = picture_side(x, x_t, units, scalars, w, pieces)
    *outward, unit, grad = results
    grad, far_t = lax.optimization_barrier((grad, far_t))
    outward[0], far_t = lax.optimization_barrier((outward[0], far_t))

    arrived = []
    for block in outward:
        if arrived:
            block, arrived[-1] = lax.optimization_barrier((block, arrived[-1]))
        arrived.append(along(block, swap))
    unit1, unit2 = shifted(unit, -1), shifted(unit, -2)
    begin, terms, after = 0, [], []
    for parts, block in zip(CROSS_PARTS, arrived):
        kept, *sent = pair_product(begin, parts, x_t, far_t, grad, block, after)
        nears = [along(n, [(1, 2), (2, 1), (0, 0), (3, 3)]) for n in sent[:parts]]
        ends = [(0, 1), (3, 2)] if block is arrived[-1] else []
        fars = [along(n, [(1, 3), (2, 0)] + ends) for n in sent[parts:]]
        after = []
        terms.append((begin, width, kept, nears, fars))
        begin += block.shape[1]
    text_grad, done = text_side(text, scalars, unit, unit1, unit2)
    head = total(*terms[0], [])
    for term in terms[1:]:
        head = total(*term, [head, done] if term is terms[-1] else [head])
    return head, text_grad


def plain_body(n_dp, n_fsdp, x, text, w, sharp, bias):
    def shifted(value, by):
        return lax.ppermute(value, "dp", [(d, (d + by) % n_dp) for d in range(n_dp)])

    rows, width = x.shape
    proj = jnp.dot(
        x, lax.all_gather(w, "fsdp", axis=0, tiled=True), preferred_element_type=F32
    )
    norm = jnp.sqrt(jnp.sum(proj * proj, axis=-1, keepdims=True) + EPS)
    direction = proj / norm
    unit = direction.astype(BF16)
    values = text.astype(F32)
    txt_norm = jnp.sqrt(jnp.sum(values * values, axis=-1, keepdims=True) + EPS)
    txt_dir = values / txt_norm
    slot = txt_dir.astype(BF16)
    scale = sharp[0]
    slope = jnp.zeros((rows, width), F32)
    txt_slope = jnp.zeros((rows, width), F32)
    for step in range(STEPS):
        if step > 0:
            slot = shifted(slot, 1)
        logits = scale * jnp.dot(unit, slot.T, preferred_element_type=F32) + bias[0]
        coefficient = jax.nn.sigmoid(logits)
        if step == 0:
            coefficient = coefficient - jnp.eye(rows, dtype=F32)
        coefficient = coefficient.astype(BF16)
        slope = slope + scale * jnp.dot(coefficient, slot, preferred_element_type=F32)
        share = scale * lax.dot_general(
            coefficient, unit, (((0,), (0,)), ((), ())), preferred_element_type=F32
        )
        if step > 0:
            share = shifted(share.astype(BF16), -step).astype(F32)
        txt_slope = txt_slope + share
    grad = (
        (slope - direction * jnp.sum(direction * slope, axis=-1, keepdims=True)) / norm
    ).astype(BF16)
    text_grad = (
        txt_slope - txt_dir * jnp.sum(txt_dir * txt_slope, axis=-1, keepdims=True)
    ) / txt_norm
    partial = lax.dot_general(
        x, grad, (((0,), (0,)), ((), ())), preferred_element_type=F32
    ).astype(BF16)
    head = lax.psum_scatter(partial, "fsdp", scatter_dimension=0, tiled=True).astype(F32)
    return head[None], text_grad


def solution(mesh):
    n_dp, n_fsdp = mesh.shape["dp"], mesh.shape["fsdp"]
    line = n_fsdp == 4 and n_dp % 4 == 0
    placed = (P(("dp", "fsdp"), None), P(("dp", "fsdp"), None), P("fsdp", None), P(), P())
    return jax.shard_map(
        functools.partial(line_body if line else plain_body, n_dp, n_fsdp),
        mesh=mesh,
        in_specs=placed,
        out_specs=(P("dp", "fsdp", None), P(("dp", "fsdp"), None)),
        check_vma=False,
    )
```

```python
import functools

import jax
import jax.numpy as jnp
from jax import lax
from jax.experimental import pallas as pl
from jax.experimental.pallas import tpu as pltpu
from jax.sharding import PartitionSpec as P

STEPS = 3
EPS = 1e-06
SHARES = (1, 2)
CROSS_PARTS = (1, 3)
TEXT_PARTS = 2
VMEM_BYTES = 24 * 1024 * 1024
BF16, F32 = jnp.bfloat16, jnp.float32


def spaces(count):
    return [pl.BlockSpec(memory_space=pltpu.VMEM)] * count


def params(size=VMEM_BYTES):
    return pltpu.CompilerParams(vmem_limit_bytes=size)


def cost():
    return pl.CostEstimate(flops=0, bytes_accessed=0, transcendentals=0)


IN_HBM = pl.BlockSpec(memory_space=pltpu.HBM)


def place():
    where = lax.axis_index("dp")
    return lax.axis_index("fsdp"), lax.rem(where, 2), lax.rem(lax.div(where, 2), 2)


def cut_kernel(short, own, whole, part, sem):
    _, core, column = place()
    half = whole.shape[0]
    first = pltpu.make_async_copy(
        own.at[pl.ds(pl.multiple_of(core * half, 16), half), :], whole, sem.at[0]
    )
    start = pl.multiple_of(core * half + column * (half - short), 16)
    second = pltpu.make_async_copy(own.at[pl.ds(start, short), :], part, sem.at[1])
    first.start()
    second.start()
    first.wait()
    second.wait()


def cut(short, own):
    half, width = own.shape[0] // 2, own.shape[1]
    outs = (
        jax.ShapeDtypeStruct((half, width), BF16),
        jax.ShapeDtypeStruct((short, width), BF16),
    )
    return pl.pallas_call(
        functools.partial(cut_kernel, short),
        out_shape=outs,
        in_specs=[IN_HBM],
        out_specs=spaces(2),
        scratch_shapes=[pltpu.SemaphoreType.DMA((2,))],
        compiler_params=params(),
        cost_estimate=cost(),
        name="cut",
    )(own)


def prepare_kernel(t0, twin0, t2, sharp, bias, *rest):
    twin2, (units, scalars) = rest[:TEXT_PARTS], rest[TEXT_PARTS:]
    rows = t0.shape[0]
    _, core, _ = place()
    scalars[0:1, :] = jnp.broadcast_to(sharp[...], (1, scalars.shape[1]))
    scalars[1:2, :] = jnp.broadcast_to(bias[...], (1, scalars.shape[1]))

    def fill(start, block):
        values = block[...].astype(F32)
        inverse = 1.0 / jnp.sqrt(jnp.sum(values * values, axis=-1, keepdims=True) + EPS)
        units[start : start + block.shape[0], :] = (values * inverse).astype(BF16)

    fill(0, t0)
    fill(2 * rows, t2)

    @pl.when(core == 0)
    def _():
        for k, block in enumerate(twin2):
            fill(rows + k * block.shape[0], block)

    pl.when(core == 1)(lambda: fill(rows, twin0))


def prepare(t0, twin0, t2, sharp, bias, twin2):
    rows, width = t0.shape
    return pl.pallas_call(
        prepare_kernel,
        out_shape=(
            jax.ShapeDtypeStruct((STEPS * rows, width), BF16),
            jax.ShapeDtypeStruct((8, 128), F32),
        ),
        in_specs=spaces(5 + TEXT_PARTS),
        out_specs=tuple(spaces(2)),
        compiler_params=params(),
        cost_estimate=cost(),
        name="prepare",
    )(t0, twin0, t2, sharp, bias, *twin2)


def turn_kernel(depth, x, x_t, outer_t):
    x_t[...] = x[...].T
    start = jnp.where(lax.axis_index("fsdp") == 0, depth, 0)
    outer_t[...] = x_t[pl.ds(pl.multiple_of(start, 16), outer_t.shape[0]), :]


def turned(depth, x):
    rows, width = x.shape
    return pl.pallas_call(
        functools.partial(turn_kernel, depth),
        out_shape=(
            jax.ShapeDtypeStruct((width, rows), BF16),
            jax.ShapeDtypeStruct((width - depth, rows), BF16),
        ),
        in_specs=spaces(1),
        out_specs=tuple(spaces(2)),
        compiler_params=params(),
        cost_estimate=cost(),
        name="turned",
    )(x)


def rows_of(ref, block, depth):
    return ref[pl.ds(pl.multiple_of(block * depth, 16), depth), :]


def weights(mine, others, scale, bias):
    product = lax.dot_general(
        mine, others, (((1,), (1,)), ((), ())), preferred_element_type=F32
    )
    coefficient = jax.nn.sigmoid(scale * product + bias)
    row = lax.broadcasted_iota(jnp.int32, coefficient.shape, 0)
    column = lax.broadcasted_iota(jnp.int32, coefficient.shape, 1)
    coefficient = jnp.where(row == column, coefficient - 1.0, coefficient).astype(BF16)
    return coefficient, scale * jnp.sum(coefficient.astype(F32) * product, axis=-1, keepdims=True)


def picture_kernel(x, x_t, units, scalars, own, *rest):
    pieces, outs = rest[:8], rest[8 : 8 + len(SHARES)]
    unit, grad, w, proj = rest[-4:]
    part, core, column = place()
    depth = own.shape[0]
    half = depth // 2
    short = pieces[2].shape[0]
    rest_rows = half - short
    rows = x.shape[0]
    w[pl.ds(pl.multiple_of(part * depth, 16), depth), :] = own[...]
    for twin in (0, 1):
        lane = core if twin == 0 else 1 - core
        plus, minus, two, two_crossed = pieces[4 * twin : 4 * twin + 4]
        for piece, from_part in ((plus, part + 3), (minus, part + 1)):
            start = pl.multiple_of(lax.rem(from_part, 4) * depth + lane * half, 16)
            w[pl.ds(start, half), :] = piece[...]
        base = lax.rem(part + 2, 4) * depth + lane * half
        start = pl.multiple_of(base + column * rest_rows, 16)
        w[pl.ds(start, short), :] = two[...]
        source = pl.multiple_of((1 - column) * (short - rest_rows), 16)
        start = pl.multiple_of(base + (1 - column) * short, 16)
        w[pl.ds(start, rest_rows), :] = two_crossed[pl.ds(source, rest_rows), :]

    proj[...] = jnp.dot(x[...], w[...], preferred_element_type=F32)
    values = proj[...]
    inverse = 1.0 / jnp.sqrt(jnp.sum(values * values, axis=-1, keepdims=True) + EPS)
    unit[...] = (values * inverse).astype(BF16)
    scale = scalars[0:1, 0:1]
    coefficient, along = weights(unit[...], units[...], scale, scalars[1:2, 0:1])
    slope = jnp.dot(coefficient, units[...], preferred_element_type=F32)
    grad[...] = (slope * (scale * inverse) - proj[...] * (along * inverse * inverse)).astype(BF16)
    inner = jnp.logical_or(part == 1, part == 2)

    @pl.when(inner)
    def _():
        block = rows_of(x_t, 3 * (part - 1), depth)
        begin = 0
        for out in outs:
            stop = begin + out.shape[1]
            out[...] = jnp.dot(block, grad[:, begin:stop], preferred_element_type=F32).astype(BF16)
            begin = stop

    @pl.when(jnp.logical_not(inner))
    def _():
        begin = 0
        for out in outs:
            stop = begin + out.shape[1]
            out[:rows, :] = grad[:, begin:stop]
            out[rows:, :] = jnp.zeros((depth - rows, stop - begin), BF16)
            begin = stop


def picture_side(x, x_t, units, scalars, own, pieces):
    rows, width = x.shape
    depth = own.shape[0]
    out = jax.ShapeDtypeStruct((rows, width), BF16)
    sizes = [width * share // sum(SHARES) for share in SHARES]
    outs = tuple(jax.ShapeDtypeStruct((depth, size), BF16) for size in sizes)
    outs = outs + (out, out)
    return pl.pallas_call(
        picture_kernel,
        out_shape=outs,
        in_specs=spaces(13),
        out_specs=spaces(len(outs)),
        scratch_shapes=[
            pltpu.VMEM((width, width), BF16),
            pltpu.VMEM((rows, width), F32),
        ],
        compiler_params=params(),
        cost_estimate=cost(),
        name="picture_side",
    )(x, x_t, units, scalars, own, *pieces)


def text_kernel(text, scalars, u0, u1, u2, out, done, units):
    rows = text.shape[0]
    done[...] = jnp.zeros_like(done)
    for k, block in enumerate((u0, u1, u2)):
        units[k * rows : (k + 1) * rows, :] = block[...]
    values = text[...].astype(F32)
    inverse = 1.0 / jnp.sqrt(jnp.sum(values * values, axis=-1, keepdims=True) + EPS)
    scale = scalars[0:1, 0:1]
    coefficient, along = weights(
        (values * inverse).astype(BF16), units[...], scale, scalars[1:2, 0:1]
    )
    slope = jnp.dot(coefficient, units[...], preferred_element_type=F32)
    out[...] = slope * (scale * inverse) - values * (along * inverse * inverse)


def text_side(text, scalars, u0, u1, u2):
    rows, width = text.shape
    return pl.pallas_call(
        text_kernel,
        out_shape=(jax.ShapeDtypeStruct((rows, width), F32), jax.ShapeDtypeStruct((8, 128), F32)),
        in_specs=spaces(5),
        out_specs=tuple(spaces(2)),
        scratch_shapes=[pltpu.VMEM((STEPS * rows, width), BF16)],
        compiler_params=params(),
        cost_estimate=cost(),
        name="text_side",
    )(text, scalars, u0, u1, u2)


def pair_kernel(begin, parts, x_t, far_t, grad, arrived, *rest):
    outs = rest[-1 - 2 * parts :]
    kept, fars, nears = outs[0], outs[1 : 1 + parts], outs[1 + parts :]
    rows = grad.shape[0]
    depth, size = arrived.shape
    part = lax.axis_index("fsdp")
    inner = jnp.logical_or(part == 1, part == 2)
    mine = grad[:, begin : begin + size]

    def product(block):
        return jnp.dot(rows_of(x_t, block, depth), mine, preferred_element_type=F32)

    @pl.when(inner)
    def _():
        other = arrived[:rows, :]
        first = jnp.where(part == 1, 1, 0)
        for block, out in ((3 - part, nears), (lax.rem(part + 2, 4), fars), (part, [kept])):
            both = product(block) + jnp.dot(
                rows_of(far_t, block - first, depth), other, preferred_element_type=F32
            )
            size = depth // len(out)
            for k, piece in enumerate(out):
                piece[...] = both[k * size : (k + 1) * size].astype(piece.dtype)

    @pl.when(jnp.logical_not(inner))
    def _():
        kept[...] = product(part) + arrived[...].astype(F32)
        for piece in nears + fars:
            piece[...] = jnp.zeros_like(piece)


def pair_product(begin, parts, x_t, far_t, grad, arrived, after):
    depth, size = arrived.shape
    piece = jax.ShapeDtypeStruct((depth // parts, size), BF16)
    outs = (jax.ShapeDtypeStruct((depth, size), F32),) + (piece,) * (2 * parts)
    return pl.pallas_call(
        functools.partial(pair_kernel, begin, parts),
        out_shape=outs,
        in_specs=spaces(4 + len(after)),
        out_specs=spaces(len(outs)),
        compiler_params=params(),
        cost_estimate=cost(),
        name="pair_product",
    )(x_t, far_t, grad, arrived, *after)


def total_kernel(begin, parts, kept, *rest):
    nears, fars, (out, summed, sem) = rest[:parts], rest[parts : 2 * parts], rest[-3:]
    size = kept.shape[0] // parts
    for k, (near, far) in enumerate(zip(nears, fars)):
        at = slice(k * size, (k + 1) * size)
        summed[at, :] = kept[at, :] + near[...].astype(F32) + far[...].astype(F32)
    copy = pltpu.make_async_copy(summed, out.at[0, :, begin : begin + kept.shape[1]], sem)
    copy.start()
    copy.wait()


def total(begin, width, kept, nears, fars, held):
    depth, parts = kept.shape[0], len(nears)
    return pl.pallas_call(
        functools.partial(total_kernel, begin, parts),
        out_shape=jax.ShapeDtypeStruct((1, depth, width), F32),
        in_specs=spaces(1 + 2 * parts) + [IN_HBM] * len(held[:1]) + spaces(len(held[1:])),
        out_specs=IN_HBM,
        scratch_shapes=[pltpu.VMEM(kept.shape, F32), pltpu.SemaphoreType.DMA],
        input_output_aliases={1 + 2 * parts: 0} if held else {},
        compiler_params=params(),
        cost_estimate=cost(),
        name="total",
    )(kept, *nears, *fars, *held)


def line_body(n_dp, n_fsdp, x, text, w, sharp, bias):
    depth, width = w.shape
    half = depth // 2
    short = (half // 2 + 15) // 16 * 16

    def along(value, pairs):
        return lax.ppermute(value, "fsdp", pairs)

    def across(value):
        return lax.ppermute(value, "dp", [(d, d ^ 1) for d in range(n_dp)])

    def shifted(value, by):
        return lax.ppermute(value, "dp", [(d, (d + by) % n_dp) for d in range(n_dp)])

    sharp, bias = sharp.reshape(1, 1), bias.reshape(1, 1)
    swap = [(0, 1), (1, 0), (2, 3), (3, 2)]
    whole, piece = cut(short, w)
    whole, piece, text = lax.optimization_barrier((whole, piece, text))
    two = along(piece, [(f, (f + 2) % n_fsdp) for f in range(n_fsdp)])
    plus = along(whole, [(f, (f + 1) % n_fsdp) for f in range(n_fsdp)])
    minus = along(whole, [(f, (f - 1) % n_fsdp) for f in range(n_fsdp)])
    text2 = shifted(text, 2)
    x_t, outer_t = turned(depth, x)
    two, outer_t, text2 = lax.optimization_barrier((two, outer_t, text2))
    two_crossed = lax.ppermute(two, "dp", [(d, d ^ 2) for d in range(n_dp)])
    far_t = along(outer_t, swap)
    size = text.shape[0] // TEXT_PARTS
    twin2 = [across(text2[k * size : (k + 1) * size]) for k in range(TEXT_PARTS)]
    units, scalars = prepare(text, across(text), text2, sharp, bias, twin2)
    plus, minus, units, scalars, x_t = lax.optimization_barrier((plus, minus, units, scalars, x_t))
    pieces = [plus, minus, two, two_crossed]
    pieces = pieces + [across(piece) for piece in pieces]
    results = picture_side(x, x_t, units, scalars, w, pieces)
    *outward, unit, grad = results
    grad, far_t = lax.optimization_barrier((grad, far_t))
    outward[0], far_t = lax.optimization_barrier((outward[0], far_t))

    arrived = []
    for block in outward:
        if arrived:
            block, arrived[-1] = lax.optimization_barrier((block, arrived[-1]))
        arrived.append(along(block, swap))
    unit1, unit2 = shifted(unit, -1), shifted(unit, -2)
    begin, terms, after = 0, [], []
    for parts, block in zip(CROSS_PARTS, arrived):
        kept, *sent = pair_product(begin, parts, x_t, far_t, grad, block, after)
        fars = [along(n, [(1, 3), (2, 0), (0, 1), (3, 2)]) for n in sent[:parts]]
        nears = [along(n, [(1, 2), (2, 1), (0, 0), (3, 3)]) for n in sent[parts:]]
        after = []
        terms.append((begin, width, kept, fars, nears))
        begin += block.shape[1]
    text_grad, done = text_side(text, scalars, unit, unit1, unit2)
    head = total(*terms[0], [])
    for term in terms[1:]:
        head = total(*term, [head, done])
    return head, text_grad


def plain_body(n_dp, n_fsdp, x, text, w, sharp, bias):
    def shifted(value, by):
        return lax.ppermute(value, "dp", [(d, (d + by) % n_dp) for d in range(n_dp)])

    rows, width = x.shape
    proj = jnp.dot(
        x, lax.all_gather(w, "fsdp", axis=0, tiled=True), preferred_element_type=F32
    )
    norm = jnp.sqrt(jnp.sum(proj * proj, axis=-1, keepdims=True) + EPS)
    direction = proj / norm
    unit = direction.astype(BF16)
    values = text.astype(F32)
    txt_norm = jnp.sqrt(jnp.sum(values * values, axis=-1, keepdims=True) + EPS)
    txt_dir = values / txt_norm
    slot = txt_dir.astype(BF16)
    scale = sharp[0]
    slope = jnp.zeros((rows, width), F32)
    txt_slope = jnp.zeros((rows, width), F32)
    for step in range(STEPS):
        if step > 0:
            slot = shifted(slot, 1)
        logits = scale * jnp.dot(unit, slot.T, preferred_element_type=F32) + bias[0]
        coefficient = jax.nn.sigmoid(logits)
        if step == 0:
            coefficient = coefficient - jnp.eye(rows, dtype=F32)
        coefficient = coefficient.astype(BF16)
        slope = slope + scale * jnp.dot(coefficient, slot, preferred_element_type=F32)
        share = scale * lax.dot_general(
            coefficient, unit, (((0,), (0,)), ((), ())), preferred_element_type=F32
        )
        if step > 0:
            share = shifted(share.astype(BF16), -step).astype(F32)
        txt_slope = txt_slope + share
    grad = (
        (slope - direction * jnp.sum(direction * slope, axis=-1, keepdims=True)) / norm
    ).astype(BF16)
    text_grad = (
        txt_slope - txt_dir * jnp.sum(txt_dir * txt_slope, axis=-1, keepdims=True)
    ) / txt_norm
    partial = lax.dot_general(
        x, grad, (((0,), (0,)), ((), ())), preferred_element_type=F32
    ).astype(BF16)
    head = lax.psum_scatter(partial, "fsdp", scatter_dimension=0, tiled=True).astype(F32)
    return head[None], text_grad


def solution(mesh):
    n_dp, n_fsdp = mesh.shape["dp"], mesh.shape["fsdp"]
    line = n_fsdp == 4 and n_dp % 4 == 0
    placed = (P(("dp", "fsdp"), None), P(("dp", "fsdp"), None), P("fsdp", None), P(), P())
    return jax.shard_map(
        functools.partial(line_body if line else plain_body, n_dp, n_fsdp),
        mesh=mesh,
        in_specs=placed,
        out_specs=(P("dp", "fsdp", None), P(("dp", "fsdp"), None)),
        check_vma=False,
    )
```

```python
import functools

import jax
import jax.numpy as jnp
from jax import lax
from jax.experimental import pallas as pl
from jax.experimental.pallas import tpu as pltpu
from jax.sharding import PartitionSpec as P

STEPS = 3
EPS = 1e-06
SHARES = (4, 5)
CROSS_PARTS = (1, 2)
TEXT_PARTS = 2
VMEM_BYTES = 24 * 1024 * 1024
BF16, F32 = jnp.bfloat16, jnp.float32


def spaces(count):
    return [pl.BlockSpec(memory_space=pltpu.VMEM)] * count


def params(size=VMEM_BYTES):
    return pltpu.CompilerParams(vmem_limit_bytes=size)


def cost():
    return pl.CostEstimate(flops=0, bytes_accessed=0, transcendentals=0)


IN_HBM = pl.BlockSpec(memory_space=pltpu.HBM)


def place():
    where = lax.axis_index("dp")
    return lax.axis_index("fsdp"), lax.rem(where, 2), lax.rem(lax.div(where, 2), 2)


def cut_kernel(short, own, whole, part, sem):
    _, core, column = place()
    half = whole.shape[0]
    first = pltpu.make_async_copy(
        own.at[pl.ds(pl.multiple_of(core * half, 16), half), :], whole, sem.at[0]
    )
    start = pl.multiple_of(core * half + column * (half - short), 16)
    second = pltpu.make_async_copy(own.at[pl.ds(start, short), :], part, sem.at[1])
    first.start()
    second.start()
    first.wait()
    second.wait()


def cut(short, own):
    half, width = own.shape[0] // 2, own.shape[1]
    outs = (
        jax.ShapeDtypeStruct((half, width), BF16),
        jax.ShapeDtypeStruct((short, width), BF16),
    )
    return pl.pallas_call(
        functools.partial(cut_kernel, short),
        out_shape=outs,
        in_specs=[IN_HBM],
        out_specs=spaces(2),
        scratch_shapes=[pltpu.SemaphoreType.DMA((2,))],
        compiler_params=params(),
        cost_estimate=cost(),
        name="cut",
    )(own)


def prepare_kernel(t0, twin0, t2, sharp, bias, *rest):
    twin2, (units, scalars) = rest[:TEXT_PARTS], rest[TEXT_PARTS:]
    rows = t0.shape[0]
    _, core, _ = place()
    scalars[0:1, :] = jnp.broadcast_to(sharp[...], (1, scalars.shape[1]))
    scalars[1:2, :] = jnp.broadcast_to(bias[...], (1, scalars.shape[1]))

    def fill(start, block):
        values = block[...].astype(F32)
        inverse = 1.0 / jnp.sqrt(jnp.sum(values * values, axis=-1, keepdims=True) + EPS)
        units[start : start + block.shape[0], :] = (values * inverse).astype(BF16)

    fill(0, t0)
    fill(2 * rows, t2)

    @pl.when(core == 0)
    def _():
        for k, block in enumerate(twin2):
            fill(rows + k * block.shape[0], block)

    pl.when(core == 1)(lambda: fill(rows, twin0))


def prepare(t0, twin0, t2, sharp, bias, twin2):
    rows, width = t0.shape
    return pl.pallas_call(
        prepare_kernel,
        out_shape=(
            jax.ShapeDtypeStruct((STEPS * rows, width), BF16),
            jax.ShapeDtypeStruct((8, 128), F32),
        ),
        in_specs=spaces(5 + TEXT_PARTS),
        out_specs=tuple(spaces(2)),
        compiler_params=params(),
        cost_estimate=cost(),
        name="prepare",
    )(t0, twin0, t2, sharp, bias, *twin2)


def turn_kernel(depth, x, x_t, outer_t):
    x_t[...] = x[...].T
    start = jnp.where(lax.axis_index("fsdp") == 0, depth, 0)
    outer_t[...] = x_t[pl.ds(pl.multiple_of(start, 16), outer_t.shape[0]), :]


def turned(depth, x):
    rows, width = x.shape
    return pl.pallas_call(
        functools.partial(turn_kernel, depth),
        out_shape=(
            jax.ShapeDtypeStruct((width, rows), BF16),
            jax.ShapeDtypeStruct((width - depth, rows), BF16),
        ),
        in_specs=spaces(1),
        out_specs=tuple(spaces(2)),
        compiler_params=params(),
        cost_estimate=cost(),
        name="turned",
    )(x)


def rows_of(ref, block, depth):
    return ref[pl.ds(pl.multiple_of(block * depth, 16), depth), :]


def weights(mine, others, scale, bias):
    product = lax.dot_general(
        mine, others, (((1,), (1,)), ((), ())), preferred_element_type=F32
    )
    coefficient = jax.nn.sigmoid(scale * product + bias)
    row = lax.broadcasted_iota(jnp.int32, coefficient.shape, 0)
    column = lax.broadcasted_iota(jnp.int32, coefficient.shape, 1)
    coefficient = jnp.where(row == column, coefficient - 1.0, coefficient).astype(BF16)
    return coefficient, scale * jnp.sum(coefficient.astype(F32) * product, axis=-1, keepdims=True)


def picture_kernel(x, x_t, units, scalars, own, *rest):
    pieces, outs = rest[:8], rest[8 : 8 + len(SHARES)]
    unit, grad, w, proj = rest[-4:]
    part, core, column = place()
    depth = own.shape[0]
    half = depth // 2
    short = pieces[2].shape[0]
    rest_rows = half - short
    rows = x.shape[0]
    w[pl.ds(pl.multiple_of(part * depth, 16), depth), :] = own[...]
    for twin in (0, 1):
        lane = core if twin == 0 else 1 - core
        plus, minus, two, two_crossed = pieces[4 * twin : 4 * twin + 4]
        for piece, from_part in ((plus, part + 3), (minus, part + 1)):
            start = pl.multiple_of(lax.rem(from_part, 4) * depth + lane * half, 16)
            w[pl.ds(start, half), :] = piece[...]
        base = lax.rem(part + 2, 4) * depth + lane * half
        start = pl.multiple_of(base + column * rest_rows, 16)
        w[pl.ds(start, short), :] = two[...]
        source = pl.multiple_of((1 - column) * (short - rest_rows), 16)
        start = pl.multiple_of(base + (1 - column) * short, 16)
        w[pl.ds(start, rest_rows), :] = two_crossed[pl.ds(source, rest_rows), :]

    proj[...] = jnp.dot(x[...], w[...], preferred_element_type=F32)
    values = proj[...]
    inverse = 1.0 / jnp.sqrt(jnp.sum(values * values, axis=-1, keepdims=True) + EPS)
    unit[...] = (values * inverse).astype(BF16)
    scale = scalars[0:1, 0:1]
    coefficient, along = weights(unit[...], units[...], scale, scalars[1:2, 0:1])
    slope = jnp.dot(coefficient, units[...], preferred_element_type=F32)
    grad[...] = (slope * (scale * inverse) - proj[...] * (along * inverse * inverse)).astype(BF16)
    inner = jnp.logical_or(part == 1, part == 2)

    @pl.when(inner)
    def _():
        block = rows_of(x_t, 3 * (part - 1), depth)
        begin = 0
        for out in outs:
            stop = begin + out.shape[1]
            out[...] = jnp.dot(block, grad[:, begin:stop], preferred_element_type=F32).astype(BF16)
            begin = stop

    @pl.when(jnp.logical_not(inner))
    def _():
        begin = 0
        for out in outs:
            stop = begin + out.shape[1]
            out[:rows, :] = grad[:, begin:stop]
            out[rows:, :] = jnp.zeros((depth - rows, stop - begin), BF16)
            begin = stop


def picture_side(x, x_t, units, scalars, own, pieces):
    rows, width = x.shape
    depth = own.shape[0]
    out = jax.ShapeDtypeStruct((rows, width), BF16)
    sizes = [width * share // sum(SHARES) for share in SHARES]
    outs = tuple(jax.ShapeDtypeStruct((depth, size), BF16) for size in sizes)
    outs = outs + (out, out)
    return pl.pallas_call(
        picture_kernel,
        out_shape=outs,
        in_specs=spaces(13),
        out_specs=spaces(len(outs)),
        scratch_shapes=[
            pltpu.VMEM((width, width), BF16),
            pltpu.VMEM((rows, width), F32),
        ],
        compiler_params=params(),
        cost_estimate=cost(),
        name="picture_side",
    )(x, x_t, units, scalars, own, *pieces)


def text_kernel(text, scalars, u0, u1, u2, out, done, units):
    rows = text.shape[0]
    done[...] = jnp.zeros_like(done)
    for k, block in enumerate((u0, u1, u2)):
        units[k * rows : (k + 1) * rows, :] = block[...]
    values = text[...].astype(F32)
    inverse = 1.0 / jnp.sqrt(jnp.sum(values * values, axis=-1, keepdims=True) + EPS)
    scale = scalars[0:1, 0:1]
    coefficient, along = weights(
        (values * inverse).astype(BF16), units[...], scale, scalars[1:2, 0:1]
    )
    slope = jnp.dot(coefficient, units[...], preferred_element_type=F32)
    out[...] = slope * (scale * inverse) - values * (along * inverse * inverse)


def text_side(text, scalars, u0, u1, u2):
    rows, width = text.shape
    return pl.pallas_call(
        text_kernel,
        out_shape=(jax.ShapeDtypeStruct((rows, width), F32), jax.ShapeDtypeStruct((8, 128), F32)),
        in_specs=spaces(5),
        out_specs=tuple(spaces(2)),
        scratch_shapes=[pltpu.VMEM((STEPS * rows, width), BF16)],
        compiler_params=params(),
        cost_estimate=cost(),
        name="text_side",
    )(text, scalars, u0, u1, u2)


def pair_kernel(begin, parts, x_t, far_t, grad, arrived, *rest):
    outs = rest[-1 - 2 * parts :]
    kept, fars, nears = outs[0], outs[1 : 1 + parts], outs[1 + parts :]
    rows = grad.shape[0]
    depth, size = arrived.shape
    part = lax.axis_index("fsdp")
    inner = jnp.logical_or(part == 1, part == 2)
    mine = grad[:, begin : begin + size]

    def product(block):
        return jnp.dot(rows_of(x_t, block, depth), mine, preferred_element_type=F32)

    @pl.when(inner)
    def _():
        other = arrived[:rows, :]
        first = jnp.where(part == 1, 1, 0)
        for block, out in ((3 - part, nears), (lax.rem(part + 2, 4), fars), (part, [kept])):
            both = product(block) + jnp.dot(
                rows_of(far_t, block - first, depth), other, preferred_element_type=F32
            )
            size = depth // len(out)
            for k, piece in enumerate(out):
                piece[...] = both[k * size : (k + 1) * size].astype(piece.dtype)

    @pl.when(jnp.logical_not(inner))
    def _():
        kept[...] = product(part) + arrived[...].astype(F32)
        for piece in nears + fars:
            piece[...] = jnp.zeros_like(piece)


def pair_product(begin, parts, x_t, far_t, grad, arrived, after):
    depth, size = arrived.shape
    piece = jax.ShapeDtypeStruct((depth // parts, size), BF16)
    outs = (jax.ShapeDtypeStruct((depth, size), F32),) + (piece,) * (2 * parts)
    return pl.pallas_call(
        functools.partial(pair_kernel, begin, parts),
        out_shape=outs,
        in_specs=spaces(4 + len(after)),
        out_specs=spaces(len(outs)),
        compiler_params=params(),
        cost_estimate=cost(),
        name="pair_product",
    )(x_t, far_t, grad, arrived, *after)


def total_kernel(begin, parts, kept, *rest):
    nears, fars, (out, summed, sem) = rest[:parts], rest[parts : 2 * parts], rest[-3:]
    size = kept.shape[0] // parts
    for k, (near, far) in enumerate(zip(nears, fars)):
        at = slice(k * size, (k + 1) * size)
        summed[at, :] = kept[at, :] + near[...].astype(F32) + far[...].astype(F32)
    copy = pltpu.make_async_copy(summed, out.at[0, :, begin : begin + kept.shape[1]], sem)
    copy.start()
    copy.wait()


def total(begin, width, kept, nears, fars, held):
    depth, parts = kept.shape[0], len(nears)
    return pl.pallas_call(
        functools.partial(total_kernel, begin, parts),
        out_shape=jax.ShapeDtypeStruct((1, depth, width), F32),
        in_specs=spaces(1 + 2 * parts) + [IN_HBM] * len(held[:1]) + spaces(len(held[1:])),
        out_specs=IN_HBM,
        scratch_shapes=[pltpu.VMEM(kept.shape, F32), pltpu.SemaphoreType.DMA],
        input_output_aliases={1 + 2 * parts: 0} if held else {},
        compiler_params=params(),
        cost_estimate=cost(),
        name="total",
    )(kept, *nears, *fars, *held)


def line_body(n_dp, n_fsdp, x, text, w, sharp, bias):
    depth, width = w.shape
    half = depth // 2
    short = (half // 2 + 15) // 16 * 16

    def along(value, pairs):
        return lax.ppermute(value, "fsdp", pairs)

    def across(value):
        return lax.ppermute(value, "dp", [(d, d ^ 1) for d in range(n_dp)])

    def shifted(value, by):
        return lax.ppermute(value, "dp", [(d, (d + by) % n_dp) for d in range(n_dp)])

    sharp, bias = sharp.reshape(1, 1), bias.reshape(1, 1)
    swap = [(0, 1), (1, 0), (2, 3), (3, 2)]
    whole, piece = cut(short, w)
    whole, piece, text = lax.optimization_barrier((whole, piece, text))
    two = along(piece, [(f, (f + 2) % n_fsdp) for f in range(n_fsdp)])
    plus = along(whole, [(f, (f + 1) % n_fsdp) for f in range(n_fsdp)])
    minus = along(whole, [(f, (f - 1) % n_fsdp) for f in range(n_fsdp)])
    text2 = shifted(text, 2)
    x_t, outer_t = turned(depth, x)
    two, outer_t, text2 = lax.optimization_barrier((two, outer_t, text2))
    two_crossed = lax.ppermute(two, "dp", [(d, d ^ 2) for d in range(n_dp)])
    far_t = along(outer_t, swap)
    size = text.shape[0] // TEXT_PARTS
    twin2 = [across(text2[k * size : (k + 1) * size]) for k in range(TEXT_PARTS)]
    units, scalars = prepare(text, across(text), text2, sharp, bias, twin2)
    plus, minus, units, scalars, x_t = lax.optimization_barrier((plus, minus, units, scalars, x_t))
    pieces = [plus, minus, two, two_crossed]
    pieces = pieces + [across(piece) for piece in pieces]
    results = picture_side(x, x_t, units, scalars, w, pieces)
    *outward, unit, grad = results
    grad, far_t = lax.optimization_barrier((grad, far_t))
    outward[0], far_t = lax.optimization_barrier((outward[0], far_t))

    arrived = []
    for block in outward:
        if arrived:
            block, arrived[-1] = lax.optimization_barrier((block, arrived[-1]))
        arrived.append(along(block, swap))
    unit1, unit2 = shifted(unit, -1), shifted(unit, -2)
    begin, terms, after = 0, [], []
    for parts, block in zip(CROSS_PARTS, arrived):
        kept, *sent = pair_product(begin, parts, x_t, far_t, grad, block, after)
        fars = [along(n, [(1, 3), (2, 0), (0, 1), (3, 2)]) for n in sent[:parts]]
        nears = [along(n, [(1, 2), (2, 1), (0, 0), (3, 3)]) for n in sent[parts:]]
        after = []
        terms.append((begin, width, kept, fars, nears))
        begin += block.shape[1]
    text_grad, done = text_side(text, scalars, unit, unit1, unit2)
    head = total(*terms[0], [])
    for term in terms[1:]:
        head = total(*term, [head, done])
    return head, text_grad


def plain_body(n_dp, n_fsdp, x, text, w, sharp, bias):
    def shifted(value, by):
        return lax.ppermute(value, "dp", [(d, (d + by) % n_dp) for d in range(n_dp)])

    rows, width = x.shape
    proj = jnp.dot(
        x, lax.all_gather(w, "fsdp", axis=0, tiled=True), preferred_element_type=F32
    )
    norm = jnp.sqrt(jnp.sum(proj * proj, axis=-1, keepdims=True) + EPS)
    direction = proj / norm
    unit = direction.astype(BF16)
    values = text.astype(F32)
    txt_norm = jnp.sqrt(jnp.sum(values * values, axis=-1, keepdims=True) + EPS)
    txt_dir = values / txt_norm
    slot = txt_dir.astype(BF16)
    scale = sharp[0]
    slope = jnp.zeros((rows, width), F32)
    txt_slope = jnp.zeros((rows, width), F32)
    for step in range(STEPS):
        if step > 0:
            slot = shifted(slot, 1)
        logits = scale * jnp.dot(unit, slot.T, preferred_element_type=F32) + bias[0]
        coefficient = jax.nn.sigmoid(logits)
        if step == 0:
            coefficient = coefficient - jnp.eye(rows, dtype=F32)
        coefficient = coefficient.astype(BF16)
        slope = slope + scale * jnp.dot(coefficient, slot, preferred_element_type=F32)
        share = scale * lax.dot_general(
            coefficient, unit, (((0,), (0,)), ((), ())), preferred_element_type=F32
        )
        if step > 0:
            share = shifted(share.astype(BF16), -step).astype(F32)
        txt_slope = txt_slope + share
    grad = (
        (slope - direction * jnp.sum(direction * slope, axis=-1, keepdims=True)) / norm
    ).astype(BF16)
    text_grad = (
        txt_slope - txt_dir * jnp.sum(txt_dir * txt_slope, axis=-1, keepdims=True)
    ) / txt_norm
    partial = lax.dot_general(
        x, grad, (((0,), (0,)), ((), ())), preferred_element_type=F32
    ).astype(BF16)
    head = lax.psum_scatter(partial, "fsdp", scatter_dimension=0, tiled=True).astype(F32)
    return head[None], text_grad


def solution(mesh):
    n_dp, n_fsdp = mesh.shape["dp"], mesh.shape["fsdp"]
    line = n_fsdp == 4 and n_dp % 4 == 0
    placed = (P(("dp", "fsdp"), None), P(("dp", "fsdp"), None), P("fsdp", None), P(), P())
    return jax.shard_map(
        functools.partial(line_body if line else plain_body, n_dp, n_fsdp),
        mesh=mesh,
        in_specs=placed,
        out_specs=(P("dp", "fsdp", None), P(("dp", "fsdp"), None)),
        check_vma=False,
    )
```

```python
import functools

import jax
import jax.numpy as jnp
from jax import lax
from jax.experimental import pallas as pl
from jax.experimental.pallas import tpu as pltpu
from jax.sharding import PartitionSpec as P

STEPS = 3
EPS = 1e-06
SHARES = (5, 4)
CROSS_PARTS = (1, 2)
TEXT_PARTS = 2
VMEM_BYTES = 24 * 1024 * 1024
BF16, F32 = jnp.bfloat16, jnp.float32


def spaces(count):
    return [pl.BlockSpec(memory_space=pltpu.VMEM)] * count


def params(size=VMEM_BYTES):
    return pltpu.CompilerParams(vmem_limit_bytes=size)


def cost():
    return pl.CostEstimate(flops=0, bytes_accessed=0, transcendentals=0)


IN_HBM = pl.BlockSpec(memory_space=pltpu.HBM)


def place():
    where = lax.axis_index("dp")
    return lax.axis_index("fsdp"), lax.rem(where, 2), lax.rem(lax.div(where, 2), 2)


def cut_kernel(short, own, whole, part, sem):
    _, core, column = place()
    half = whole.shape[0]
    first = pltpu.make_async_copy(
        own.at[pl.ds(pl.multiple_of(core * half, 16), half), :], whole, sem.at[0]
    )
    start = pl.multiple_of(core * half + column * (half - short), 16)
    second = pltpu.make_async_copy(own.at[pl.ds(start, short), :], part, sem.at[1])
    first.start()
    second.start()
    first.wait()
    second.wait()


def cut(short, own):
    half, width = own.shape[0] // 2, own.shape[1]
    outs = (
        jax.ShapeDtypeStruct((half, width), BF16),
        jax.ShapeDtypeStruct((short, width), BF16),
    )
    return pl.pallas_call(
        functools.partial(cut_kernel, short),
        out_shape=outs,
        in_specs=[IN_HBM],
        out_specs=spaces(2),
        scratch_shapes=[pltpu.SemaphoreType.DMA((2,))],
        compiler_params=params(),
        cost_estimate=cost(),
        name="cut",
    )(own)


def prepare_kernel(t0, twin0, t2, sharp, bias, *rest):
    twin2, (units, scalars) = rest[:TEXT_PARTS], rest[TEXT_PARTS:]
    rows = t0.shape[0]
    _, core, _ = place()
    scalars[0:1, :] = jnp.broadcast_to(sharp[...], (1, scalars.shape[1]))
    scalars[1:2, :] = jnp.broadcast_to(bias[...], (1, scalars.shape[1]))

    def fill(start, block):
        values = block[...].astype(F32)
        inverse = 1.0 / jnp.sqrt(jnp.sum(values * values, axis=-1, keepdims=True) + EPS)
        units[start : start + block.shape[0], :] = (values * inverse).astype(BF16)

    fill(0, t0)
    fill(2 * rows, t2)

    @pl.when(core == 0)
    def _():
        for k, block in enumerate(twin2):
            fill(rows + k * block.shape[0], block)

    pl.when(core == 1)(lambda: fill(rows, twin0))


def prepare(t0, twin0, t2, sharp, bias, twin2):
    rows, width = t0.shape
    return pl.pallas_call(
        prepare_kernel,
        out_shape=(
            jax.ShapeDtypeStruct((STEPS * rows, width), BF16),
            jax.ShapeDtypeStruct((8, 128), F32),
        ),
        in_specs=spaces(5 + TEXT_PARTS),
        out_specs=tuple(spaces(2)),
        compiler_params=params(),
        cost_estimate=cost(),
        name="prepare",
    )(t0, twin0, t2, sharp, bias, *twin2)


def turn_kernel(depth, x, x_t, outer_t):
    x_t[...] = x[...].T
    start = jnp.where(lax.axis_index("fsdp") == 0, depth, 0)
    outer_t[...] = x_t[pl.ds(pl.multiple_of(start, 16), outer_t.shape[0]), :]


def turned(depth, x):
    rows, width = x.shape
    return pl.pallas_call(
        functools.partial(turn_kernel, depth),
        out_shape=(
            jax.ShapeDtypeStruct((width, rows), BF16),
            jax.ShapeDtypeStruct((width - depth, rows), BF16),
        ),
        in_specs=spaces(1),
        out_specs=tuple(spaces(2)),
        compiler_params=params(),
        cost_estimate=cost(),
        name="turned",
    )(x)


def rows_of(ref, block, depth):
    return ref[pl.ds(pl.multiple_of(block * depth, 16), depth), :]


def weights(mine, others, scale, bias):
    product = lax.dot_general(
        mine, others, (((1,), (1,)), ((), ())), preferred_element_type=F32
    )
    coefficient = jax.nn.sigmoid(scale * product + bias)
    row = lax.broadcasted_iota(jnp.int32, coefficient.shape, 0)
    column = lax.broadcasted_iota(jnp.int32, coefficient.shape, 1)
    coefficient = jnp.where(row == column, coefficient - 1.0, coefficient).astype(BF16)
    return coefficient, scale * jnp.sum(coefficient.astype(F32) * product, axis=-1, keepdims=True)


def picture_kernel(x, x_t, units, scalars, own, *rest):
    pieces, outs = rest[:8], rest[8 : 8 + len(SHARES)]
    unit, grad, w, proj = rest[-4:]
    part, core, column = place()
    depth = own.shape[0]
    half = depth // 2
    short = pieces[2].shape[0]
    rest_rows = half - short
    rows = x.shape[0]
    w[pl.ds(pl.multiple_of(part * depth, 16), depth), :] = own[...]
    for twin in (0, 1):
        lane = core if twin == 0 else 1 - core
        plus, minus, two, two_crossed = pieces[4 * twin : 4 * twin + 4]
        for piece, from_part in ((plus, part + 3), (minus, part + 1)):
            start = pl.multiple_of(lax.rem(from_part, 4) * depth + lane * half, 16)
            w[pl.ds(start, half), :] = piece[...]
        base = lax.rem(part + 2, 4) * depth + lane * half
        start = pl.multiple_of(base + column * rest_rows, 16)
        w[pl.ds(start, short), :] = two[...]
        source = pl.multiple_of((1 - column) * (short - rest_rows), 16)
        start = pl.multiple_of(base + (1 - column) * short, 16)
        w[pl.ds(start, rest_rows), :] = two_crossed[pl.ds(source, rest_rows), :]

    proj[...] = jnp.dot(x[...], w[...], preferred_element_type=F32)
    values = proj[...]
    inverse = 1.0 / jnp.sqrt(jnp.sum(values * values, axis=-1, keepdims=True) + EPS)
    unit[...] = (values * inverse).astype(BF16)
    scale = scalars[0:1, 0:1]
    coefficient, along = weights(unit[...], units[...], scale, scalars[1:2, 0:1])
    slope = jnp.dot(coefficient, units[...], preferred_element_type=F32)
    grad[...] = (slope * (scale * inverse) - proj[...] * (along * inverse * inverse)).astype(BF16)
    inner = jnp.logical_or(part == 1, part == 2)

    @pl.when(inner)
    def _():
        block = rows_of(x_t, 3 * (part - 1), depth)
        begin = 0
        for out in outs:
            stop = begin + out.shape[1]
            out[...] = jnp.dot(block, grad[:, begin:stop], preferred_element_type=F32).astype(BF16)
            begin = stop

    @pl.when(jnp.logical_not(inner))
    def _():
        begin = 0
        for out in outs:
            stop = begin + out.shape[1]
            out[:rows, :] = grad[:, begin:stop]
            out[rows:, :] = jnp.zeros((depth - rows, stop - begin), BF16)
            begin = stop


def picture_side(x, x_t, units, scalars, own, pieces):
    rows, width = x.shape
    depth = own.shape[0]
    out = jax.ShapeDtypeStruct((rows, width), BF16)
    sizes = [width * share // sum(SHARES) for share in SHARES]
    outs = tuple(jax.ShapeDtypeStruct((depth, size), BF16) for size in sizes)
    outs = outs + (out, out)
    return pl.pallas_call(
        picture_kernel,
        out_shape=outs,
        in_specs=spaces(13),
        out_specs=spaces(len(outs)),
        scratch_shapes=[
            pltpu.VMEM((width, width), BF16),
            pltpu.VMEM((rows, width), F32),
        ],
        compiler_params=params(),
        cost_estimate=cost(),
        name="picture_side",
    )(x, x_t, units, scalars, own, *pieces)


def text_kernel(text, scalars, u0, u1, u2, out, done, units):
    rows = text.shape[0]
    done[...] = jnp.zeros_like(done)
    for k, block in enumerate((u0, u1, u2)):
        units[k * rows : (k + 1) * rows, :] = block[...]
    values = text[...].astype(F32)
    inverse = 1.0 / jnp.sqrt(jnp.sum(values * values, axis=-1, keepdims=True) + EPS)
    scale = scalars[0:1, 0:1]
    coefficient, along = weights(
        (values * inverse).astype(BF16), units[...], scale, scalars[1:2, 0:1]
    )
    slope = jnp.dot(coefficient, units[...], preferred_element_type=F32)
    out[...] = slope * (scale * inverse) - values * (along * inverse * inverse)


def text_side(text, scalars, u0, u1, u2):
    rows, width = text.shape
    return pl.pallas_call(
        text_kernel,
        out_shape=(jax.ShapeDtypeStruct((rows, width), F32), jax.ShapeDtypeStruct((8, 128), F32)),
        in_specs=spaces(5),
        out_specs=tuple(spaces(2)),
        scratch_shapes=[pltpu.VMEM((STEPS * rows, width), BF16)],
        compiler_params=params(),
        cost_estimate=cost(),
        name="text_side",
    )(text, scalars, u0, u1, u2)


def pair_kernel(begin, parts, x_t, far_t, grad, arrived, *rest):
    outs = rest[-1 - 2 * parts :]
    kept, fars, nears = outs[0], outs[1 : 1 + parts], outs[1 + parts :]
    rows = grad.shape[0]
    depth, size = arrived.shape
    part = lax.axis_index("fsdp")
    inner = jnp.logical_or(part == 1, part == 2)
    mine = grad[:, begin : begin + size]

    def product(block):
        return jnp.dot(rows_of(x_t, block, depth), mine, preferred_element_type=F32)

    @pl.when(inner)
    def _():
        other = arrived[:rows, :]
        first = jnp.where(part == 1, 1, 0)
        for block, out in ((3 - part, nears), (lax.rem(part + 2, 4), fars), (part, [kept])):
            both = product(block) + jnp.dot(
                rows_of(far_t, block - first, depth), other, preferred_element_type=F32
            )
            size = depth // len(out)
            for k, piece in enumerate(out):
                piece[...] = both[k * size : (k + 1) * size].astype(piece.dtype)

    @pl.when(jnp.logical_not(inner))
    def _():
        kept[...] = product(part) + arrived[...].astype(F32)
        for piece in nears + fars:
            piece[...] = jnp.zeros_like(piece)


def pair_product(begin, parts, x_t, far_t, grad, arrived, after):
    depth, size = arrived.shape
    piece = jax.ShapeDtypeStruct((depth // parts, size), BF16)
    outs = (jax.ShapeDtypeStruct((depth, size), F32),) + (piece,) * (2 * parts)
    return pl.pallas_call(
        functools.partial(pair_kernel, begin, parts),
        out_shape=outs,
        in_specs=spaces(4 + len(after)),
        out_specs=spaces(len(outs)),
        compiler_params=params(),
        cost_estimate=cost(),
        name="pair_product",
    )(x_t, far_t, grad, arrived, *after)


def total_kernel(begin, parts, kept, *rest):
    nears, fars, (out, summed, sem) = rest[:parts], rest[parts : 2 * parts], rest[-3:]
    size = kept.shape[0] // parts
    for k, (near, far) in enumerate(zip(nears, fars)):
        at = slice(k * size, (k + 1) * size)
        summed[at, :] = kept[at, :] + near[...].astype(F32) + far[...].astype(F32)
    copy = pltpu.make_async_copy(summed, out.at[0, :, begin : begin + kept.shape[1]], sem)
    copy.start()
    copy.wait()


def total(begin, width, kept, nears, fars, held):
    depth, parts = kept.shape[0], len(nears)
    return pl.pallas_call(
        functools.partial(total_kernel, begin, parts),
        out_shape=jax.ShapeDtypeStruct((1, depth, width), F32),
        in_specs=spaces(1 + 2 * parts) + [IN_HBM] * len(held[:1]) + spaces(len(held[1:])),
        out_specs=IN_HBM,
        scratch_shapes=[pltpu.VMEM(kept.shape, F32), pltpu.SemaphoreType.DMA],
        input_output_aliases={1 + 2 * parts: 0} if held else {},
        compiler_params=params(),
        cost_estimate=cost(),
        name="total",
    )(kept, *nears, *fars, *held)


def line_body(n_dp, n_fsdp, x, text, w, sharp, bias):
    depth, width = w.shape
    half = depth // 2
    short = (half // 2 + 15) // 16 * 16

    def along(value, pairs):
        return lax.ppermute(value, "fsdp", pairs)

    def across(value):
        return lax.ppermute(value, "dp", [(d, d ^ 1) for d in range(n_dp)])

    def shifted(value, by):
        return lax.ppermute(value, "dp", [(d, (d + by) % n_dp) for d in range(n_dp)])

    sharp, bias = sharp.reshape(1, 1), bias.reshape(1, 1)
    swap = [(0, 1), (1, 0), (2, 3), (3, 2)]
    whole, piece = cut(short, w)
    whole, piece, text = lax.optimization_barrier((whole, piece, text))
    two = along(piece, [(f, (f + 2) % n_fsdp) for f in range(n_fsdp)])
    plus = along(whole, [(f, (f + 1) % n_fsdp) for f in range(n_fsdp)])
    minus = along(whole, [(f, (f - 1) % n_fsdp) for f in range(n_fsdp)])
    text2 = shifted(text, 2)
    x_t, outer_t = turned(depth, x)
    two, outer_t, text2 = lax.optimization_barrier((two, outer_t, text2))
    two_crossed = lax.ppermute(two, "dp", [(d, d ^ 2) for d in range(n_dp)])
    far_t = along(outer_t, swap)
    size = text.shape[0] // TEXT_PARTS
    twin2 = [across(text2[k * size : (k + 1) * size]) for k in range(TEXT_PARTS)]
    units, scalars = prepare(text, across(text), text2, sharp, bias, twin2)
    plus, minus, units, scalars, x_t = lax.optimization_barrier((plus, minus, units, scalars, x_t))
    pieces = [plus, minus, two, two_crossed]
    pieces = pieces + [across(piece) for piece in pieces]
    results = picture_side(x, x_t, units, scalars, w, pieces)
    *outward, unit, grad = results
    grad, far_t = lax.optimization_barrier((grad, far_t))
    outward[0], far_t = lax.optimization_barrier((outward[0], far_t))

    arrived = []
    for block in outward:
        if arrived:
            block, arrived[-1] = lax.optimization_barrier((block, arrived[-1]))
        arrived.append(along(block, swap))
    unit1, unit2 = shifted(unit, -1), shifted(unit, -2)
    begin, terms, after = 0, [], []
    for parts, block in zip(CROSS_PARTS, arrived):
        kept, *sent = pair_product(begin, parts, x_t, far_t, grad, block, after)
        fars = [along(n, [(1, 3), (2, 0), (0, 1), (3, 2)]) for n in sent[:parts]]
        nears = [along(n, [(1, 2), (2, 1), (0, 0), (3, 3)]) for n in sent[parts:]]
        after = []
        terms.append((begin, width, kept, fars, nears))
        begin += block.shape[1]
    text_grad, done = text_side(text, scalars, unit, unit1, unit2)
    head = total(*terms[0], [])
    for term in terms[1:]:
        head = total(*term, [head, done])
    return head, text_grad


def plain_body(n_dp, n_fsdp, x, text, w, sharp, bias):
    def shifted(value, by):
        return lax.ppermute(value, "dp", [(d, (d + by) % n_dp) for d in range(n_dp)])

    rows, width = x.shape
    proj = jnp.dot(
        x, lax.all_gather(w, "fsdp", axis=0, tiled=True), preferred_element_type=F32
    )
    norm = jnp.sqrt(jnp.sum(proj * proj, axis=-1, keepdims=True) + EPS)
    direction = proj / norm
    unit = direction.astype(BF16)
    values = text.astype(F32)
    txt_norm = jnp.sqrt(jnp.sum(values * values, axis=-1, keepdims=True) + EPS)
    txt_dir = values / txt_norm
    slot = txt_dir.astype(BF16)
    scale = sharp[0]
    slope = jnp.zeros((rows, width), F32)
    txt_slope = jnp.zeros((rows, width), F32)
    for step in range(STEPS):
        if step > 0:
            slot = shifted(slot, 1)
        logits = scale * jnp.dot(unit, slot.T, preferred_element_type=F32) + bias[0]
        coefficient = jax.nn.sigmoid(logits)
        if step == 0:
            coefficient = coefficient - jnp.eye(rows, dtype=F32)
        coefficient = coefficient.astype(BF16)
        slope = slope + scale * jnp.dot(coefficient, slot, preferred_element_type=F32)
        share = scale * lax.dot_general(
            coefficient, unit, (((0,), (0,)), ((), ())), preferred_element_type=F32
        )
        if step > 0:
            share = shifted(share.astype(BF16), -step).astype(F32)
        txt_slope = txt_slope + share
    grad = (
        (slope - direction * jnp.sum(direction * slope, axis=-1, keepdims=True)) / norm
    ).astype(BF16)
    text_grad = (
        txt_slope - txt_dir * jnp.sum(txt_dir * txt_slope, axis=-1, keepdims=True)
    ) / txt_norm
    partial = lax.dot_general(
        x, grad, (((0,), (0,)), ((), ())), preferred_element_type=F32
    ).astype(BF16)
    head = lax.psum_scatter(partial, "fsdp", scatter_dimension=0, tiled=True).astype(F32)
    return head[None], text_grad


def solution(mesh):
    n_dp, n_fsdp = mesh.shape["dp"], mesh.shape["fsdp"]
    line = n_fsdp == 4 and n_dp % 4 == 0
    placed = (P(("dp", "fsdp"), None), P(("dp", "fsdp"), None), P("fsdp", None), P(), P())
    return jax.shard_map(
        functools.partial(line_body if line else plain_body, n_dp, n_fsdp),
        mesh=mesh,
        in_specs=placed,
        out_specs=(P("dp", "fsdp", None), P(("dp", "fsdp"), None)),
        check_vma=False,
    )
```

```python
import functools

import jax
import jax.numpy as jnp
from jax import lax
from jax.experimental import pallas as pl
from jax.experimental.pallas import tpu as pltpu
from jax.sharding import PartitionSpec as P

STEPS = 3
EPS = 1e-06
SHARES = (4, 5)
CROSS_PARTS = (1, 2)
TEXT_PARTS = 2
VMEM_BYTES = 24 * 1024 * 1024
BF16, F32 = jnp.bfloat16, jnp.float32


def spaces(count):
    return [pl.BlockSpec(memory_space=pltpu.VMEM)] * count


def params(size=VMEM_BYTES):
    return pltpu.CompilerParams(vmem_limit_bytes=size)


def cost():
    return pl.CostEstimate(flops=0, bytes_accessed=0, transcendentals=0)


IN_HBM = pl.BlockSpec(memory_space=pltpu.HBM)


def place():
    where = lax.axis_index("dp")
    return lax.axis_index("fsdp"), lax.rem(where, 2), lax.rem(lax.div(where, 2), 2)


def cut_kernel(short, own, whole, part, sem):
    _, core, column = place()
    half = whole.shape[0]
    first = pltpu.make_async_copy(
        own.at[pl.ds(pl.multiple_of(core * half, 16), half), :], whole, sem.at[0]
    )
    start = pl.multiple_of(core * half + column * (half - short), 16)
    second = pltpu.make_async_copy(own.at[pl.ds(start, short), :], part, sem.at[1])
    first.start()
    second.start()
    first.wait()
    second.wait()


def cut(short, own):
    half, width = own.shape[0] // 2, own.shape[1]
    outs = (
        jax.ShapeDtypeStruct((half, width), BF16),
        jax.ShapeDtypeStruct((short, width), BF16),
    )
    return pl.pallas_call(
        functools.partial(cut_kernel, short),
        out_shape=outs,
        in_specs=[IN_HBM],
        out_specs=spaces(2),
        scratch_shapes=[pltpu.SemaphoreType.DMA((2,))],
        compiler_params=params(),
        cost_estimate=cost(),
        name="cut",
    )(own)


def prepare_kernel(t0, twin0, t2, sharp, bias, *rest):
    twin2, (units, scalars) = rest[:TEXT_PARTS], rest[TEXT_PARTS:]
    rows = t0.shape[0]
    _, core, _ = place()
    scalars[0:1, :] = jnp.broadcast_to(sharp[...], (1, scalars.shape[1]))
    scalars[1:2, :] = jnp.broadcast_to(bias[...], (1, scalars.shape[1]))

    def fill(start, block):
        values = block[...].astype(F32)
        inverse = 1.0 / jnp.sqrt(jnp.sum(values * values, axis=-1, keepdims=True) + EPS)
        units[start : start + block.shape[0], :] = (values * inverse).astype(BF16)

    fill(0, t0)
    fill(2 * rows, t2)

    @pl.when(core == 0)
    def _():
        for k, block in enumerate(twin2):
            fill(rows + k * block.shape[0], block)

    pl.when(core == 1)(lambda: fill(rows, twin0))


def prepare(t0, twin0, t2, sharp, bias, twin2):
    rows, width = t0.shape
    return pl.pallas_call(
        prepare_kernel,
        out_shape=(
            jax.ShapeDtypeStruct((STEPS * rows, width), BF16),
            jax.ShapeDtypeStruct((8, 128), F32),
        ),
        in_specs=spaces(5 + TEXT_PARTS),
        out_specs=tuple(spaces(2)),
        compiler_params=params(),
        cost_estimate=cost(),
        name="prepare",
    )(t0, twin0, t2, sharp, bias, *twin2)


def turn_kernel(depth, x, x_t, outer_t):
    x_t[...] = x[...].T
    start = jnp.where(lax.axis_index("fsdp") == 0, depth, 0)
    outer_t[...] = x_t[pl.ds(pl.multiple_of(start, 16), outer_t.shape[0]), :]


def turned(depth, x):
    rows, width = x.shape
    return pl.pallas_call(
        functools.partial(turn_kernel, depth),
        out_shape=(
            jax.ShapeDtypeStruct((width, rows), BF16),
            jax.ShapeDtypeStruct((width - depth, rows), BF16),
        ),
        in_specs=spaces(1),
        out_specs=tuple(spaces(2)),
        compiler_params=params(),
        cost_estimate=cost(),
        name="turned",
    )(x)


def rows_of(ref, block, depth):
    return ref[pl.ds(pl.multiple_of(block * depth, 16), depth), :]


def weights(mine, others, scale, bias):
    product = lax.dot_general(
        mine, others, (((1,), (1,)), ((), ())), preferred_element_type=F32
    )
    coefficient = jax.nn.sigmoid(scale * product + bias)
    row = lax.broadcasted_iota(jnp.int32, coefficient.shape, 0)
    column = lax.broadcasted_iota(jnp.int32, coefficient.shape, 1)
    coefficient = jnp.where(row == column, coefficient - 1.0, coefficient).astype(BF16)
    return coefficient, scale * jnp.sum(coefficient.astype(F32) * product, axis=-1, keepdims=True)


def picture_kernel(x, x_t, units, scalars, own, *rest):
    pieces, outs = rest[:8], rest[8 : 8 + len(SHARES)]
    unit, grad, w, proj = rest[-4:]
    part, core, column = place()
    depth = own.shape[0]
    half = depth // 2
    short = pieces[2].shape[0]
    rest_rows = half - short
    rows = x.shape[0]
    w[pl.ds(pl.multiple_of(part * depth, 16), depth), :] = own[...]
    for twin in (0, 1):
        lane = core if twin == 0 else 1 - core
        plus, minus, two, two_crossed = pieces[4 * twin : 4 * twin + 4]
        for piece, from_part in ((plus, part + 3), (minus, part + 1)):
            start = pl.multiple_of(lax.rem(from_part, 4) * depth + lane * half, 16)
            w[pl.ds(start, half), :] = piece[...]
        base = lax.rem(part + 2, 4) * depth + lane * half
        start = pl.multiple_of(base + column * rest_rows, 16)
        w[pl.ds(start, short), :] = two[...]
        source = pl.multiple_of((1 - column) * (short - rest_rows), 16)
        start = pl.multiple_of(base + (1 - column) * short, 16)
        w[pl.ds(start, rest_rows), :] = two_crossed[pl.ds(source, rest_rows), :]

    proj[...] = jnp.dot(x[...], w[...], preferred_element_type=F32)
    values = proj[...]
    inverse = 1.0 / jnp.sqrt(jnp.sum(values * values, axis=-1, keepdims=True) + EPS)
    unit[...] = (values * inverse).astype(BF16)
    scale = scalars[0:1, 0:1]
    coefficient, along = weights(unit[...], units[...], scale, scalars[1:2, 0:1])
    slope = jnp.dot(coefficient, units[...], preferred_element_type=F32)
    grad[...] = (slope * (scale * inverse) - proj[...] * (along * inverse * inverse)).astype(BF16)
    inner = jnp.logical_or(part == 1, part == 2)

    @pl.when(inner)
    def _():
        block = rows_of(x_t, 3 * (part - 1), depth)
        begin = 0
        for out in outs:
            stop = begin + out.shape[1]
            out[...] = jnp.dot(block, grad[:, begin:stop], preferred_element_type=F32).astype(BF16)
            begin = stop

    @pl.when(jnp.logical_not(inner))
    def _():
        begin = 0
        for out in outs:
            stop = begin + out.shape[1]
            out[:rows, :] = grad[:, begin:stop]
            out[rows:, :] = jnp.zeros((depth - rows, stop - begin), BF16)
            begin = stop


def picture_side(x, x_t, units, scalars, own, pieces):
    rows, width = x.shape
    depth = own.shape[0]
    out = jax.ShapeDtypeStruct((rows, width), BF16)
    sizes = [width * share // sum(SHARES) for share in SHARES]
    outs = tuple(jax.ShapeDtypeStruct((depth, size), BF16) for size in sizes)
    outs = outs + (out, out)
    return pl.pallas_call(
        picture_kernel,
        out_shape=outs,
        in_specs=spaces(13),
        out_specs=spaces(len(outs)),
        scratch_shapes=[
            pltpu.VMEM((width, width), BF16),
            pltpu.VMEM((rows, width), F32),
        ],
        compiler_params=params(),
        cost_estimate=cost(),
        name="picture_side",
    )(x, x_t, units, scalars, own, *pieces)


def text_kernel(text, scalars, u0, u1, u2, out, done, units):
    rows = text.shape[0]
    done[...] = jnp.zeros_like(done)
    for k, block in enumerate((u0, u1, u2)):
        units[k * rows : (k + 1) * rows, :] = block[...]
    values = text[...].astype(F32)
    inverse = 1.0 / jnp.sqrt(jnp.sum(values * values, axis=-1, keepdims=True) + EPS)
    scale = scalars[0:1, 0:1]
    coefficient, along = weights(
        (values * inverse).astype(BF16), units[...], scale, scalars[1:2, 0:1]
    )
    slope = jnp.dot(coefficient, units[...], preferred_element_type=F32)
    out[...] = slope * (scale * inverse) - values * (along * inverse * inverse)


def text_side(text, scalars, u0, u1, u2):
    rows, width = text.shape
    return pl.pallas_call(
        text_kernel,
        out_shape=(jax.ShapeDtypeStruct((rows, width), F32), jax.ShapeDtypeStruct((8, 128), F32)),
        in_specs=spaces(5),
        out_specs=tuple(spaces(2)),
        scratch_shapes=[pltpu.VMEM((STEPS * rows, width), BF16)],
        compiler_params=params(),
        cost_estimate=cost(),
        name="text_side",
    )(text, scalars, u0, u1, u2)


def pair_kernel(begin, parts, x_t, far_t, grad, arrived, *rest):
    outs = rest[-1 - 2 * parts :]
    kept, fars, nears = outs[0], outs[1 : 1 + parts], outs[1 + parts :]
    rows = grad.shape[0]
    depth, size = arrived.shape
    part = lax.axis_index("fsdp")
    inner = jnp.logical_or(part == 1, part == 2)
    mine = grad[:, begin : begin + size]

    def product(block):
        return jnp.dot(rows_of(x_t, block, depth), mine, preferred_element_type=F32)

    @pl.when(inner)
    def _():
        other = arrived[:rows, :]
        first = jnp.where(part == 1, 1, 0)
        for block, out in ((3 - part, nears), (lax.rem(part + 2, 4), fars), (part, [kept])):
            both = product(block) + jnp.dot(
                rows_of(far_t, block - first, depth), other, preferred_element_type=F32
            )
            size = depth // len(out)
            for k, piece in enumerate(out):
                piece[...] = both[k * size : (k + 1) * size].astype(piece.dtype)

    @pl.when(jnp.logical_not(inner))
    def _():
        kept[...] = product(part) + arrived[...].astype(F32)
        for piece in nears + fars:
            piece[...] = jnp.zeros_like(piece)


def pair_product(begin, parts, x_t, far_t, grad, arrived, after):
    depth, size = arrived.shape
    piece = jax.ShapeDtypeStruct((depth // parts, size), BF16)
    outs = (jax.ShapeDtypeStruct((depth, size), F32),) + (piece,) * (2 * parts)
    return pl.pallas_call(
        functools.partial(pair_kernel, begin, parts),
        out_shape=outs,
        in_specs=spaces(4 + len(after)),
        out_specs=spaces(len(outs)),
        compiler_params=params(),
        cost_estimate=cost(),
        name="pair_product",
    )(x_t, far_t, grad, arrived, *after)


def total_kernel(begin, parts, kept, *rest):
    nears, fars, (out, summed, sem) = rest[:parts], rest[parts : 2 * parts], rest[-3:]
    size = kept.shape[0] // parts
    copies = []
    for k, (near, far) in enumerate(zip(nears, fars)):
        at = slice(k * size, (k + 1) * size)
        summed[at, :] = kept[at, :] + near[...].astype(F32) + far[...].astype(F32)
        target = out.at[0, at, begin : begin + kept.shape[1]]
        copies.append(pltpu.make_async_copy(summed.at[at, :], target, sem.at[k]))
        copies[-1].start()
    for copy in copies:
        copy.wait()


def total(begin, width, kept, nears, fars, held):
    depth, parts = kept.shape[0], len(nears)
    return pl.pallas_call(
        functools.partial(total_kernel, begin, parts),
        out_shape=jax.ShapeDtypeStruct((1, depth, width), F32),
        in_specs=spaces(1 + 2 * parts) + [IN_HBM] * len(held[:1]) + spaces(len(held[1:])),
        out_specs=IN_HBM,
        scratch_shapes=[pltpu.VMEM(kept.shape, F32), pltpu.SemaphoreType.DMA((parts,))],
        input_output_aliases={1 + 2 * parts: 0} if held else {},
        compiler_params=params(),
        cost_estimate=cost(),
        name="total",
    )(kept, *nears, *fars, *held)


def line_body(n_dp, n_fsdp, x, text, w, sharp, bias):
    depth, width = w.shape
    half = depth // 2
    short = (half // 2 + 15) // 16 * 16

    def along(value, pairs):
        return lax.ppermute(value, "fsdp", pairs)

    def across(value):
        return lax.ppermute(value, "dp", [(d, d ^ 1) for d in range(n_dp)])

    def shifted(value, by):
        return lax.ppermute(value, "dp", [(d, (d + by) % n_dp) for d in range(n_dp)])

    sharp, bias = sharp.reshape(1, 1), bias.reshape(1, 1)
    swap = [(0, 1), (1, 0), (2, 3), (3, 2)]
    whole, piece = cut(short, w)
    whole, piece, text = lax.optimization_barrier((whole, piece, text))
    two = along(piece, [(f, (f + 2) % n_fsdp) for f in range(n_fsdp)])
    plus = along(whole, [(f, (f + 1) % n_fsdp) for f in range(n_fsdp)])
    minus = along(whole, [(f, (f - 1) % n_fsdp) for f in range(n_fsdp)])
    text2 = shifted(text, 2)
    x_t, outer_t = turned(depth, x)
    two, outer_t, text2 = lax.optimization_barrier((two, outer_t, text2))
    two_crossed = lax.ppermute(two, "dp", [(d, d ^ 2) for d in range(n_dp)])
    far_t = along(outer_t, swap)
    size = text.shape[0] // TEXT_PARTS
    twin2 = [across(text2[k * size : (k + 1) * size]) for k in range(TEXT_PARTS)]
    units, scalars = prepare(text, across(text), text2, sharp, bias, twin2)
    plus, minus, units, scalars, x_t = lax.optimization_barrier((plus, minus, units, scalars, x_t))
    pieces = [plus, minus, two, two_crossed]
    pieces = pieces + [across(piece) for piece in pieces]
    results = picture_side(x, x_t, units, scalars, w, pieces)
    *outward, unit, grad = results
    grad, far_t = lax.optimization_barrier((grad, far_t))
    outward[0], far_t = lax.optimization_barrier((outward[0], far_t))

    arrived = []
    for block in outward:
        if arrived:
            block, arrived[-1] = lax.optimization_barrier((block, arrived[-1]))
        arrived.append(along(block, swap))
    unit1, unit2 = shifted(unit, -1), shifted(unit, -2)
    begin, terms, after = 0, [], []
    for parts, block in zip(CROSS_PARTS, arrived):
        kept, *sent = pair_product(begin, parts, x_t, far_t, grad, block, after)
        fars = [along(n, [(1, 3), (2, 0), (0, 1), (3, 2)]) for n in sent[:parts]]
        nears = [along(n, [(1, 2), (2, 1), (0, 0), (3, 3)]) for n in sent[parts:]]
        after = []
        terms.append((begin, width, kept, fars, nears))
        begin += block.shape[1]
    text_grad, done = text_side(text, scalars, unit, unit1, unit2)
    head = total(*terms[0], [])
    for term in terms[1:]:
        head = total(*term, [head, done])
    return head, text_grad


def plain_body(n_dp, n_fsdp, x, text, w, sharp, bias):
    def shifted(value, by):
        return lax.ppermute(value, "dp", [(d, (d + by) % n_dp) for d in range(n_dp)])

    rows, width = x.shape
    proj = jnp.dot(
        x, lax.all_gather(w, "fsdp", axis=0, tiled=True), preferred_element_type=F32
    )
    norm = jnp.sqrt(jnp.sum(proj * proj, axis=-1, keepdims=True) + EPS)
    direction = proj / norm
    unit = direction.astype(BF16)
    values = text.astype(F32)
    txt_norm = jnp.sqrt(jnp.sum(values * values, axis=-1, keepdims=True) + EPS)
    txt_dir = values / txt_norm
    slot = txt_dir.astype(BF16)
    scale = sharp[0]
    slope = jnp.zeros((rows, width), F32)
    txt_slope = jnp.zeros((rows, width), F32)
    for step in range(STEPS):
        if step > 0:
            slot = shifted(slot, 1)
        logits = scale * jnp.dot(unit, slot.T, preferred_element_type=F32) + bias[0]
        coefficient = jax.nn.sigmoid(logits)
        if step == 0:
            coefficient = coefficient - jnp.eye(rows, dtype=F32)
        coefficient = coefficient.astype(BF16)
        slope = slope + scale * jnp.dot(coefficient, slot, preferred_element_type=F32)
        share = scale * lax.dot_general(
            coefficient, unit, (((0,), (0,)), ((), ())), preferred_element_type=F32
        )
        if step > 0:
            share = shifted(share.astype(BF16), -step).astype(F32)
        txt_slope = txt_slope + share
    grad = (
        (slope - direction * jnp.sum(direction * slope, axis=-1, keepdims=True)) / norm
    ).astype(BF16)
    text_grad = (
        txt_slope - txt_dir * jnp.sum(txt_dir * txt_slope, axis=-1, keepdims=True)
    ) / txt_norm
    partial = lax.dot_general(
        x, grad, (((0,), (0,)), ((), ())), preferred_element_type=F32
    ).astype(BF16)
    head = lax.psum_scatter(partial, "fsdp", scatter_dimension=0, tiled=True).astype(F32)
    return head[None], text_grad


def solution(mesh):
    n_dp, n_fsdp = mesh.shape["dp"], mesh.shape["fsdp"]
    line = n_fsdp == 4 and n_dp % 4 == 0
    placed = (P(("dp", "fsdp"), None), P(("dp", "fsdp"), None), P("fsdp", None), P(), P())
    return jax.shard_map(
        functools.partial(line_body if line else plain_body, n_dp, n_fsdp),
        mesh=mesh,
        in_specs=placed,
        out_specs=(P("dp", "fsdp", None), P(("dp", "fsdp"), None)),
        check_vma=False,
    )
```
